128 devices in a mesh: dp: 16 (over y_lo, x, core), proto: 8 (over z, y_hi).
Axes of the slice: x: 4, y: 4 (y_hi: 2, y_lo: 2; y = y_hi * 2 + y_lo), z: 4, core: 2. Of those that a mesh axis runs over, the one named last changes fastest.
Arguments:
- teacher_feats: bfloat16 [4096, 256], P('dp')
- student_feats: bfloat16 [4096, 256], P('dp')
- proto_weight: bfloat16 [256, 262144], P(None, 'proto')
Outputs:
- feature_grad: float32 [4096, 256], P('dp')
- proto_grad: float32 [256, 262144], P('dp', 'proto')
All inputs are finite; a program needn't handle non-finite values.
Results may differ from the reference program's by a relative error of at most 0.0003.
The reference program's roundings to bfloat16 on the way (of `proto_unit` and `dlogit`) count: a program that leaves them out, or rounds other values in their place, can miss the bound.
Values may be sent and summed in bfloat16 or wider, within the bound.
No kernel may reach another device: no remote copies, remote signals or barrier semaphores. Data moves between devices by JAX's collectives and lax.ppermute only.
A program may use at most 256 MiB of HBM per device.

```python
import jax
import jax.numpy as jnp
from jax import lax

D = 256
K = 262144
ITERS = 3
ROWS = 4096


def feature_draw(key, salt):
    key = jax.random.fold_in(key, salt)
    return jax.random.normal(key, (ROWS, D), jnp.float32).astype(jnp.bfloat16)


def draw_teacher_feats(key, part):
    return feature_draw(key, 11)


def draw_student_feats(key, part):
    return feature_draw(key, 12)


def draw_proto_weight(key, part):
    key = jax.random.fold_in(key, 13)
    base = jax.random.normal(key, (D, K), jnp.float32)
    return (0.0625 * base).astype(jnp.bfloat16)


def setup_inputs(seed: int = 0) -> dict:
    splits = jax.random.split(jax.random.key(seed), 4)
    teacher_feats = draw_teacher_feats(jax.random.fold_in(splits[3], 71), 0)
    student_feats = draw_student_feats(jax.random.fold_in(splits[3], 71), 0)
    proto_weight = draw_proto_weight(jax.random.fold_in(splits[3], 71), 0)
    return dict(teacher_feats=teacher_feats, student_feats=student_feats, proto_weight=proto_weight)


EPS = 1e-06
TEACH = 0.07
STUD = 0.1

def unit_rows(feats):
    wide = feats.astype(jnp.float32)
    squares = lax.optimization_barrier(jnp.sum(wide * wide, axis=1, keepdims=True))
    return (wide * lax.rsqrt(squares + EPS)).astype(jnp.bfloat16)

def unit_cols(weight):
    wide = weight.astype(jnp.float32)
    squares = lax.optimization_barrier(jnp.sum(wide * wide, axis=0, keepdims=True))
    return (wide * lax.rsqrt(squares + EPS)).astype(jnp.bfloat16)

def reference(teacher_feats, student_feats, proto_weight):
    teacher_unit = unit_rows(teacher_feats)
    student_unit = unit_rows(student_feats)
    proto_unit = unit_cols(proto_weight)
    width = min(K, 8192)
    count = K // width
    blocks = proto_unit.reshape(D, count, width).transpose(1, 0, 2)

    def kernel_of(wblock):
        return jnp.exp(jnp.dot(teacher_unit, wblock, preferred_element_type=jnp.float32) / TEACH)

    def student_of(wblock):
        return jnp.exp(jnp.dot(student_unit, wblock, preferred_element_type=jnp.float32) / STUD)
    row_scale = jnp.ones((ROWS,), jnp.float32)
    col_blocks = jnp.zeros((count, width), jnp.float32)
    for step in range(ITERS):

        def sweep(acc, wblock, row_scale=row_scale):
            kernel = kernel_of(wblock)
            col_scale = 1.0 / lax.optimization_barrier(jnp.sum(row_scale[:, None] * kernel, axis=0))
            return (acc + lax.optimization_barrier(jnp.sum(kernel * col_scale[None, :], axis=1)), col_scale)
        row_total, col_blocks = lax.scan(sweep, jnp.zeros((ROWS,), jnp.float32), blocks)
        row_scale = 1.0 / row_total

    def student_sum(acc, wblock):
        return (acc + lax.optimization_barrier(jnp.sum(student_of(wblock), axis=1)), None)
    total, unused = lax.scan(student_sum, jnp.zeros((ROWS,), jnp.float32), blocks)

    def gradient(acc, pair):
        wblock, col_scale = pair
        target = row_scale[:, None] * kernel_of(wblock) * col_scale[None, :]
        dlogit = ((student_of(wblock) / total[:, None] - target) / STUD).astype(jnp.bfloat16)
        acc = acc + jnp.dot(dlogit, wblock.T, preferred_element_type=jnp.float32)
        return (acc, jnp.dot(student_unit.T, dlogit, preferred_element_type=jnp.float32))
    feat_acc, proto_blocks = lax.scan(gradient, jnp.zeros((ROWS, D), jnp.float32), (blocks, col_blocks))
    feature_grad = 512.0 * feat_acc
    proto_grad = 4096.0 * proto_blocks.transpose(1, 0, 2).reshape(D, K)
    return (feature_grad, proto_grad)
```

```python
import functools
import math

import jax
import jax.numpy as jnp
import numpy as np
from jax import lax
from jax.experimental import pallas as pl
from jax.experimental.pallas import tpu as pltpu
from jax.sharding import PartitionSpec as P

ITERS = 3
EPS = 1e-06
TEACH = float(np.float32(0.07))
STUD = float(np.float32(0.1))
LOG2E = math.log2(math.e)
TSCALE = LOG2E / TEACH
SSCALE = LOG2E / STUD
LOG_INV = -math.log2(STUD)
F32 = jnp.float32
BF16 = jnp.bfloat16
LANES = 128
VMEM_LIMIT = 60 * 1024 * 1024


def unit_rows(feats):
    wide = feats.astype(F32)
    squares = jnp.sum(wide * wide, axis=1, keepdims=True)
    return (wide * lax.rsqrt(squares + EPS)).astype(BF16)


def unit_cols(weight):
    wide = weight.astype(F32)
    squares = jnp.sum(wide * wide, axis=0, keepdims=True)
    return (wide * lax.rsqrt(squares + EPS)).astype(BF16)


def dot(a, b):
    return jnp.dot(a, b, preferred_element_type=F32)


def dot_nt(a, b):
    return lax.dot_general(a, b, (((1,), (1,)), ((), ())), preferred_element_type=F32)


def fold_rows(value):
    return jnp.sum(value.reshape(value.shape[0] // 8, 8, value.shape[1]), axis=0)


def params():
    return pltpu.CompilerParams(vmem_limit_bytes=VMEM_LIMIT)


def sweep_kernel(copies, parts_ref, protos_ref, teach_ref, col_ref, out_ref, scale, kern, acc):
    step = pl.program_id(0)
    blocks, _, rows = teach_ref.shape
    per = rows // LANES

    @pl.when(step == 0)
    def _():
        if parts_ref is None:
            scale[...] = jnp.ones_like(scale)
        else:
            scale[...] = 1.0 / jnp.sum(parts_ref[...], axis=0)
        acc[...] = jnp.zeros_like(acc)

    protos = protos_ref[...]
    col_acc = jnp.zeros((protos.shape[0], LANES), F32)
    for block in range(blocks):
        logits = dot(protos, teach_ref[block])
        for part in range(per):
            value = jnp.exp2(logits[:, part * LANES : (part + 1) * LANES] * TSCALE)
            at = block * per + part
            kern[:, at * LANES : (at + 1) * LANES] = value
            col_acc = col_acc + value * scale[at : at + 1, :]
    col = 1.0 / jnp.sum(col_acc, axis=1, keepdims=True)
    wide_col = jnp.broadcast_to(col, (protos.shape[0], LANES))
    col_ref[...] = wide_col
    for at in range(blocks * per):
        acc[:, at * LANES : (at + 1) * LANES] += fold_rows(
            kern[:, at * LANES : (at + 1) * LANES] * wide_col
        )

    @pl.when(step == pl.num_programs(0) - 1)
    def _():
        for at in range(blocks * per):
            total = jnp.sum(acc[:, at * LANES : (at + 1) * LANES], axis=0, keepdims=True)
            for copy in range(copies):
                out_ref[copy, at : at + 1, :] = total


def sweep(parts, protos, teach, copies, tile=256):
    count, depth = protos.shape
    blocks, _, rows = teach.shape
    groups = blocks * rows // LANES
    body = functools.partial(sweep_kernel, copies)
    in_specs = [
        pl.BlockSpec((tile, depth), lambda i: (i, 0)),
        pl.BlockSpec(teach.shape, lambda i: (0, 0, 0)),
    ]
    args = [protos, teach]
    if parts is None:
        body = functools.partial(body, None)
    else:
        in_specs.insert(0, pl.BlockSpec(parts.shape, lambda i: (0, 0, 0)))
        args.insert(0, parts)
    return pl.pallas_call(
        body,
        grid=(count // tile,),
        in_specs=in_specs,
        out_specs=[
            pl.BlockSpec((tile, LANES), lambda i: (i, 0)),
            pl.BlockSpec((copies, groups, LANES), lambda i: (0, 0, 0)),
        ],
        out_shape=[
            jax.ShapeDtypeStruct((count, LANES), F32),
            jax.ShapeDtypeStruct((copies, groups, LANES), F32),
        ],
        scratch_shapes=[
            pltpu.VMEM((groups, LANES), F32),
            pltpu.VMEM((tile, blocks * rows), F32),
            pltpu.VMEM((8, blocks * rows), F32),
        ],
        compiler_params=params(),
        name="sweep",
    )(*args)


def totals_kernel(protos_ref, stud_ref, out_ref, acc):
    step = pl.program_id(0)

    @pl.when(step == 0)
    def _():
        acc[...] = jnp.zeros_like(acc)

    protos = protos_ref[...]
    blocks, _, rows = stud_ref.shape
    for block in range(blocks):
        logits = dot(protos, stud_ref[block])
        acc[:, block * rows : (block + 1) * rows] += fold_rows(jnp.exp2(logits * SSCALE))

    @pl.when(step == pl.num_programs(0) - 1)
    def _():
        for at in range(blocks * rows // LANES):
            out_ref[at : at + 1, :] = jnp.sum(
                acc[:, at * LANES : (at + 1) * LANES], axis=0, keepdims=True
            )


def totals(protos, stud, tile=256):
    count, depth = protos.shape
    blocks, _, rows = stud.shape
    groups = blocks * rows // LANES
    return pl.pallas_call(
        totals_kernel,
        grid=(count // tile,),
        in_specs=[
            pl.BlockSpec((tile, depth), lambda i: (i, 0)),
            pl.BlockSpec(stud.shape, lambda i: (0, 0, 0)),
        ],
        out_specs=pl.BlockSpec((groups, LANES), lambda i: (0, 0)),
        out_shape=jax.ShapeDtypeStruct((groups, LANES), F32),
        scratch_shapes=[pltpu.VMEM((8, blocks * rows), F32)],
        compiler_params=params(),
        name="totals",
    )(protos, stud)


def hop_kernel(copies, in_ref, out_ref):
    total = jnp.sum(in_ref[...], axis=0)
    for copy in range(copies):
        out_ref[copy] = total


def hop(parts, copies):
    return pl.pallas_call(
        functools.partial(hop_kernel, copies),
        out_shape=jax.ShapeDtypeStruct((copies,) + parts.shape[1:], F32),
        name="hop",
    )(parts)


def spread(parts, size):
    parts = lax.all_to_all(parts, "dp", 0, 0, tiled=True)
    parts = hop(parts, size)
    return lax.all_to_all(parts, "proto", 0, 0, tiled=True)


def grad_kernel(
    rows_ref, total_ref, col_ref, protos_ref, cols_ref, teach_ref, stud_ref, feat_ref, pgrad_ref, scale, norm, diff
):
    step = pl.program_id(0)
    blocks, _, rows = teach_ref.shape
    per = rows // LANES

    @pl.when(step == 0)
    def _():
        scale[...] = LOG_INV - jnp.log2(jnp.sum(rows_ref[...], axis=0))
        norm[...] = LOG_INV - jnp.log2(jnp.sum(total_ref[...], axis=0))
        feat_ref[...] = jnp.zeros_like(feat_ref)

    protos = protos_ref[...]
    cols = cols_ref[...]
    log_col = jnp.log2(col_ref[...])
    pgrad = jnp.zeros(pgrad_ref.shape, F32)
    for block in range(blocks):
        teach_logits = dot(protos, teach_ref[block])
        stud_logits = dot(protos, stud_ref[block])
        for part in range(per):
            at = block * per + part
            lanes = slice(part * LANES, (part + 1) * LANES)
            target = jnp.exp2(teach_logits[:, lanes] * TSCALE + (scale[at : at + 1, :] + log_col))
            prob = jnp.exp2(stud_logits[:, lanes] * SSCALE + norm[at : at + 1, :])
            diff[:, at * LANES : (at + 1) * LANES] = (prob - target).astype(BF16)
        here = diff[:, block * rows : (block + 1) * rows]
        feat_ref[block] += dot(cols, here)
        pgrad = pgrad + dot_nt(stud_ref[block], here)
    pgrad_ref[...] = pgrad


def gradients(rows_parts, total_parts, col, protos, cols, teach, stud, tile=256):
    count, depth = protos.shape
    blocks, _, rows = teach.shape
    groups = blocks * rows // LANES
    whole3 = lambda i: (0, 0, 0)
    return pl.pallas_call(
        grad_kernel,
        grid=(count // tile,),
        in_specs=[
            pl.BlockSpec(rows_parts.shape, whole3),
            pl.BlockSpec(total_parts.shape, whole3),
            pl.BlockSpec((tile, LANES), lambda i: (i, 0)),
            pl.BlockSpec((tile, depth), lambda i: (i, 0)),
            pl.BlockSpec((depth, tile), lambda i: (0, i)),
            pl.BlockSpec(teach.shape, whole3),
            pl.BlockSpec(stud.shape, whole3),
        ],
        out_specs=[
            pl.BlockSpec((blocks, depth, rows), whole3),
            pl.BlockSpec((depth, tile), lambda i: (0, i)),
        ],
        out_shape=[
            jax.ShapeDtypeStruct((blocks, depth, rows), F32),
            jax.ShapeDtypeStruct((depth, count), F32),
        ],
        scratch_shapes=[
            pltpu.VMEM((groups, LANES), F32),
            pltpu.VMEM((groups, LANES), F32),
            pltpu.VMEM((tile, blocks * rows), BF16),
        ],
        compiler_params=params(),
        name="gradients",
    )(rows_parts, total_parts, col, protos, cols, teach, stud)


def on_device(dp, proto, teacher_feats, student_feats, proto_weight):
    depth, held = proto_weight.shape
    count = held // dp
    teach_own = unit_rows(teacher_feats).T
    teach = lax.all_gather(teach_own, "dp")
    stud_own = unit_rows(student_feats).T
    stud_own, teach = lax.optimization_barrier((stud_own, teach))
    stud = lax.all_gather(stud_own, "dp")

    mine = lax.axis_index("dp")
    cols = unit_cols(lax.dynamic_slice(proto_weight, (0, mine * count), (depth, count)))
    protos = cols.T

    parts = None
    for step in range(ITERS):
        col, copies = sweep(parts, protos, teach, dp)
        parts = spread(copies, proto)
        if step == 0:
            total = totals(protos, stud)
            total_parts = spread(jnp.broadcast_to(total[None], (dp,) + total.shape), proto)

    feat, pgrad = gradients(parts, total_parts, col, protos, cols, teach, stud)

    feat = jnp.sum(lax.all_to_all(feat, "dp", 0, 0, tiled=True), axis=0)
    feat = feat.reshape(proto, depth // proto, -1)
    feat = jnp.sum(lax.all_to_all(feat, "proto", 0, 0, tiled=True), axis=0)
    feat = lax.all_to_all(
        jnp.broadcast_to(feat[None], (proto,) + feat.shape), "proto", 0, 0, tiled=True
    )
    feature_grad = 512.0 * feat.reshape(depth, -1).T

    pgrad = pgrad.reshape(dp, depth // dp, count)
    pgrad = lax.all_to_all(pgrad, "dp", 0, 0, tiled=True)
    proto_grad = 4096.0 * pgrad.transpose(1, 0, 2).reshape(depth // dp, held)
    return feature_grad, proto_grad


def solution(mesh):
    placed = (P("dp", None), P("dp", None), P(None, "proto"))
    return jax.shard_map(
        functools.partial(on_device, mesh.shape["dp"], mesh.shape["proto"]),
        mesh=mesh,
        in_specs=placed,
        out_specs=(P("dp", None), P("dp", "proto")),
        check_vma=False,
    )
```

```python
import functools
import math

import jax
import jax.numpy as jnp
import numpy as np
from jax import lax
from jax.experimental import pallas as pl
from jax.experimental.pallas import tpu as pltpu
from jax.sharding import PartitionSpec as P

ITERS = 3
EPS = 1e-06
TEACH = float(np.float32(0.07))
STUD = float(np.float32(0.1))
LOG2E = math.log2(math.e)
TSCALE = LOG2E / TEACH
SSCALE = LOG2E / STUD
LOG_INV = -math.log2(STUD)
F32 = jnp.float32
BF16 = jnp.bfloat16
LANES = 128
MIB = 1024 * 1024
AXES = ("yl", "x", "c", "z", "yh")
DP = ("yl", "x", "c")
PROTO = ("z", "yh")
CHIPS = ("yl", "x")
PLANE = ("yl", "x", "yh")
PILLAR = ("z", "c")


def unit_rows(feats):
    wide = feats.astype(F32)
    squares = jnp.sum(wide * wide, axis=1, keepdims=True)
    return (wide * lax.rsqrt(squares + EPS)).astype(BF16)


def unit_cols(weight):
    wide = weight.astype(F32)
    squares = jnp.sum(wide * wide, axis=0, keepdims=True)
    return (wide * lax.rsqrt(squares + EPS)).astype(BF16)


def dot(a, b):
    return jnp.dot(a, b, preferred_element_type=F32)


def dot_nt(a, b):
    return lax.dot_general(a, b, (((1,), (1,)), ((), ())), preferred_element_type=F32)


def fold_rows(value):
    return jnp.sum(value.reshape(value.shape[0] // 8, 8, value.shape[1]), axis=0)


def params(mib):
    return pltpu.CompilerParams(vmem_limit_bytes=mib * MIB)


def vmem():
    return pl.BlockSpec(memory_space=pltpu.VMEM)


def smem():
    return pl.BlockSpec(memory_space=pltpu.SMEM)


def rows_of(near_ref, far_ref, block):
    return jnp.concatenate([near_ref[block], far_ref[block]], axis=1)


def sweep_kernel(copies, tile, has_parts, has_extra, *refs):
    refs = list(refs)
    parts_ref = refs.pop(0) if has_parts else None
    extra_ref = refs.pop(0) if has_extra else None
    protos_ref, near_ref, far_ref, col_ref, out_ref, scale, kern, acc = refs
    blocks, rows, _ = near_ref.shape
    per = rows // LANES
    groups = blocks * per
    if has_parts:
        scale[...] = 1.0 / jnp.sum(parts_ref[...], axis=0)
    else:
        scale[...] = jnp.ones_like(scale)
    acc[...] = jnp.zeros_like(acc)

    def one_tile(step, carry):
        here = pl.ds(pl.multiple_of(step * tile, tile), tile)
        protos = protos_ref[here, :]
        col_acc = jnp.zeros((tile, LANES), F32)
        for block in range(blocks):
            logits = dot_nt(protos, rows_of(near_ref, far_ref, block))
            for part in range(per):
                value = jnp.exp2(logits[:, part * LANES : (part + 1) * LANES] * TSCALE)
                at = block * per + part
                kern[:, at * LANES : (at + 1) * LANES] = value
                col_acc = col_acc + value * scale[at : at + 1, :]
        col = 1.0 / jnp.sum(col_acc, axis=1, keepdims=True)
        wide_col = jnp.broadcast_to(col, (tile, LANES))
        col_ref[here, :] = wide_col
        for at in range(groups):
            lanes = slice(at * LANES, (at + 1) * LANES)
            acc[:, lanes] += fold_rows(kern[:, lanes] * wide_col)
        return carry

    lax.fori_loop(0, protos_ref.shape[0] // tile, one_tile, 0)
    for at in range(groups):
        total = jnp.sum(acc[:, at * LANES : (at + 1) * LANES], axis=0, keepdims=True)
        for copy in range(copies):
            out_ref[copy, at : at + 1, :] = total
    if has_extra:
        extra = extra_ref[...]
        for copy in range(copies):
            out_ref[copy, groups:, :] = extra


def sweep(parts, extra, protos, near, far, copies, tile=256):
    count = protos.shape[0]
    blocks, rows, _ = near.shape
    groups = blocks * rows // LANES
    sent = groups if extra is None else groups + extra.shape[0]
    args = [a for a in (parts, extra) if a is not None] + [protos, near, far]
    return pl.pallas_call(
        functools.partial(sweep_kernel, copies, tile, parts is not None, extra is not None),
        in_specs=[vmem()] * len(args),
        out_specs=[vmem()] * 2,
        out_shape=[
            jax.ShapeDtypeStruct((count, LANES), F32),
            jax.ShapeDtypeStruct((copies, sent, LANES), F32),
        ],
        scratch_shapes=[
            pltpu.VMEM((groups, LANES), F32),
            pltpu.VMEM((tile, blocks * rows), F32),
            pltpu.VMEM((8, blocks * rows), F32),
        ],
        compiler_params=params(24),
        name="sweep",
    )(*args)


def totals_kernel(tile, protos_ref, stud_ref, out_ref, acc):
    acc[...] = jnp.zeros_like(acc)
    blocks, rows, _ = stud_ref.shape

    def one_tile(step, carry):
        protos = protos_ref[pl.ds(pl.multiple_of(step * tile, tile), tile), :]
        for block in range(blocks):
            logits = dot_nt(protos, stud_ref[block])
            acc[:, block * rows : (block + 1) * rows] += fold_rows(jnp.exp2(logits * SSCALE))
        return carry

    lax.fori_loop(0, protos_ref.shape[0] // tile, one_tile, 0)
    for at in range(blocks * rows // LANES):
        out_ref[at : at + 1, :] = jnp.sum(
            acc[:, at * LANES : (at + 1) * LANES], axis=0, keepdims=True
        )


def totals(protos, stud, tile=512):
    count, depth = protos.shape
    blocks, rows, _ = stud.shape
    groups = blocks * rows // LANES
    return pl.pallas_call(
        functools.partial(totals_kernel, tile),
        in_specs=[vmem()] * 2,
        out_specs=vmem(),
        out_shape=jax.ShapeDtypeStruct((groups, LANES), F32),
        scratch_shapes=[pltpu.VMEM((8, blocks * rows), F32)],
        compiler_params=params(24),
        cost_estimate=pl.CostEstimate(
            flops=2 * count * depth * blocks * rows,
            bytes_accessed=4 * MIB,
            transcendentals=count * blocks * rows,
        ),
        name="totals",
    )(protos, stud)


def hop_kernel(copies, in_ref, out_ref):
    total = jnp.sum(in_ref[...], axis=0)
    for copy in range(copies):
        out_ref[copy] = total


def hop(parts, copies):
    return pl.pallas_call(
        functools.partial(hop_kernel, copies),
        in_specs=[vmem()],
        out_specs=vmem(),
        out_shape=jax.ShapeDtypeStruct((copies,) + parts.shape[1:], F32),
        compiler_params=params(4),
        name="hop",
    )(parts)


def exchange(parts, axes):
    return lax.all_to_all(parts, axes, 0, 0, tiled=True)


def spread(parts, pillar):
    return exchange(hop(exchange(parts, PLANE), pillar), PILLAR)


def grad_kernel(
    tile, core_ref, parts_ref, col_ref, protos_ref, near_protos_ref, cols_ref, near_ref, far_ref, stud_ref,
    mine_ref, other_ref, pgrad_ref, scale, norm, diff,
):
    blocks, rows, _ = near_ref.shape
    per = rows // LANES
    groups = blocks * per
    core = core_ref[0]
    sums = LOG_INV - jnp.log2(jnp.sum(parts_ref[...], axis=0))
    scale[...] = sums[:groups]
    norm[...] = sums[groups:]
    mine_ref[...] = jnp.zeros_like(mine_ref)
    other_ref[...] = jnp.zeros_like(other_ref)

    def one_tile(step, carry):
        here = pl.ds(pl.multiple_of(step * tile, tile), tile)
        log_col = jnp.log2(col_ref[here, :])
        for block in range(blocks):
            teach_logits = dot_nt(near_protos_ref[here, :], rows_of(near_ref, far_ref, block))
            stud_logits = dot_nt(protos_ref[here, :], stud_ref[block])
            for part in range(per):
                at = block * per + part
                lanes = slice(part * LANES, (part + 1) * LANES)
                target = jnp.exp2(teach_logits[:, lanes] * TSCALE + (scale[at : at + 1, :] + log_col))
                prob = jnp.exp2(stud_logits[:, lanes] * SSCALE + norm[at : at + 1, :])
                diff[:, at * LANES : (at + 1) * LANES] = (prob - target).astype(BF16)
        cols = cols_ref[:, here]
        for pair in range(blocks // 2):
            for first, ref in ((core, mine_ref), (1 - core, other_ref)):
                start = pl.multiple_of((2 * pair + first) * rows, rows)
                ref[pair] += dot(cols, diff[:, pl.ds(start, rows)])
        stud = stud_ref[...].reshape(blocks * rows, stud_ref.shape[2])
        pgrad_ref[:, here] = (4096.0 * dot(diff[...], stud)).T
        return carry

    lax.fori_loop(0, protos_ref.shape[0] // tile, one_tile, 0)


def gradients(core, parts, col, protos, near_protos, cols, near, far, stud, tile=256):
    count, depth = protos.shape
    blocks, rows, _ = near.shape
    groups = blocks * rows // LANES
    return pl.pallas_call(
        functools.partial(grad_kernel, tile),
        in_specs=[smem()] + [vmem()] * 8,
        out_specs=[vmem()] * 3,
        out_shape=[
            jax.ShapeDtypeStruct((blocks // 2, depth, rows), F32),
            jax.ShapeDtypeStruct((blocks // 2, depth, rows), F32),
            jax.ShapeDtypeStruct((depth, count), F32),
        ],
        scratch_shapes=[
            pltpu.VMEM((groups, LANES), F32),
            pltpu.VMEM((groups, LANES), F32),
            pltpu.VMEM((tile, blocks * rows), BF16),
        ],
        compiler_params=params(32),
        name="gradients",
    )(core, parts, col, protos, near_protos, cols, near, far, stud)


def swap(value):
    return lax.ppermute(value, "c", [(0, 1), (1, 0)])


def turn(value, by, size):
    return lax.ppermute(value, "z", [(i, (i + by) % size) for i in range(size)])


def copied(value, count):
    return jnp.broadcast_to(value[None], (count,) + value.shape)


def on_device(size, teacher_feats, student_feats, proto_weight):
    depth, held = proto_weight.shape
    devices = size["yl"] * size["x"] * size["c"]
    chips = size["yl"] * size["x"]
    plane = chips * size["yh"]
    pillar = size["z"] * size["c"]
    count = held // devices
    half = depth // 2
    rows = teacher_feats.shape[0]
    core = lax.axis_index("c")
    level = lax.axis_index("z")

    unit = unit_rows(teacher_feats)
    own = lax.dynamic_slice(unit, (0, core * half), (rows, half))
    given = swap(lax.dynamic_slice(unit, (0, (1 - core) * half), (rows, half)))
    both = jnp.where(core == 0, jnp.stack([own, given]), jnp.stack([given, own]))
    near = exchange(copied(both, chips), CHIPS).reshape(devices, rows, half)
    far = swap(near)

    mine = lax.axis_index(DP)
    cols = unit_cols(lax.dynamic_slice(proto_weight, (0, mine * count), (depth, count)))
    protos = cols.T
    near_cols = lax.dynamic_slice(jnp.concatenate([cols, cols]), (core * half, 0), (depth, count))
    near_protos = near_cols.T

    stud_unit, near = lax.optimization_barrier((unit_rows(student_feats), near))
    stud = lax.all_gather(stud_unit, DP)

    parts = None
    extra = None
    for step in range(ITERS):
        if step == ITERS - 1:
            extra = totals(protos, stud)
        col, copies = sweep(parts, extra, near_protos, near, far, plane)
        parts = spread(copies, pillar)

    mine_feat, other_feat, pgrad = gradients(
        core.reshape(1), parts, col, protos, near_protos, cols, near, far, stud
    )

    pgrad = exchange(pgrad.reshape(devices, depth // devices, count), DP)
    proto_grad = pgrad.transpose(1, 0, 2).reshape(depth // devices, held)

    feat = mine_feat + swap(other_feat)
    quarter = depth // size["z"]

    def cut(by):
        return lax.dynamic_slice_in_dim(feat, (level + by) % size["z"] * quarter, quarter, 1)

    feat = cut(0) + sum(turn(cut(by), by, size["z"]) for by in range(1, size["z"]))
    feat = feat.reshape(plane, quarter // size["yh"], rows)
    feat = jnp.sum(exchange(feat, PLANE), axis=0)
    feat = exchange(copied(feat, size["z"] * size["yh"]), PROTO)
    feature_grad = 512.0 * feat.reshape(depth, rows).T
    return feature_grad, proto_grad


def solution(mesh):
    split = jax.sharding.Mesh(mesh.devices.reshape(2, 4, 2, 4, 2), AXES)
    return jax.shard_map(
        functools.partial(on_device, dict(split.shape)),
        mesh=split,
        in_specs=(P(DP, None), P(DP, None), P(None, PROTO)),
        out_specs=(P(DP, None), P(DP, PROTO)),
        check_vma=False,
    )
```

```python
import functools
import math

import jax
import jax.numpy as jnp
import numpy as np
from jax import lax
from jax.experimental import pallas as pl
from jax.experimental.pallas import tpu as pltpu
from jax.sharding import PartitionSpec as P

ITERS = 3
EPS = 1e-06
TEACH = float(np.float32(0.07))
STUD = float(np.float32(0.1))
LOG2E = math.log2(math.e)
TSCALE = LOG2E / TEACH
SSCALE = LOG2E / STUD
LOG_INV = -math.log2(STUD)
F32 = jnp.float32
BF16 = jnp.bfloat16
LANES = 128
MIB = 1024 * 1024
AXES = ("yl", "x", "c", "z", "yh")
DP = ("yl", "x", "c")
PROTO = ("z", "yh")
CHIPS = ("yl", "x")
PLANE = ("yl", "x", "yh")
PILLAR = ("z", "c")


def unit_rows(feats):
    wide = feats.astype(F32)
    squares = jnp.sum(wide * wide, axis=1, keepdims=True)
    return (wide * lax.rsqrt(squares + EPS)).astype(BF16)


def dot(a, b):
    return jnp.dot(a, b, preferred_element_type=F32)


def dot_nt(a, b):
    return lax.dot_general(a, b, (((1,), (1,)), ((), ())), preferred_element_type=F32)


def fold_rows(value):
    return jnp.sum(value.reshape(value.shape[0] // 8, 8, value.shape[1]), axis=0)


def params(mib):
    return pltpu.CompilerParams(vmem_limit_bytes=mib * MIB)


def vmem():
    return pl.BlockSpec(memory_space=pltpu.VMEM)


def smem():
    return pl.BlockSpec(memory_space=pltpu.SMEM)


def rows_of(near_ref, far_ref, block):
    return jnp.concatenate([near_ref[block], far_ref[block]], axis=1)


def sweep_kernel(copies, tile, has_parts, has_extra, *refs):
    refs = list(refs)
    parts_ref = refs.pop(0) if has_parts else None
    extra_ref = refs.pop(0) if has_extra else None
    protos_ref, near_ref, far_ref, col_ref, out_ref, scale, kern, acc = refs
    blocks, rows, _ = near_ref.shape
    per = rows // LANES
    groups = blocks * per
    if has_parts:
        scale[...] = 1.0 / jnp.sum(parts_ref[...], axis=0)
    else:
        scale[...] = jnp.ones_like(scale)
    acc[...] = jnp.zeros_like(acc)

    def one_tile(step, carry):
        here = pl.ds(pl.multiple_of(step * tile, tile), tile)
        protos = protos_ref[here, :]
        col_acc = jnp.zeros((tile, LANES), F32)
        for block in range(blocks):
            logits = dot_nt(protos, rows_of(near_ref, far_ref, block))
            for part in range(per):
                value = jnp.exp2(logits[:, part * LANES : (part + 1) * LANES] * TSCALE)
                at = block * per + part
                kern[:, at * LANES : (at + 1) * LANES] = value
                col_acc = col_acc + value * scale[at : at + 1, :]
        col = 1.0 / jnp.sum(col_acc, axis=1, keepdims=True)
        wide_col = jnp.broadcast_to(col, (tile, LANES))
        col_ref[here, :] = wide_col
        for at in range(groups):
            lanes = slice(at * LANES, (at + 1) * LANES)
            acc[:, lanes] += fold_rows(kern[:, lanes] * wide_col)
        return carry

    lax.fori_loop(0, protos_ref.shape[0] // tile, one_tile, 0)
    for at in range(groups):
        total = jnp.sum(acc[:, at * LANES : (at + 1) * LANES], axis=0, keepdims=True)
        for copy in range(copies):
            out_ref[copy, at : at + 1, :] = total
    if has_extra:
        extra = extra_ref[...]
        for copy in range(copies):
            out_ref[copy, groups:, :] = extra


def sweep(parts, extra, protos, near, far, copies, tile=256):
    count = protos.shape[0]
    blocks, rows, _ = near.shape
    groups = blocks * rows // LANES
    sent = groups if extra is None else groups + extra.shape[0]
    args = [a for a in (parts, extra) if a is not None] + [protos, near, far]
    return pl.pallas_call(
        functools.partial(sweep_kernel, copies, tile, parts is not None, extra is not None),
        in_specs=[vmem()] * len(args),
        out_specs=[vmem()] * 2,
        out_shape=[
            jax.ShapeDtypeStruct((count, LANES), F32),
            jax.ShapeDtypeStruct((copies, sent, LANES), F32),
        ],
        scratch_shapes=[
            pltpu.VMEM((groups, LANES), F32),
            pltpu.VMEM((tile, blocks * rows), F32),
            pltpu.VMEM((8, blocks * rows), F32),
        ],
        compiler_params=params(24),
        name="sweep",
    )(*args)


def totals_kernel(tile, protos_ref, stud_ref, out_ref, acc):
    acc[...] = jnp.zeros_like(acc)
    blocks, rows, _ = stud_ref.shape

    def one_tile(step, carry):
        protos = protos_ref[pl.ds(pl.multiple_of(step * tile, tile), tile), :]
        for block in range(blocks):
            logits = dot_nt(protos, stud_ref[block])
            acc[:, block * rows : (block + 1) * rows] += fold_rows(jnp.exp2(logits * SSCALE))
        return carry

    lax.fori_loop(0, protos_ref.shape[0] // tile, one_tile, 0)
    for at in range(blocks * rows // LANES):
        out_ref[at : at + 1, :] = jnp.sum(
            acc[:, at * LANES : (at + 1) * LANES], axis=0, keepdims=True
        )


def totals(protos, stud, tile=512):
    count, depth = protos.shape
    blocks, rows, _ = stud.shape
    groups = blocks * rows // LANES
    return pl.pallas_call(
        functools.partial(totals_kernel, tile),
        in_specs=[vmem()] * 2,
        out_specs=vmem(),
        out_shape=jax.ShapeDtypeStruct((groups, LANES), F32),
        scratch_shapes=[pltpu.VMEM((8, blocks * rows), F32)],
        compiler_params=params(24),
        cost_estimate=pl.CostEstimate(
            flops=2 * count * depth * blocks * rows,
            bytes_accessed=4 * MIB,
            transcendentals=count * blocks * rows,
        ),
        name="totals",
    )(protos, stud)


def hop_kernel(copies, in_ref, out_ref):
    total = jnp.sum(in_ref[...], axis=0)
    for copy in range(copies):
        out_ref[copy] = total


def hop(parts, copies):
    return pl.pallas_call(
        functools.partial(hop_kernel, copies),
        in_specs=[vmem()],
        out_specs=vmem(),
        out_shape=jax.ShapeDtypeStruct((copies,) + parts.shape[1:], F32),
        compiler_params=params(4),
        name="hop",
    )(parts)


def exchange(parts, axes):
    return lax.all_to_all(parts, axes, 0, 0, tiled=True)


def spread(parts, pillar):
    return exchange(hop(exchange(parts, PLANE), pillar), PILLAR)


def diff_kernel(
    tile, core_ref, parts_ref, col_ref, protos_ref, near_protos_ref, cols_ref, near_ref, far_ref, stud_ref,
    out_ref, mine_ref, other_ref, scale, norm, diff, sems,
):
    blocks, rows, _ = near_ref.shape
    per = rows // LANES
    groups = blocks * per
    core = core_ref[0]
    sums = LOG_INV - jnp.log2(jnp.sum(parts_ref[...], axis=0))
    scale[...] = sums[:groups]
    norm[...] = sums[groups:]
    tiles = protos_ref.shape[0] // tile

    def span(step):
        return pl.ds(pl.multiple_of(step * tile, tile), tile)

    def store(step):
        return pltpu.make_async_copy(diff.at[span(step), :], out_ref.at[span(step), :], sems.at[step])

    def one_tile(step, carry):
        here = span(step)
        log_col = jnp.log2(col_ref[here, :])
        for block in range(blocks):
            teach_logits = dot_nt(near_protos_ref[here, :], rows_of(near_ref, far_ref, block))
            stud_logits = dot_nt(protos_ref[here, :], stud_ref[block])
            for part in range(per):
                at = block * per + part
                lanes = slice(part * LANES, (part + 1) * LANES)
                target = jnp.exp2(teach_logits[:, lanes] * TSCALE + (scale[at : at + 1, :] + log_col))
                prob = jnp.exp2(stud_logits[:, lanes] * SSCALE + norm[at : at + 1, :])
                diff[here, at * LANES : (at + 1) * LANES] = (prob - target).astype(BF16)
        store(step).start()
        return carry

    lax.fori_loop(0, tiles, one_tile, 0)

    def one_pair(pair, carry):
        for first, ref in ((core, mine_ref), (1 - core, other_ref)):
            start = pl.multiple_of((2 * pair + first) * rows, rows)
            ref[pair] = dot(cols_ref[...], diff[:, pl.ds(start, rows)])
        return carry

    lax.fori_loop(0, blocks // 2, one_pair, 0)

    def finish(step, carry):
        store(step).wait()
        return carry

    lax.fori_loop(0, tiles, finish, 0)


def differences(core, parts, col, protos, near_protos, cols, near, far, stud, tile=512):
    count, depth = protos.shape
    blocks, rows, _ = near.shape
    groups = blocks * rows // LANES
    return pl.pallas_call(
        functools.partial(diff_kernel, tile),
        in_specs=[smem()] + [vmem()] * 8,
        out_specs=[pl.BlockSpec(memory_space=pl.ANY)] + [vmem()] * 2,
        out_shape=[
            jax.ShapeDtypeStruct((count, blocks * rows), BF16),
            jax.ShapeDtypeStruct((blocks // 2, depth, rows), F32),
            jax.ShapeDtypeStruct((blocks // 2, depth, rows), F32),
        ],
        scratch_shapes=[
            pltpu.VMEM((groups, LANES), F32),
            pltpu.VMEM((groups, LANES), F32),
            pltpu.VMEM((count, blocks * rows), BF16),
            pltpu.SemaphoreType.DMA((count // tile,)),
        ],
        compiler_params=params(40),
        name="differences",
    )(core, parts, col, protos, near_protos, cols, near, far, stud)


def pgrad_kernel(tile, diff_ref, stud_ref, out_ref, diff, sems):
    tiles = diff.shape[0] // tile
    blocks, rows, depth = stud_ref.shape

    def span(step):
        return pl.ds(pl.multiple_of(step * tile, tile), tile)

    def load(step):
        return pltpu.make_async_copy(diff_ref.at[span(step), :], diff.at[span(step), :], sems.at[step])

    def begin(step, carry):
        load(step).start()
        return carry

    def one_tile(step, carry):
        load(step).wait()
        stud = stud_ref[...].reshape(blocks * rows, depth)
        out_ref[:, span(step)] = (4096.0 * dot(diff[span(step), :], stud)).T
        return carry

    lax.fori_loop(0, tiles, begin, 0)
    lax.fori_loop(0, tiles, one_tile, 0)


def proto_part(diff, stud, tile=512):
    count, total = diff.shape
    depth = stud.shape[2]
    return pl.pallas_call(
        functools.partial(pgrad_kernel, tile),
        in_specs=[pl.BlockSpec(memory_space=pl.ANY), vmem()],
        out_specs=vmem(),
        out_shape=jax.ShapeDtypeStruct((depth, count), F32),
        scratch_shapes=[pltpu.VMEM((count, total), BF16), pltpu.SemaphoreType.DMA((count // tile,))],
        compiler_params=params(32),
        cost_estimate=pl.CostEstimate(
            flops=2 * count * total * depth, bytes_accessed=20 * MIB, transcendentals=0
        ),
        name="proto_part",
    )(diff, stud)


def protos_kernel(place_ref, weight_ref, cols_ref, protos_ref, near_ref, held, sem):
    depth, count = cols_ref.shape
    start = pl.multiple_of(place_ref[0] * count, count)
    copy = pltpu.make_async_copy(weight_ref.at[:, pl.ds(start, count)], held, sem)
    copy.start()
    copy.wait()
    tile = 512
    half = depth // 2
    first = place_ref[1] == 0
    for at in range(0, count, tile):
        wide = held[:, at : at + tile].astype(F32)
        squares = jnp.sum(wide * wide, axis=0, keepdims=True)
        unit = wide * lax.rsqrt(squares + EPS)
        cols_ref[:, at : at + tile] = unit.astype(BF16)
        turned = unit.T
        low = turned[:, :half]
        high = turned[:, half:]
        protos_ref[at : at + tile, :] = turned.astype(BF16)
        near_ref[at : at + tile, :half] = jnp.where(first, low, high).astype(BF16)
        near_ref[at : at + tile, half:] = jnp.where(first, high, low).astype(BF16)


def unit_protos(place, weight, count):
    depth = weight.shape[0]
    return pl.pallas_call(
        protos_kernel,
        in_specs=[smem(), pl.BlockSpec(memory_space=pl.ANY)],
        out_specs=[vmem()] * 3,
        out_shape=[
            jax.ShapeDtypeStruct((depth, count), BF16),
            jax.ShapeDtypeStruct((count, depth), BF16),
            jax.ShapeDtypeStruct((count, depth), BF16),
        ],
        scratch_shapes=[pltpu.VMEM((depth, count), BF16), pltpu.SemaphoreType.DMA(())],
        compiler_params=params(24),
        cost_estimate=pl.CostEstimate(
            flops=8 * count * depth, bytes_accessed=20 * MIB, transcendentals=count
        ),
        name="unit_protos",
    )(place, weight)


def swap(value):
    return lax.ppermute(value, "c", [(0, 1), (1, 0)])


def turn(value, by, size):
    return lax.ppermute(value, "z", [(i, (i + by) % size) for i in range(size)])


def copied(value, count):
    return jnp.broadcast_to(value[None], (count,) + value.shape)


def on_device(size, teacher_feats, student_feats, proto_weight):
    depth, held = proto_weight.shape
    devices = size["yl"] * size["x"] * size["c"]
    chips = size["yl"] * size["x"]
    plane = chips * size["yh"]
    pillar = size["z"] * size["c"]
    count = held // devices
    half = depth // 2
    rows = teacher_feats.shape[0]
    core = lax.axis_index("c")
    level = lax.axis_index("z")

    unit = unit_rows(teacher_feats)
    own = lax.dynamic_slice(unit, (0, core * half), (rows, half))
    given = swap(lax.dynamic_slice(unit, (0, (1 - core) * half), (rows, half)))
    both = jnp.where(core == 0, jnp.stack([own, given]), jnp.stack([given, own]))
    near = exchange(copied(both, chips), CHIPS).reshape(devices, rows, half)
    far = swap(near)

    mine = lax.axis_index(DP)
    cols, protos, near_protos = unit_protos(jnp.stack([mine, core]), proto_weight, count)

    stud_unit, near = lax.optimization_barrier((unit_rows(student_feats), near))
    stud = lax.all_gather(stud_unit, DP)

    parts = None
    extra = None
    for step in range(ITERS):
        if step == ITERS - 1:
            extra = totals(protos, stud)
        col, copies = sweep(parts, extra, near_protos, near, far, plane)
        parts = spread(copies, pillar)

    diff, mine_feat, other_feat = differences(
        core.reshape(1), parts, col, protos, near_protos, cols, near, far, stud
    )
    given_feat = swap(other_feat)
    pgrad = proto_part(diff, stud)
    quarter = depth // size["z"]

    def cut(by):
        start = (level + by) % size["z"] * quarter
        shares = [lax.dynamic_slice_in_dim(part, start, quarter, 1) for part in (mine_feat, given_feat)]
        return shares[0] + shares[1]

    turned = [turn(cut(by), by, size["z"]) for by in range(1, size["z"])]
    pgrad = exchange(pgrad.reshape(devices, depth // devices, count), DP)
    *turned, pgrad = lax.optimization_barrier((*turned, pgrad))
    proto_grad = pgrad.transpose(1, 0, 2).reshape(depth // devices, held)
    feat = cut(0) + sum(turned)
    feat = feat.reshape(plane, quarter // size["yh"], rows)
    feat = jnp.sum(exchange(feat, PLANE), axis=0)
    feat = exchange(copied(feat, size["z"] * size["yh"]), PROTO)
    feature_grad = 512.0 * feat.reshape(depth, rows).T
    return feature_grad, proto_grad


def solution(mesh):
    split = jax.sharding.Mesh(mesh.devices.reshape(2, 4, 2, 4, 2), AXES)
    return jax.shard_map(
        functools.partial(on_device, dict(split.shape)),
        mesh=split,
        in_specs=(P(DP, None), P(DP, None), P(None, PROTO)),
        out_specs=(P(DP, None), P(DP, PROTO)),
        check_vma=False,
    )
```

```python
import functools
import math

import jax
import jax.numpy as jnp
import numpy as np
from jax import lax
from jax.experimental import pallas as pl
from jax.experimental.pallas import tpu as pltpu
from jax.sharding import PartitionSpec as P

ITERS = 3
EPS = 1e-06
TEACH = float(np.float32(0.07))
STUD = float(np.float32(0.1))
LOG2E = math.log2(math.e)
TSCALE = LOG2E / TEACH
SSCALE = LOG2E / STUD
LOG_INV = -math.log2(STUD)
F32 = jnp.float32
BF16 = jnp.bfloat16
LANES = 128
MIB = 1024 * 1024
AXES = ("yl", "x", "c", "z", "yh")
DP = ("yl", "x", "c")
PROTO = ("z", "yh")
CHIPS = ("yl", "x")
PLANE = ("yl", "x", "yh")
PILLAR = ("z", "c")


def unit_rows(feats):
    wide = feats.astype(F32)
    squares = jnp.sum(wide * wide, axis=1, keepdims=True)
    return (wide * lax.rsqrt(squares + EPS)).astype(BF16)


def dot(a, b):
    return jnp.dot(a, b, preferred_element_type=F32)


def dot_nt(a, b):
    return lax.dot_general(a, b, (((1,), (1,)), ((), ())), preferred_element_type=F32)


def fold_rows(value):
    return jnp.sum(value.reshape(value.shape[0] // 8, 8, value.shape[1]), axis=0)


def params(mib):
    return pltpu.CompilerParams(vmem_limit_bytes=mib * MIB)


def vmem():
    return pl.BlockSpec(memory_space=pltpu.VMEM)


def smem():
    return pl.BlockSpec(memory_space=pltpu.SMEM)


def rows_of(near_ref, far_ref, block):
    return jnp.concatenate([near_ref[block], far_ref[block]], axis=1)


def sweep_kernel(copies, tile, has_parts, has_extra, *refs):
    refs = list(refs)
    parts_ref = refs.pop(0) if has_parts else None
    extra_ref = refs.pop(0) if has_extra else None
    protos_ref, near_ref, far_ref, col_ref, out_ref, scale, kern, acc = refs
    blocks, rows, _ = near_ref.shape
    per = rows // LANES
    groups = blocks * per
    if has_parts:
        scale[...] = 1.0 / jnp.sum(parts_ref[...], axis=0)
    else:
        scale[...] = jnp.ones_like(scale)
    acc[...] = jnp.zeros_like(acc)

    def one_tile(step, carry):
        here = pl.ds(pl.multiple_of(step * tile, tile), tile)
        protos = protos_ref[here, :]
        col_acc = jnp.zeros((tile, LANES), F32)
        for block in range(blocks):
            logits = dot_nt(protos, rows_of(near_ref, far_ref, block))
            for part in range(per):
                value = jnp.exp2(logits[:, part * LANES : (part + 1) * LANES] * TSCALE)
                at = block * per + part
                kern[:, at * LANES : (at + 1) * LANES] = value
                col_acc = col_acc + value * scale[at : at + 1, :]
        col = 1.0 / jnp.sum(col_acc, axis=1, keepdims=True)
        wide_col = jnp.broadcast_to(col, (tile, LANES))
        col_ref[here, :] = wide_col
        for at in range(groups):
            lanes = slice(at * LANES, (at + 1) * LANES)
            acc[:, lanes] += fold_rows(kern[:, lanes] * wide_col)
        return carry

    lax.fori_loop(0, protos_ref.shape[0] // tile, one_tile, 0)
    for at in range(groups):
        total = jnp.sum(acc[:, at * LANES : (at + 1) * LANES], axis=0, keepdims=True)
        for copy in range(copies):
            out_ref[copy, at : at + 1, :] = total
    if has_extra:
        extra = extra_ref[...]
        for copy in range(copies):
            out_ref[copy, groups:, :] = extra


def sweep(parts, extra, protos, near, far, copies, tile=256):
    count = protos.shape[0]
    blocks, rows, _ = near.shape
    groups = blocks * rows // LANES
    sent = groups if extra is None else groups + extra.shape[0]
    args = [a for a in (parts, extra) if a is not None] + [protos, near, far]
    return pl.pallas_call(
        functools.partial(sweep_kernel, copies, tile, parts is not None, extra is not None),
        in_specs=[vmem()] * len(args),
        out_specs=[vmem()] * 2,
        out_shape=[
            jax.ShapeDtypeStruct((count, LANES), F32),
            jax.ShapeDtypeStruct((copies, sent, LANES), F32),
        ],
        scratch_shapes=[
            pltpu.VMEM((groups, LANES), F32),
            pltpu.VMEM((tile, blocks * rows), F32),
            pltpu.VMEM((8, blocks * rows), F32),
        ],
        compiler_params=params(24),
        name="sweep",
    )(*args)


def totals_kernel(tile, protos_ref, stud_ref, out_ref, acc):
    acc[...] = jnp.zeros_like(acc)
    blocks, rows, _ = stud_ref.shape

    def one_tile(step, carry):
        protos = protos_ref[pl.ds(pl.multiple_of(step * tile, tile), tile), :]
        for block in range(blocks):
            logits = dot_nt(protos, stud_ref[block])
            acc[:, block * rows : (block + 1) * rows] += fold_rows(jnp.exp2(logits * SSCALE))
        return carry

    lax.fori_loop(0, protos_ref.shape[0] // tile, one_tile, 0)
    for at in range(blocks * rows // LANES):
        out_ref[at : at + 1, :] = jnp.sum(
            acc[:, at * LANES : (at + 1) * LANES], axis=0, keepdims=True
        )


def totals(protos, stud, tile=512):
    count, depth = protos.shape
    blocks, rows, _ = stud.shape
    groups = blocks * rows // LANES
    return pl.pallas_call(
        functools.partial(totals_kernel, tile),
        in_specs=[vmem()] * 2,
        out_specs=vmem(),
        out_shape=jax.ShapeDtypeStruct((groups, LANES), F32),
        scratch_shapes=[pltpu.VMEM((8, blocks * rows), F32)],
        compiler_params=params(24),
        cost_estimate=pl.CostEstimate(
            flops=2 * count * depth * blocks * rows,
            bytes_accessed=4 * MIB,
            transcendentals=count * blocks * rows,
        ),
        name="totals",
    )(protos, stud)


def hop_kernel(copies, in_ref, out_ref):
    total = jnp.sum(in_ref[...], axis=0)
    for copy in range(copies):
        out_ref[copy] = total


def hop(parts, copies):
    return pl.pallas_call(
        functools.partial(hop_kernel, copies),
        in_specs=[vmem()],
        out_specs=vmem(),
        out_shape=jax.ShapeDtypeStruct((copies,) + parts.shape[1:], F32),
        compiler_params=params(4),
        name="hop",
    )(parts)


def exchange(parts, axes):
    return lax.all_to_all(parts, axes, 0, 0, tiled=True)


def spread(parts, pillar):
    return exchange(hop(exchange(parts, PLANE), pillar), PILLAR)


def diff_kernel(
    tile, core_ref, parts_ref, col_ref, protos_ref, near_protos_ref, cols_ref, near_ref, far_ref, stud_ref,
    out_ref, mine_ref, other_ref, scale, norm, diff, sems,
):
    blocks, rows, _ = near_ref.shape
    per = rows // LANES
    groups = blocks * per
    core = core_ref[0]
    sums = LOG_INV - jnp.log2(jnp.sum(parts_ref[...], axis=0))
    scale[...] = sums[:groups]
    norm[...] = sums[groups:]
    tiles = protos_ref.shape[0] // tile

    def span(step):
        return pl.ds(pl.multiple_of(step * tile, tile), tile)

    def store(step):
        return pltpu.make_async_copy(diff.at[span(step), :], out_ref.at[span(step), :], sems.at[step])

    def one_tile(step, carry):
        here = span(step)
        log_col = jnp.log2(col_ref[here, :])
        for block in range(blocks):
            teach_logits = dot_nt(near_protos_ref[here, :], rows_of(near_ref, far_ref, block))
            stud_logits = dot_nt(protos_ref[here, :], stud_ref[block])
            for part in range(per):
                at = block * per + part
                lanes = slice(part * LANES, (part + 1) * LANES)
                target = jnp.exp2(teach_logits[:, lanes] * TSCALE + (scale[at : at + 1, :] + log_col))
                prob = jnp.exp2(stud_logits[:, lanes] * SSCALE + norm[at : at + 1, :])
                diff[here, at * LANES : (at + 1) * LANES] = (prob - target).astype(BF16)
        store(step).start()
        return carry

    lax.fori_loop(0, tiles, one_tile, 0)

    def one_pair(pair, carry):
        for first, ref in ((core, mine_ref), (1 - core, other_ref)):
            start = pl.multiple_of((2 * pair + first) * rows, rows)
            ref[pair] = dot(cols_ref[...], diff[:, pl.ds(start, rows)])
        return carry

    lax.fori_loop(0, blocks // 2, one_pair, 0)

    def finish(step, carry):
        store(step).wait()
        return carry

    lax.fori_loop(0, tiles, finish, 0)


def differences(core, parts, col, protos, near_protos, cols, near, far, stud, tile=512):
    count, depth = protos.shape
    blocks, rows, _ = near.shape
    groups = blocks * rows // LANES
    return pl.pallas_call(
        functools.partial(diff_kernel, tile),
        in_specs=[smem()] + [vmem()] * 8,
        out_specs=[pl.BlockSpec(memory_space=pl.ANY)] + [vmem()] * 2,
        out_shape=[
            jax.ShapeDtypeStruct((count, blocks * rows), BF16),
            jax.ShapeDtypeStruct((blocks // 2, depth, rows), F32),
            jax.ShapeDtypeStruct((blocks // 2, depth, rows), F32),
        ],
        scratch_shapes=[
            pltpu.VMEM((groups, LANES), F32),
            pltpu.VMEM((groups, LANES), F32),
            pltpu.VMEM((count, blocks * rows), BF16),
            pltpu.SemaphoreType.DMA((count // tile,)),
        ],
        compiler_params=params(40),
        name="differences",
    )(core, parts, col, protos, near_protos, cols, near, far, stud)


SPAN = 250.0
FLOOR = 125.0


def encode(values):
    top = jnp.maximum(jnp.max(jnp.abs(values), axis=0, keepdims=True), 2.0**-120)
    power = jnp.minimum(jnp.ceil(jnp.log2(top)), 126.0)
    size = jnp.exp2(jnp.minimum(jnp.abs(values) * jnp.exp2(-power), 1.0) * SPAN - FLOOR)
    return jnp.where(values < 0, -size, size).astype(BF16), power


def decode(code, power):
    wide = code.astype(F32)
    size = (jnp.log2(jnp.abs(wide)) + FLOOR) * (1.0 / SPAN) * jnp.exp2(power)
    return jnp.where(wide < 0, -size, size)


def decode_kernel(code_ref, out_ref):
    sources, share, width = code_ref.shape
    count = out_ref.shape[1] // sources

    def one_source(source, carry):
        powers = code_ref[source, :, count:].astype(F32)
        for part in range(count // LANES):
            code = code_ref[source, :, part * LANES : (part + 1) * LANES]
            start = pl.multiple_of(source * count + part * LANES, LANES)
            out_ref[:, pl.ds(start, LANES)] = decode(code, powers[part : part + 1, :])
        return carry

    lax.fori_loop(0, sources, one_source, 0)


def decoded(codes):
    sources, share, width = codes.shape
    return pl.pallas_call(
        decode_kernel,
        in_specs=[vmem()],
        out_specs=vmem(),
        out_shape=jax.ShapeDtypeStruct((share, sources * (width - LANES)), F32),
        compiler_params=params(16),
        cost_estimate=pl.CostEstimate(flops=16 * sources * share * width, bytes_accessed=4 * MIB, transcendentals=0),
        name="decoded",
    )(codes)


def pgrad_kernel(tile, diff_ref, stud_ref, out_ref, diff, powers, sems):
    tiles = diff.shape[0] // tile
    blocks, rows, depth = stud_ref.shape

    def span(step):
        return pl.ds(pl.multiple_of(step * tile, tile), tile)

    def load(step):
        return pltpu.make_async_copy(diff_ref.at[span(step), :], diff.at[span(step), :], sems.at[step])

    def begin(step, carry):
        load(step).start()
        return carry

    def one_tile(step, carry):
        load(step).wait()
        stud = stud_ref[...].reshape(blocks * rows, depth)
        share = out_ref.shape[1]
        grads = (4096.0 * dot(diff[span(step), :], stud)).T
        for dest in range(depth // share):
            values = grads[dest * share : (dest + 1) * share, :]
            code, power = encode(values)
            out_ref[dest, :, span(step)] = code
            for part in range(tile // LANES):
                row = step * (tile // LANES) + part
                powers[dest, pl.ds(row, 1), :] = power[:, part * LANES : (part + 1) * LANES]
        return carry

    lax.fori_loop(0, tiles, begin, 0)
    lax.fori_loop(0, tiles, one_tile, 0)
    out_ref[:, :, diff.shape[0] :] = powers[...].astype(BF16)


def proto_part(diff, stud, dests, tile=512):
    count, total = diff.shape
    depth = stud.shape[2]
    return pl.pallas_call(
        functools.partial(pgrad_kernel, tile),
        in_specs=[pl.BlockSpec(memory_space=pl.ANY), vmem()],
        out_specs=vmem(),
        out_shape=jax.ShapeDtypeStruct((dests, depth // dests, count + LANES), BF16),
        scratch_shapes=[
            pltpu.VMEM((count, total), BF16),
            pltpu.VMEM((dests, count // LANES, LANES), F32),
            pltpu.SemaphoreType.DMA((count // tile,)),
        ],
        compiler_params=params(56),
        cost_estimate=pl.CostEstimate(
            flops=2 * count * total * depth, bytes_accessed=20 * MIB, transcendentals=0
        ),
        name="proto_part",
    )(diff, stud)


def protos_kernel(place_ref, weight_ref, cols_ref, protos_ref, near_ref, held, sem):
    depth, count = cols_ref.shape
    start = pl.multiple_of(place_ref[0] * count, count)
    copy = pltpu.make_async_copy(weight_ref.at[:, pl.ds(start, count)], held, sem)
    copy.start()
    copy.wait()
    tile = 512
    half = depth // 2
    first = place_ref[1] == 0
    for at in range(0, count, tile):
        wide = held[:, at : at + tile].astype(F32)
        squares = jnp.sum(wide * wide, axis=0, keepdims=True)
        unit = wide * lax.rsqrt(squares + EPS)
        cols_ref[:, at : at + tile] = unit.astype(BF16)
        turned = unit.T
        low = turned[:, :half]
        high = turned[:, half:]
        protos_ref[at : at + tile, :] = turned.astype(BF16)
        near_ref[at : at + tile, :half] = jnp.where(first, low, high).astype(BF16)
        near_ref[at : at + tile, half:] = jnp.where(first, high, low).astype(BF16)


def unit_protos(place, weight, count):
    depth = weight.shape[0]
    return pl.pallas_call(
        protos_kernel,
        in_specs=[smem(), pl.BlockSpec(memory_space=pl.ANY)],
        out_specs=[vmem()] * 3,
        out_shape=[
            jax.ShapeDtypeStruct((depth, count), BF16),
            jax.ShapeDtypeStruct((count, depth), BF16),
            jax.ShapeDtypeStruct((count, depth), BF16),
        ],
        scratch_shapes=[pltpu.VMEM((depth, count), BF16), pltpu.SemaphoreType.DMA(())],
        compiler_params=params(56),
        cost_estimate=pl.CostEstimate(
            flops=8 * count * depth, bytes_accessed=20 * MIB, transcendentals=count
        ),
        name="unit_protos",
    )(place, weight)


def swap(value):
    return lax.ppermute(value, "c", [(0, 1), (1, 0)])


def turn(value, by, size):
    return lax.ppermute(value, "z", [(i, (i + by) % size) for i in range(size)])


def copied(value, count):
    return jnp.broadcast_to(value[None], (count,) + value.shape)


def on_device(size, teacher_feats, student_feats, proto_weight):
    depth, held = proto_weight.shape
    devices = size["yl"] * size["x"] * size["c"]
    chips = size["yl"] * size["x"]
    plane = chips * size["yh"]
    pillar = size["z"] * size["c"]
    count = held // devices
    half = depth // 2
    rows = teacher_feats.shape[0]
    core = lax.axis_index("c")
    level = lax.axis_index("z")

    unit = unit_rows(teacher_feats)
    own = lax.dynamic_slice(unit, (0, core * half), (rows, half))
    given = swap(lax.dynamic_slice(unit, (0, (1 - core) * half), (rows, half)))
    both = jnp.where(core == 0, jnp.stack([own, given]), jnp.stack([given, own]))
    near = exchange(copied(both, chips), CHIPS).reshape(devices, rows, half)
    far = swap(near)

    mine = lax.axis_index(DP)
    cols, protos, near_protos = unit_protos(jnp.stack([mine, core]), proto_weight, count)

    stud_unit, near = lax.optimization_barrier((unit_rows(student_feats), near))
    stud = lax.all_gather(stud_unit, DP)

    parts = None
    extra = None
    for step in range(ITERS):
        if step == ITERS - 1:
            extra = totals(protos, stud)
        col, copies = sweep(parts, extra, near_protos, near, far, plane)
        parts = spread(copies, pillar)

    diff, mine_feat, other_feat = differences(
        core.reshape(1), parts, col, protos, near_protos, cols, near, far, stud
    )
    given_feat = swap(other_feat)
    quarter = depth // size["z"]

    def cut(by):
        start = (level + by) % size["z"] * quarter
        shares = [lax.dynamic_slice_in_dim(part, start, quarter, 1) for part in (mine_feat, given_feat)]
        return shares[0] + shares[1]

    cuts = [cut(by) for by in range(1, size["z"])]
    turned = [turn(part, by + 1, size["z"]) for by, part in enumerate(cuts)]
    codes = exchange(proto_part(diff, stud, devices), DP)
    *turned, codes = lax.optimization_barrier((*turned, codes))
    proto_grad = decoded(codes)
    feat = cut(0) + sum(turned)
    feat = feat.reshape(plane, quarter // size["yh"], rows)
    feat = jnp.sum(exchange(feat, PLANE), axis=0)
    feat = exchange(copied(feat, size["z"] * size["yh"]), PROTO)
    feature_grad = 512.0 * feat.reshape(depth, rows).T
    return feature_grad, proto_grad


def solution(mesh):
    split = jax.sharding.Mesh(mesh.devices.reshape(2, 4, 2, 4, 2), AXES)
    return jax.shard_map(
        functools.partial(on_device, dict(split.shape)),
        mesh=split,
        in_specs=(P(DP, None), P(DP, None), P(None, PROTO)),
        out_specs=(P(DP, None), P(DP, PROTO)),
        check_vma=False,
    )
```

```python
import functools
import math

import jax
import jax.numpy as jnp
import numpy as np
from jax import lax
from jax.experimental import pallas as pl
from jax.experimental.pallas import tpu as pltpu
from jax.sharding import PartitionSpec as P

ITERS = 3
EPS = 1e-06
TEACH = float(np.float32(0.07))
STUD = float(np.float32(0.1))
LOG2E = math.log2(math.e)
TSCALE = LOG2E / TEACH
SSCALE = LOG2E / STUD
LOG_INV = -math.log2(STUD)
F32 = jnp.float32
BF16 = jnp.bfloat16
LANES = 128
MIB = 1024 * 1024
AXES = ("yl", "x", "c", "z", "yh")
DP = ("yl", "x", "c")
PROTO = ("z", "yh")
CHIPS = ("yl", "x")
PLANE = ("yl", "x", "yh")
PILLAR = ("z", "c")


def unit_rows(feats):
    wide = feats.astype(F32)
    squares = jnp.sum(wide * wide, axis=1, keepdims=True)
    return (wide * lax.rsqrt(squares + EPS)).astype(BF16)


def dot(a, b):
    return jnp.dot(a, b, preferred_element_type=F32)


def dot_nt(a, b):
    return lax.dot_general(a, b, (((1,), (1,)), ((), ())), preferred_element_type=F32)


def fold_rows(value):
    return jnp.sum(value.reshape(value.shape[0] // 8, 8, value.shape[1]), axis=0)


def params(mib):
    return pltpu.CompilerParams(vmem_limit_bytes=mib * MIB)


def vmem():
    return pl.BlockSpec(memory_space=pltpu.VMEM)


def smem():
    return pl.BlockSpec(memory_space=pltpu.SMEM)


def rows_of(near_ref, far_ref, block):
    return jnp.concatenate([near_ref[block], far_ref[block]], axis=1)


def sweep_kernel(copies, tile, has_parts, has_extra, *refs):
    refs = list(refs)
    parts_ref = refs.pop(0) if has_parts else None
    extra_ref = refs.pop(0) if has_extra else None
    protos_ref, near_ref, far_ref, col_ref, out_ref, scale, kern, acc = refs
    blocks, rows, _ = near_ref.shape
    per = rows // LANES
    groups = blocks * per
    if has_parts:
        scale[...] = 1.0 / jnp.sum(parts_ref[...], axis=0)
    else:
        scale[...] = jnp.ones_like(scale)
    acc[...] = jnp.zeros_like(acc)

    def one_tile(step, carry):
        here = pl.ds(pl.multiple_of(step * tile, tile), tile)
        protos = protos_ref[here, :]
        col_acc = jnp.zeros((tile, LANES), F32)
        for block in range(blocks):
            logits = dot_nt(protos, rows_of(near_ref, far_ref, block))
            for part in range(per):
                value = jnp.exp2(logits[:, part * LANES : (part + 1) * LANES] * TSCALE)
                at = block * per + part
                kern[:, at * LANES : (at + 1) * LANES] = value
                col_acc = col_acc + value * scale[at : at + 1, :]
        col = 1.0 / jnp.sum(col_acc, axis=1, keepdims=True)
        wide_col = jnp.broadcast_to(col, (tile, LANES))
        col_ref[here, :] = wide_col
        for at in range(groups):
            lanes = slice(at * LANES, (at + 1) * LANES)
            acc[:, lanes] += fold_rows(kern[:, lanes] * wide_col)
        return carry

    lax.fori_loop(0, protos_ref.shape[0] // tile, one_tile, 0)
    for at in range(groups):
        total = jnp.sum(acc[:, at * LANES : (at + 1) * LANES], axis=0, keepdims=True)
        for copy in range(copies):
            out_ref[copy, at : at + 1, :] = total
    if has_extra:
        extra = extra_ref[...]
        for copy in range(copies):
            out_ref[copy, groups:, :] = extra


def sweep(parts, extra, protos, near, far, copies, tile=256):
    count = protos.shape[0]
    blocks, rows, _ = near.shape
    groups = blocks * rows // LANES
    sent = groups if extra is None else groups + extra.shape[0]
    args = [a for a in (parts, extra) if a is not None] + [protos, near, far]
    return pl.pallas_call(
        functools.partial(sweep_kernel, copies, tile, parts is not None, extra is not None),
        in_specs=[vmem()] * len(args),
        out_specs=[vmem()] * 2,
        out_shape=[
            jax.ShapeDtypeStruct((count, LANES), F32),
            jax.ShapeDtypeStruct((copies, sent, LANES), F32),
        ],
        scratch_shapes=[
            pltpu.VMEM((groups, LANES), F32),
            pltpu.VMEM((tile, blocks * rows), F32),
            pltpu.VMEM((8, blocks * rows), F32),
        ],
        compiler_params=params(24),
        name="sweep",
    )(*args)


def totals_kernel(tile, protos_ref, stud_ref, out_ref, acc):
    acc[...] = jnp.zeros_like(acc)
    blocks, rows, _ = stud_ref.shape

    def one_tile(step, carry):
        protos = protos_ref[pl.ds(pl.multiple_of(step * tile, tile), tile), :]
        for block in range(blocks):
            logits = dot_nt(protos, stud_ref[block])
            acc[:, block * rows : (block + 1) * rows] += fold_rows(jnp.exp2(logits * SSCALE))
        return carry

    lax.fori_loop(0, protos_ref.shape[0] // tile, one_tile, 0)
    for at in range(blocks * rows // LANES):
        out_ref[at : at + 1, :] = jnp.sum(
            acc[:, at * LANES : (at + 1) * LANES], axis=0, keepdims=True
        )


def totals(protos, stud, tile=512):
    count, depth = protos.shape
    blocks, rows, _ = stud.shape
    groups = blocks * rows // LANES
    return pl.pallas_call(
        functools.partial(totals_kernel, tile),
        in_specs=[vmem()] * 2,
        out_specs=vmem(),
        out_shape=jax.ShapeDtypeStruct((groups, LANES), F32),
        scratch_shapes=[pltpu.VMEM((8, blocks * rows), F32)],
        compiler_params=params(24),
        cost_estimate=pl.CostEstimate(
            flops=2 * count * depth * blocks * rows,
            bytes_accessed=4 * MIB,
            transcendentals=count * blocks * rows,
        ),
        name="totals",
    )(protos, stud)


def hop_kernel(copies, in_ref, out_ref):
    total = jnp.sum(in_ref[...], axis=0)
    for copy in range(copies):
        out_ref[copy] = total


def hop(parts, copies):
    return pl.pallas_call(
        functools.partial(hop_kernel, copies),
        in_specs=[vmem()],
        out_specs=vmem(),
        out_shape=jax.ShapeDtypeStruct((copies,) + parts.shape[1:], F32),
        compiler_params=params(4),
        name="hop",
    )(parts)


def exchange(parts, axes):
    return lax.all_to_all(parts, axes, 0, 0, tiled=True)


def spread(parts, pillar):
    return exchange(hop(exchange(parts, PLANE), pillar), PILLAR)


def diff_kernel(
    tile, core_ref, parts_ref, col_ref, protos_ref, near_protos_ref, cols_ref, near_ref, far_ref, stud_ref,
    out_ref, mine_ref, other_ref, scale, norm, diff, sems,
):
    blocks, rows, _ = near_ref.shape
    per = rows // LANES
    groups = blocks * per
    core = core_ref[0]
    sums = LOG_INV - jnp.log2(jnp.sum(parts_ref[...], axis=0))
    scale[...] = sums[:groups]
    norm[...] = sums[groups:]
    tiles = protos_ref.shape[0] // tile

    def span(step):
        return pl.ds(pl.multiple_of(step * tile, tile), tile)

    def store(step):
        return pltpu.make_async_copy(diff.at[span(step), :], out_ref.at[span(step), :], sems.at[step])

    def one_tile(step, carry):
        here = span(step)
        log_col = jnp.log2(col_ref[here, :])
        for block in range(blocks):
            teach_logits = dot_nt(near_protos_ref[here, :], rows_of(near_ref, far_ref, block))
            stud_logits = dot_nt(protos_ref[here, :], stud_ref[block])
            for part in range(per):
                at = block * per + part
                lanes = slice(part * LANES, (part + 1) * LANES)
                target = jnp.exp2(teach_logits[:, lanes] * TSCALE + (scale[at : at + 1, :] + log_col))
                prob = jnp.exp2(stud_logits[:, lanes] * SSCALE + norm[at : at + 1, :])
                diff[here, at * LANES : (at + 1) * LANES] = (prob - target).astype(BF16)
        store(step).start()
        return carry

    lax.fori_loop(0, tiles, one_tile, 0)

    def one_pair(pair, carry):
        for first, ref in ((core, mine_ref), (1 - core, other_ref)):
            start = pl.multiple_of((2 * pair + first) * rows, rows)
            ref[pair] = dot(cols_ref[...], diff[:, pl.ds(start, rows)])
        return carry

    lax.fori_loop(0, blocks // 2, one_pair, 0)

    def finish(step, carry):
        store(step).wait()
        return carry

    lax.fori_loop(0, tiles, finish, 0)


def differences(core, parts, col, protos, near_protos, cols, near, far, stud, tile=512):
    count, depth = protos.shape
    blocks, rows, _ = near.shape
    groups = blocks * rows // LANES
    return pl.pallas_call(
        functools.partial(diff_kernel, tile),
        in_specs=[smem()] + [vmem()] * 8,
        out_specs=[pl.BlockSpec(memory_space=pl.ANY)] + [vmem()] * 2,
        out_shape=[
            jax.ShapeDtypeStruct((count, blocks * rows), BF16),
            jax.ShapeDtypeStruct((blocks // 2, depth, rows), F32),
            jax.ShapeDtypeStruct((blocks // 2, depth, rows), F32),
        ],
        scratch_shapes=[
            pltpu.VMEM((groups, LANES), F32),
            pltpu.VMEM((groups, LANES), F32),
            pltpu.VMEM((count, blocks * rows), BF16),
            pltpu.SemaphoreType.DMA((count // tile,)),
        ],
        compiler_params=params(40),
        name="differences",
    )(core, parts, col, protos, near_protos, cols, near, far, stud)


SPAN = 250.0
FLOOR = 125.0


def power_of(top):
    return jnp.minimum(jnp.ceil(jnp.log2(jnp.maximum(top, 2.0**-120))), 126.0)


def encode(values, power):
    size = jnp.exp2(jnp.minimum(jnp.abs(values) * jnp.exp2(-power), 1.0) * SPAN - FLOOR)
    return jnp.where(values < 0, -size, size).astype(BF16)


def decode(code, power):
    wide = code.astype(F32)
    size = (jnp.log2(jnp.abs(wide)) + FLOOR) * (1.0 / SPAN) * jnp.exp2(power)
    return jnp.where(wide < 0, -size, size)


def decode_kernel(code_ref, out_ref):
    sources, share, width = code_ref.shape
    count = out_ref.shape[1] // sources

    def one_source(source, carry):
        powers = code_ref[source, :, count:].astype(F32)
        for part in range(count // LANES):
            code = code_ref[source, :, part * LANES : (part + 1) * LANES]
            start = pl.multiple_of(source * count + part * LANES, LANES)
            out_ref[:, pl.ds(start, LANES)] = decode(code, powers[part : part + 1, :])
        return carry

    lax.fori_loop(0, sources, one_source, 0)


def decoded(codes):
    sources, share, width = codes.shape
    return pl.pallas_call(
        decode_kernel,
        in_specs=[vmem()],
        out_specs=vmem(),
        out_shape=jax.ShapeDtypeStruct((share, sources * (width - LANES)), F32),
        compiler_params=params(16),
        cost_estimate=pl.CostEstimate(flops=16 * sources * share * width, bytes_accessed=4 * MIB, transcendentals=0),
        name="decoded",
    )(codes)


def pgrad_kernel(tile, diff_ref, stud_ref, out_ref, diff, powers, sems):
    tiles = diff.shape[0] // tile
    blocks, rows, depth = stud_ref.shape

    def span(step):
        return pl.ds(pl.multiple_of(step * tile, tile), tile)

    def load(step):
        return pltpu.make_async_copy(diff_ref.at[span(step), :], diff.at[span(step), :], sems.at[step])

    def begin(step, carry):
        load(step).start()
        return carry

    def one_tile(step, carry):
        load(step).wait()
        stud = stud_ref[...].reshape(blocks * rows, depth)
        share = out_ref.shape[1]
        grads = (4096.0 * dot(diff[span(step), :], stud)).T
        for dest in range(depth // share):
            values = grads[dest * share : (dest + 1) * share, :]
            power = power_of(jnp.max(jnp.abs(values), axis=0, keepdims=True))
            out_ref[dest, :, span(step)] = encode(values, power)
            for part in range(tile // LANES):
                row = step * (tile // LANES) + part
                powers[dest, pl.ds(row, 1), :] = power[:, part * LANES : (part + 1) * LANES]
        return carry

    lax.fori_loop(0, tiles, begin, 0)
    lax.fori_loop(0, tiles, one_tile, 0)
    out_ref[:, :, diff.shape[0] :] = powers[...].astype(BF16)


def proto_part(diff, stud, dests, tile=512):
    count, total = diff.shape
    depth = stud.shape[2]
    return pl.pallas_call(
        functools.partial(pgrad_kernel, tile),
        in_specs=[pl.BlockSpec(memory_space=pl.ANY), vmem()],
        out_specs=vmem(),
        out_shape=jax.ShapeDtypeStruct((dests, depth // dests, count + LANES), BF16),
        scratch_shapes=[
            pltpu.VMEM((count, total), BF16),
            pltpu.VMEM((dests, count // LANES, LANES), F32),
            pltpu.SemaphoreType.DMA((count // tile,)),
        ],
        compiler_params=params(56),
        cost_estimate=pl.CostEstimate(
            flops=2 * count * total * depth, bytes_accessed=20 * MIB, transcendentals=0
        ),
        name="proto_part",
    )(diff, stud)


GROUP = 16


def cut_kernel(level_ref, mine_ref, given_ref, own_ref, *code_refs):
    quarter = own_ref.shape[1]
    for by in range(len(code_refs) + 1):
        start = pl.multiple_of(lax.rem(level_ref[0] + by, len(code_refs) + 1) * quarter, quarter)
        for pair in range(own_ref.shape[0]):
            values = mine_ref[pair, pl.ds(start, quarter), :] + given_ref[pair, pl.ds(start, quarter), :]
            if by == 0:
                own_ref[pair] = values
                continue
            parts = [values[at : at + GROUP] for at in range(0, quarter, GROUP)]
            power = power_of(functools.reduce(jnp.maximum, [jnp.abs(part) for part in parts]))
            for at, part in enumerate(parts):
                code_refs[by - 1][pair, at * GROUP : (at + 1) * GROUP, :] = encode(part, power)
            code_refs[by - 1][pair, quarter:, :] = power.astype(BF16)


def cuts(level, mine, given, levels):
    pairs, depth, rows = mine.shape
    quarter = depth // levels
    return pl.pallas_call(
        cut_kernel,
        in_specs=[smem(), vmem(), vmem()],
        out_specs=[vmem()] * levels,
        out_shape=[jax.ShapeDtypeStruct((pairs, quarter, rows), F32)]
        + [jax.ShapeDtypeStruct((pairs, quarter + GROUP, rows), BF16)] * (levels - 1),
        compiler_params=params(16),
        name="cuts",
    )(level, mine, given)


def join_kernel(own_ref, *refs):
    out_ref = refs[-1]
    quarter = own_ref.shape[1]
    for pair in range(own_ref.shape[0]):
        powers = [ref[pair, quarter:, :].astype(F32) for ref in refs[:-1]]
        for at in range(0, quarter, GROUP):
            total = own_ref[pair, at : at + GROUP, :]
            for ref, power in zip(refs[:-1], powers):
                total = total + decode(ref[pair, at : at + GROUP, :], power)
            out_ref[pair, at : at + GROUP, :] = total


def joined(own, codes):
    return pl.pallas_call(
        join_kernel,
        in_specs=[vmem()] * (1 + len(codes)),
        out_specs=vmem(),
        out_shape=jax.ShapeDtypeStruct(own.shape, F32),
        compiler_params=params(8),
        name="joined",
    )(own, *codes)


def protos_kernel(place_ref, weight_ref, cols_ref, protos_ref, near_ref, held, sem):
    depth, count = cols_ref.shape
    start = pl.multiple_of(place_ref[0] * count, count)
    copy = pltpu.make_async_copy(weight_ref.at[:, pl.ds(start, count)], held, sem)
    copy.start()
    copy.wait()
    tile = 512
    half = depth // 2
    first = place_ref[1] == 0
    for at in range(0, count, tile):
        wide = held[:, at : at + tile].astype(F32)
        squares = jnp.sum(wide * wide, axis=0, keepdims=True)
        unit = wide * lax.rsqrt(squares + EPS)
        cols_ref[:, at : at + tile] = unit.astype(BF16)
        turned = unit.T
        low = turned[:, :half]
        high = turned[:, half:]
        protos_ref[at : at + tile, :] = turned.astype(BF16)
        near_ref[at : at + tile, :half] = jnp.where(first, low, high).astype(BF16)
        near_ref[at : at + tile, half:] = jnp.where(first, high, low).astype(BF16)


def unit_protos(place, weight, count):
    depth = weight.shape[0]
    return pl.pallas_call(
        protos_kernel,
        in_specs=[smem(), pl.BlockSpec(memory_space=pl.ANY)],
        out_specs=[vmem()] * 3,
        out_shape=[
            jax.ShapeDtypeStruct((depth, count), BF16),
            jax.ShapeDtypeStruct((count, depth), BF16),
            jax.ShapeDtypeStruct((count, depth), BF16),
        ],
        scratch_shapes=[pltpu.VMEM((depth, count), BF16), pltpu.SemaphoreType.DMA(())],
        compiler_params=params(56),
        cost_estimate=pl.CostEstimate(
            flops=8 * count * depth, bytes_accessed=20 * MIB, transcendentals=count
        ),
        name="unit_protos",
    )(place, weight)


def swap(value):
    return lax.ppermute(value, "c", [(0, 1), (1, 0)])


def turn(value, by, size):
    return lax.ppermute(value, "z", [(i, (i + by) % size) for i in range(size)])


def copied(value, count):
    return jnp.broadcast_to(value[None], (count,) + value.shape)


def on_device(size, teacher_feats, student_feats, proto_weight):
    depth, held = proto_weight.shape
    devices = size["yl"] * size["x"] * size["c"]
    chips = size["yl"] * size["x"]
    plane = chips * size["yh"]
    pillar = size["z"] * size["c"]
    count = held // devices
    half = depth // 2
    rows = teacher_feats.shape[0]
    core = lax.axis_index("c")
    level = lax.axis_index("z")

    unit = unit_rows(teacher_feats)
    own = lax.dynamic_slice(unit, (0, core * half), (rows, half))
    given = swap(lax.dynamic_slice(unit, (0, (1 - core) * half), (rows, half)))
    both = jnp.where(core == 0, jnp.stack([own, given]), jnp.stack([given, own]))
    near = exchange(copied(both, chips), CHIPS).reshape(devices, rows, half)
    far = swap(near)

    mine = lax.axis_index(DP)
    cols, protos, near_protos = unit_protos(jnp.stack([mine, core]), proto_weight, count)

    stud_unit, near = lax.optimization_barrier((unit_rows(student_feats), near))
    stud = lax.all_gather(stud_unit, DP)

    parts = None
    extra = None
    for step in range(ITERS):
        if step == ITERS - 1:
            extra = totals(protos, stud)
        col, copies = sweep(parts, extra, near_protos, near, far, plane)
        parts = spread(copies, pillar)

    diff, mine_feat, other_feat = differences(
        core.reshape(1), parts, col, protos, near_protos, cols, near, far, stud
    )
    given_feat = swap(other_feat)
    own, *others = cuts(level.reshape(1), mine_feat, given_feat, size["z"])
    turned = [turn(part, by + 1, size["z"]) for by, part in enumerate(others)]
    codes = exchange(proto_part(diff, stud, devices), DP)
    *turned, codes = lax.optimization_barrier((*turned, codes))
    proto_grad = decoded(codes)
    feat = joined(own, turned).reshape(plane, -1, rows)
    feat = jnp.sum(exchange(feat, PLANE), axis=0)
    feat = exchange(copied(feat, size["z"] * size["yh"]), PROTO)
    feature_grad = 512.0 * feat.reshape(depth, rows).T
    return feature_grad, proto_grad


def solution(mesh):
    split = jax.sharding.Mesh(mesh.devices.reshape(2, 4, 2, 4, 2), AXES)
    return jax.shard_map(
        functools.partial(on_device, dict(split.shape)),
        mesh=split,
        in_specs=(P(DP, None), P(DP, None), P(None, PROTO)),
        out_specs=(P(DP, None), P(DP, PROTO)),
        check_vma=False,
    )
```

```python
import functools
import math

import jax
import jax.numpy as jnp
import numpy as np
from jax import lax
from jax.experimental import pallas as pl
from jax.experimental.pallas import tpu as pltpu
from jax.sharding import PartitionSpec as P

ITERS = 3
EPS = 1e-06
TEACH = float(np.float32(0.07))
STUD = float(np.float32(0.1))
LOG2E = math.log2(math.e)
TSCALE = LOG2E / TEACH
SSCALE = LOG2E / STUD
LOG_INV = -math.log2(STUD)
F32 = jnp.float32
BF16 = jnp.bfloat16
LANES = 128
MIB = 1024 * 1024
AXES = ("yl", "x", "c", "z", "yh")
DP = ("yl", "x", "c")
PROTO = ("z", "yh")
CHIPS = ("yl", "x")
PLANE = ("yl", "x", "yh")
PILLAR = ("z", "c")


def unit_rows(feats):
    wide = feats.astype(F32)
    squares = jnp.sum(wide * wide, axis=1, keepdims=True)
    return (wide * lax.rsqrt(squares + EPS)).astype(BF16)


def dot(a, b):
    return jnp.dot(a, b, preferred_element_type=F32)


def dot_nt(a, b):
    return lax.dot_general(a, b, (((1,), (1,)), ((), ())), preferred_element_type=F32)


def fold_rows(value):
    return jnp.sum(value.reshape(value.shape[0] // 8, 8, value.shape[1]), axis=0)


def params(mib):
    return pltpu.CompilerParams(vmem_limit_bytes=mib * MIB)


def vmem():
    return pl.BlockSpec(memory_space=pltpu.VMEM)


def smem():
    return pl.BlockSpec(memory_space=pltpu.SMEM)


def rows_of(near_ref, far_ref, block):
    return jnp.concatenate([near_ref[block], far_ref[block]], axis=1)


def sweep_kernel(copies, tile, has_parts, has_extra, *refs):
    refs = list(refs)
    parts_ref = refs.pop(0) if has_parts else None
    extra_ref = refs.pop(0) if has_extra else None
    protos_ref, near_ref, far_ref, col_ref, out_ref, scale, kern, acc = refs
    blocks, rows, _ = near_ref.shape
    per = rows // LANES
    groups = blocks * per
    if has_parts:
        scale[...] = 1.0 / jnp.sum(parts_ref[...], axis=0)
    acc[...] = jnp.zeros_like(acc)

    def one_tile(step, carry):
        here = pl.ds(pl.multiple_of(step * tile, tile), tile)
        protos = protos_ref[here, :]
        col_acc = jnp.zeros((tile, LANES), F32)
        for block in range(blocks):
            logits = dot_nt(protos, rows_of(near_ref, far_ref, block))
            for part in range(per):
                value = jnp.exp2(logits[:, part * LANES : (part + 1) * LANES] * TSCALE)
                at = block * per + part
                kern[:, at * LANES : (at + 1) * LANES] = value
                col_acc = col_acc + (value * scale[at : at + 1, :] if has_parts else value)
        col = 1.0 / jnp.sum(col_acc, axis=1, keepdims=True)
        wide_col = jnp.broadcast_to(col, (tile, LANES))
        col_ref[here, :] = wide_col
        for at in range(groups):
            lanes = slice(at * LANES, (at + 1) * LANES)
            acc[:, lanes] += fold_rows(kern[:, lanes] * wide_col)
        return carry

    lax.fori_loop(0, protos_ref.shape[0] // tile, one_tile, 0)
    for at in range(groups):
        total = jnp.sum(acc[:, at * LANES : (at + 1) * LANES], axis=0, keepdims=True)
        for copy in range(copies):
            out_ref[copy, at : at + 1, :] = total
    if has_extra:
        extra = extra_ref[...]
        for copy in range(copies):
            out_ref[copy, groups:, :] = extra


def sweep(parts, extra, protos, near, far, copies, tile=256):
    count = protos.shape[0]
    blocks, rows, _ = near.shape
    groups = blocks * rows // LANES
    sent = groups if extra is None else groups + extra.shape[0]
    args = [a for a in (parts, extra) if a is not None] + [protos, near, far]
    return pl.pallas_call(
        functools.partial(sweep_kernel, copies, tile, parts is not None, extra is not None),
        in_specs=[vmem()] * len(args),
        out_specs=[vmem()] * 2,
        out_shape=[
            jax.ShapeDtypeStruct((count, LANES), F32),
            jax.ShapeDtypeStruct((copies, sent, LANES), F32),
        ],
        scratch_shapes=[
            pltpu.VMEM((groups, LANES), F32),
            pltpu.VMEM((tile, blocks * rows), F32),
            pltpu.VMEM((8, blocks * rows), F32),
        ],
        compiler_params=params(24),
        name="sweep",
    )(*args)


def totals_kernel(tile, protos_ref, near_ref, far_ref, out_ref, acc):
    acc[...] = jnp.zeros_like(acc)
    blocks, rows, _ = near_ref.shape

    def one_tile(step, carry):
        protos = protos_ref[pl.ds(pl.multiple_of(step * tile, tile), tile), :]
        for block in range(blocks):
            logits = dot_nt(protos, rows_of(near_ref, far_ref, block))
            acc[:, block * rows : (block + 1) * rows] += fold_rows(jnp.exp2(logits * SSCALE))
        return carry

    lax.fori_loop(0, protos_ref.shape[0] // tile, one_tile, 0)
    for at in range(blocks * rows // LANES):
        out_ref[at : at + 1, :] = jnp.sum(
            acc[:, at * LANES : (at + 1) * LANES], axis=0, keepdims=True
        )


def totals(protos, near, far, tile=512):
    count, depth = protos.shape
    blocks, rows, _ = near.shape
    groups = blocks * rows // LANES
    return pl.pallas_call(
        functools.partial(totals_kernel, tile),
        in_specs=[vmem()] * 3,
        out_specs=vmem(),
        out_shape=jax.ShapeDtypeStruct((groups, LANES), F32),
        scratch_shapes=[pltpu.VMEM((8, blocks * rows), F32)],
        compiler_params=params(24),
        cost_estimate=pl.CostEstimate(
            flops=2 * count * depth * blocks * rows,
            bytes_accessed=4 * MIB,
            transcendentals=count * blocks * rows,
        ),
        name="totals",
    )(protos, near, far)


def hop_kernel(copies, in_ref, out_ref):
    total = jnp.sum(in_ref[...], axis=0)
    for copy in range(copies):
        out_ref[copy] = total


def hop(parts, copies):
    return pl.pallas_call(
        functools.partial(hop_kernel, copies),
        in_specs=[vmem()],
        out_specs=vmem(),
        out_shape=jax.ShapeDtypeStruct((copies,) + parts.shape[1:], F32),
        compiler_params=params(4),
        name="hop",
    )(parts)


def exchange(parts, axes):
    return lax.all_to_all(parts, axes, 0, 0, tiled=True)


def spread(parts, pillar):
    return exchange(hop(exchange(parts, PLANE), pillar), PILLAR)


def diff_kernel(
    tile, core_ref, parts_ref, col_ref, protos_ref, cols_ref, near_ref, far_ref, stud_near_ref, stud_far_ref,
    out_ref, mine_ref, other_ref, scale, norm, diff, sems,
):
    blocks, rows, _ = near_ref.shape
    per = rows // LANES
    groups = blocks * per
    core = core_ref[0]
    sums = LOG_INV - jnp.log2(jnp.sum(parts_ref[...], axis=0))
    scale[...] = sums[:groups]
    norm[...] = sums[groups:]
    tiles = protos_ref.shape[0] // tile

    def span(step):
        return pl.ds(pl.multiple_of(step * tile, tile), tile)

    def store(step):
        return pltpu.make_async_copy(diff.at[span(step), :], out_ref.at[span(step), :], sems.at[step])

    def one_tile(step, carry):
        here = span(step)
        log_col = jnp.log2(col_ref[here, :])
        for block in range(blocks):
            teach_logits = dot_nt(protos_ref[here, :], rows_of(near_ref, far_ref, block))
            stud_logits = dot_nt(protos_ref[here, :], rows_of(stud_near_ref, stud_far_ref, block))
            for part in range(per):
                at = block * per + part
                lanes = slice(part * LANES, (part + 1) * LANES)
                target = jnp.exp2(teach_logits[:, lanes] * TSCALE + (scale[at : at + 1, :] + log_col))
                prob = jnp.exp2(stud_logits[:, lanes] * SSCALE + norm[at : at + 1, :])
                diff[here, at * LANES : (at + 1) * LANES] = (prob - target).astype(BF16)
        store(step).start()
        return carry

    lax.fori_loop(0, tiles, one_tile, 0)

    def one_pair(pair, carry):
        for first, ref in ((core, mine_ref), (1 - core, other_ref)):
            start = pl.multiple_of((2 * pair + first) * rows, rows)
            ref[pair] = dot(cols_ref[...], diff[:, pl.ds(start, rows)])
        return carry

    lax.fori_loop(0, blocks // 2, one_pair, 0)

    def finish(step, carry):
        store(step).wait()
        return carry

    lax.fori_loop(0, tiles, finish, 0)


def differences(core, parts, col, protos, cols, near, far, stud_near, stud_far, tile=512):
    count, depth = protos.shape
    blocks, rows, _ = near.shape
    groups = blocks * rows // LANES
    return pl.pallas_call(
        functools.partial(diff_kernel, tile),
        in_specs=[smem()] + [vmem()] * 8,
        out_specs=[pl.BlockSpec(memory_space=pl.ANY)] + [vmem()] * 2,
        out_shape=[
            jax.ShapeDtypeStruct((count, blocks * rows), BF16),
            jax.ShapeDtypeStruct((blocks // 2, depth, rows), F32),
            jax.ShapeDtypeStruct((blocks // 2, depth, rows), F32),
        ],
        scratch_shapes=[
            pltpu.VMEM((groups, LANES), F32),
            pltpu.VMEM((groups, LANES), F32),
            pltpu.VMEM((count, blocks * rows), BF16),
            pltpu.SemaphoreType.DMA((count // tile,)),
        ],
        compiler_params=params(40),
        name="differences",
    )(core, parts, col, protos, cols, near, far, stud_near, stud_far)


SPAN = 250.0
FLOOR = 125.0


def power_of(top):
    return jnp.minimum(jnp.ceil(jnp.log2(jnp.maximum(top, 2.0**-120))), 126.0)


def encode(values, power):
    size = jnp.exp2(jnp.minimum(jnp.abs(values) * jnp.exp2(-power), 1.0) * SPAN - FLOOR)
    return jnp.where(values < 0, -size, size).astype(BF16)


def decode(code, power):
    wide = code.astype(F32)
    size = (jnp.log2(jnp.abs(wide)) + FLOOR) * (1.0 / SPAN) * jnp.exp2(power)
    return jnp.where(wide < 0, -size, size)


def decode_kernel(code_ref, out_ref):
    sources, share, width = code_ref.shape
    count = out_ref.shape[1] // sources

    def one_source(source, carry):
        powers = code_ref[source, :, count:].astype(F32)
        for part in range(count // LANES):
            code = code_ref[source, :, part * LANES : (part + 1) * LANES]
            start = pl.multiple_of(source * count + part * LANES, LANES)
            out_ref[:, pl.ds(start, LANES)] = decode(code, powers[part : part + 1, :])
        return carry

    lax.fori_loop(0, sources, one_source, 0)


def decoded(codes):
    sources, share, width = codes.shape
    return pl.pallas_call(
        decode_kernel,
        in_specs=[vmem()],
        out_specs=vmem(),
        out_shape=jax.ShapeDtypeStruct((share, sources * (width - LANES)), F32),
        compiler_params=params(16),
        cost_estimate=pl.CostEstimate(flops=16 * sources * share * width, bytes_accessed=4 * MIB, transcendentals=0),
        name="decoded",
    )(codes)


def pgrad_kernel(tile, core_ref, diff_ref, near_ref, far_ref, out_ref, diff, powers, sems):
    tiles = diff.shape[0] // tile
    blocks, rows, half = near_ref.shape
    dests, share, _ = out_ref.shape

    def span(step):
        return pl.ds(pl.multiple_of(step * tile, tile), tile)

    def load(step):
        return pltpu.make_async_copy(diff_ref.at[span(step), :], diff.at[span(step), :], sems.at[step])

    def begin(step, carry):
        load(step).start()
        return carry

    def one_tile(step, carry):
        load(step).wait()
        halves = [ref[...].reshape(blocks * rows, half) for ref in (near_ref, far_ref)]
        stud = jnp.concatenate(halves, axis=1)
        grads = (4096.0 * dot(diff[span(step), :], stud)).T
        for at in range(dests):
            values = grads[at * share : (at + 1) * share, :]
            dest = lax.rem(at + core_ref[0] * (dests // 2), dests)
            power = power_of(jnp.max(jnp.abs(values), axis=0, keepdims=True))
            out_ref[dest, :, span(step)] = encode(values, power)
            for part in range(tile // LANES):
                row = step * (tile // LANES) + part
                powers[dest, pl.ds(row, 1), :] = power[:, part * LANES : (part + 1) * LANES]
        return carry

    lax.fori_loop(0, tiles, begin, 0)
    lax.fori_loop(0, tiles, one_tile, 0)
    out_ref[:, :, diff.shape[0] :] = powers[...].astype(BF16)


def proto_part(core, diff, near, far, dests, tile=512):
    count, total = diff.shape
    depth = 2 * near.shape[2]
    return pl.pallas_call(
        functools.partial(pgrad_kernel, tile),
        in_specs=[smem(), pl.BlockSpec(memory_space=pl.ANY), vmem(), vmem()],
        out_specs=vmem(),
        out_shape=jax.ShapeDtypeStruct((dests, depth // dests, count + LANES), BF16),
        scratch_shapes=[
            pltpu.VMEM((count, total), BF16),
            pltpu.VMEM((dests, count // LANES, LANES), F32),
            pltpu.SemaphoreType.DMA((count // tile,)),
        ],
        compiler_params=params(56),
        cost_estimate=pl.CostEstimate(
            flops=2 * count * total * depth, bytes_accessed=20 * MIB, transcendentals=0
        ),
        name="proto_part",
    )(core, diff, near, far)


GROUP = 16


def cut_kernel(level_ref, mine_ref, given_ref, own_ref, *code_refs):
    quarter = own_ref.shape[1]
    for by in range(len(code_refs) + 1):
        start = pl.multiple_of(lax.rem(level_ref[0] + by, len(code_refs) + 1) * quarter, quarter)
        for pair in range(own_ref.shape[0]):
            values = mine_ref[pair, pl.ds(start, quarter), :] + given_ref[pair, pl.ds(start, quarter), :]
            if by == 0:
                own_ref[pair] = values
                continue
            parts = [values[at : at + GROUP] for at in range(0, quarter, GROUP)]
            power = power_of(functools.reduce(jnp.maximum, [jnp.abs(part) for part in parts]))
            for at, part in enumerate(parts):
                code_refs[by - 1][pair, at * GROUP : (at + 1) * GROUP, :] = encode(part, power)
            code_refs[by - 1][pair, quarter:, :] = power.astype(BF16)


def cuts(level, mine, given, levels):
    pairs, depth, rows = mine.shape
    quarter = depth // levels
    return pl.pallas_call(
        cut_kernel,
        in_specs=[smem(), vmem(), vmem()],
        out_specs=[vmem()] * levels,
        out_shape=[jax.ShapeDtypeStruct((pairs, quarter, rows), F32)]
        + [jax.ShapeDtypeStruct((pairs, quarter + GROUP, rows), BF16)] * (levels - 1),
        compiler_params=params(16),
        name="cuts",
    )(level, mine, given)


def join_kernel(own_ref, *refs):
    out_ref = refs[-1]
    quarter = own_ref.shape[1]
    for pair in range(own_ref.shape[0]):
        powers = [ref[pair, quarter:, :].astype(F32) for ref in refs[:-1]]
        for at in range(0, quarter, GROUP):
            total = own_ref[pair, at : at + GROUP, :]
            for ref, power in zip(refs[:-1], powers):
                total = total + decode(ref[pair, at : at + GROUP, :], power)
            out_ref[pair, at : at + GROUP, :] = total


def joined(own, codes):
    return pl.pallas_call(
        join_kernel,
        in_specs=[vmem()] * (1 + len(codes)),
        out_specs=vmem(),
        out_shape=jax.ShapeDtypeStruct(own.shape, F32),
        compiler_params=params(8),
        name="joined",
    )(own, *codes)


def protos_kernel(place_ref, weight_ref, cols_ref, protos_ref, held, sem):
    depth, count = cols_ref.shape
    start = pl.multiple_of(place_ref[0] * count, count)
    copy = pltpu.make_async_copy(weight_ref.at[:, pl.ds(start, count)], held, sem)
    copy.start()
    copy.wait()
    tile = 512
    half = depth // 2
    first = place_ref[1] == 0
    for at in range(0, count, tile):
        wide = held[:, at : at + tile].astype(F32)
        squares = jnp.sum(wide * wide, axis=0, keepdims=True)
        unit = wide * lax.rsqrt(squares + EPS)
        cols_ref[:, at : at + tile] = unit.astype(BF16)
        turned = unit.T
        low = turned[:, :half]
        high = turned[:, half:]
        protos_ref[at : at + tile, :half] = jnp.where(first, low, high).astype(BF16)
        protos_ref[at : at + tile, half:] = jnp.where(first, high, low).astype(BF16)


def unit_protos(place, weight, count):
    depth = weight.shape[0]
    return pl.pallas_call(
        protos_kernel,
        in_specs=[smem(), pl.BlockSpec(memory_space=pl.ANY)],
        out_specs=[vmem()] * 2,
        out_shape=[
            jax.ShapeDtypeStruct((depth, count), BF16),
            jax.ShapeDtypeStruct((count, depth), BF16),
        ],
        scratch_shapes=[pltpu.VMEM((depth, count), BF16), pltpu.SemaphoreType.DMA(())],
        compiler_params=params(56),
        cost_estimate=pl.CostEstimate(
            flops=8 * count * depth, bytes_accessed=20 * MIB, transcendentals=count
        ),
        name="unit_protos",
    )(place, weight)


def swap(value):
    return lax.ppermute(value, "c", [(0, 1), (1, 0)])


def turn(value, by, size):
    return lax.ppermute(value, "z", [(i, (i + by) % size) for i in range(size)])


def copied(value, count):
    return jnp.broadcast_to(value[None], (count,) + value.shape)


def on_device(size, teacher_feats, student_feats, proto_weight):
    depth, held = proto_weight.shape
    devices = size["yl"] * size["x"] * size["c"]
    chips = size["yl"] * size["x"]
    plane = chips * size["yh"]
    pillar = size["z"] * size["c"]
    count = held // devices
    half = depth // 2
    rows = teacher_feats.shape[0]
    core = lax.axis_index("c")
    level = lax.axis_index("z")

    def halves(feats):
        unit = unit_rows(feats)
        own = lax.dynamic_slice(unit, (0, core * half), (rows, half))
        given = swap(lax.dynamic_slice(unit, (0, (1 - core) * half), (rows, half)))
        return jnp.where(core == 0, jnp.stack([own, given]), jnp.stack([given, own]))

    near = exchange(copied(halves(teacher_feats), chips), CHIPS).reshape(devices, rows, half)
    cols, protos = unit_protos(jnp.stack([lax.axis_index(DP), core]), proto_weight, count)
    stud_own = halves(student_feats)
    near, protos, cols = lax.optimization_barrier((near, protos, cols))
    far = swap(near)
    stud_own, near = lax.optimization_barrier((stud_own, near))
    stud_near = lax.all_gather(stud_own, CHIPS).reshape(devices, rows, half)
    parts = None
    extra = None
    for step in range(ITERS):
        if step == ITERS - 1:
            extra = totals(protos, stud_near, stud_far)
        col, copies = sweep(parts, extra, protos, near, far, plane)
        parts = spread(copies, pillar)
        if step == 0:
            stud_near, parts = lax.optimization_barrier((stud_near, parts))
            stud_far = swap(stud_near)

    diff, mine_feat, other_feat = differences(
        core.reshape(1), parts, col, protos, cols, near, far, stud_near, stud_far
    )
    given_feat = swap(other_feat)
    own, *others = cuts(level.reshape(1), mine_feat, given_feat, size["z"])
    turned = [turn(part, by + 1, size["z"]) for by, part in enumerate(others)]
    codes = exchange(proto_part(core.reshape(1), diff, stud_near, stud_far, devices), DP)
    *turned, codes = lax.optimization_barrier((*turned, codes))
    proto_grad = decoded(codes)
    feat = joined(own, turned).reshape(plane, -1, rows)
    feat = jnp.sum(exchange(feat, PLANE), axis=0)
    feat = exchange(copied(feat, size["z"] * size["yh"]), PROTO)
    feature_grad = 512.0 * feat.reshape(depth, rows).T
    return feature_grad, proto_grad


def solution(mesh):
    split = jax.sharding.Mesh(mesh.devices.reshape(2, 4, 2, 4, 2), AXES)
    return jax.shard_map(
        functools.partial(on_device, dict(split.shape)),
        mesh=split,
        in_specs=(P(DP, None), P(DP, None), P(None, PROTO)),
        out_specs=(P(DP, None), P(DP, PROTO)),
        check_vma=False,
    )
```

```python
import functools
import math

import jax
import jax.numpy as jnp
import numpy as np
from jax import lax
from jax.experimental import pallas as pl
from jax.experimental.pallas import tpu as pltpu
from jax.sharding import PartitionSpec as P

ITERS = 3
EPS = 1e-06
TEACH = float(np.float32(0.07))
STUD = float(np.float32(0.1))
LOG2E = math.log2(math.e)
TSCALE = LOG2E / TEACH
SSCALE = LOG2E / STUD
LOG_INV = -math.log2(STUD)
F32 = jnp.float32
BF16 = jnp.bfloat16
LANES = 128
MIB = 1024 * 1024
AXES = ("yl", "x", "c", "z", "yh")
DP = ("yl", "x", "c")
PROTO = ("z", "yh")
CHIPS = ("yl", "x")
PLANE = ("yl", "x", "yh")
PILLAR = ("z", "c")


def unit_rows(feats):
    wide = feats.astype(F32)
    squares = jnp.sum(wide * wide, axis=1, keepdims=True)
    return (wide * lax.rsqrt(squares + EPS)).astype(BF16)


def dot(a, b):
    return jnp.dot(a, b, preferred_element_type=F32)


def dot_nt(a, b):
    return lax.dot_general(a, b, (((1,), (1,)), ((), ())), preferred_element_type=F32)


def fold_rows(value):
    return jnp.sum(value.reshape(value.shape[0] // 8, 8, value.shape[1]), axis=0)


def params(mib):
    return pltpu.CompilerParams(vmem_limit_bytes=mib * MIB)


def vmem():
    return pl.BlockSpec(memory_space=pltpu.VMEM)


def smem():
    return pl.BlockSpec(memory_space=pltpu.SMEM)


def block_of(near_ref, far_ref, block):
    pairs = near_ref.shape[0]
    return near_ref[block] if block < pairs else far_ref[block - pairs]


def places(core, pairs, per):
    found = []
    for block in range(2 * pairs):
        parity = core if block < pairs else 1 - core
        found += [(2 * (block % pairs) + parity) * per + part for part in range(per)]
    return found


def sweep_kernel(copies, tile, has_parts, has_extra, *refs):
    refs = list(refs)
    core = refs.pop(0)[0]
    parts_ref = refs.pop(0) if has_parts else None
    extra_ref = refs.pop(0) if has_extra else None
    protos_ref, near_ref, far_ref, col_ref, out_ref, sums, scale, kern, acc = refs
    pairs, rows, _ = near_ref.shape
    blocks = 2 * pairs
    per = rows // LANES
    groups = blocks * per
    placed = places(core, pairs, per)
    if has_parts:
        sums[...] = 1.0 / jnp.sum(parts_ref[...], axis=0)
        for at, place in enumerate(placed):
            scale[at : at + 1, :] = sums[pl.ds(place, 1), :]
    acc[...] = jnp.zeros_like(acc)

    def one_tile(step, carry):
        here = pl.ds(pl.multiple_of(step * tile, tile), tile)
        protos = protos_ref[here, :]
        col_acc = jnp.zeros((tile, LANES), F32)
        for block in range(blocks):
            logits = dot_nt(protos, block_of(near_ref, far_ref, block))
            for part in range(per):
                value = jnp.exp2(logits[:, part * LANES : (part + 1) * LANES] * TSCALE)
                at = block * per + part
                kern[:, at * LANES : (at + 1) * LANES] = value
                col_acc = col_acc + (value * scale[at : at + 1, :] if has_parts else value)
        col = 1.0 / jnp.sum(col_acc, axis=1, keepdims=True)
        wide_col = jnp.broadcast_to(col, (tile, LANES))
        col_ref[here, :] = wide_col
        for at in range(groups):
            lanes = slice(at * LANES, (at + 1) * LANES)
            acc[:, lanes] += fold_rows(kern[:, lanes] * wide_col)
        return carry

    lax.fori_loop(0, protos_ref.shape[0] // tile, one_tile, 0)
    for at, place in enumerate(placed):
        total = jnp.sum(acc[:, at * LANES : (at + 1) * LANES], axis=0, keepdims=True)
        for copy in range(copies):
            out_ref[copy, pl.ds(place, 1), :] = total
    if has_extra:
        extra = extra_ref[...]
        for copy in range(copies):
            out_ref[copy, groups:, :] = extra


def sweep(core, parts, extra, protos, near, far, copies, tile=256):
    count = protos.shape[0]
    pairs, rows, _ = near.shape
    total = 2 * pairs * rows
    groups = total // LANES
    sent = groups if extra is None else groups + extra.shape[0]
    args = [a for a in (parts, extra) if a is not None] + [protos, near, far]
    return pl.pallas_call(
        functools.partial(sweep_kernel, copies, tile, parts is not None, extra is not None),
        in_specs=[smem()] + [vmem()] * len(args),
        out_specs=[vmem()] * 2,
        out_shape=[
            jax.ShapeDtypeStruct((count, LANES), F32),
            jax.ShapeDtypeStruct((copies, sent, LANES), F32),
        ],
        scratch_shapes=[
            pltpu.VMEM((groups, LANES), F32),
            pltpu.VMEM((groups, LANES), F32),
            pltpu.VMEM((tile, total), F32),
            pltpu.VMEM((8, total), F32),
        ],
        compiler_params=params(24),
        name="sweep",
    )(core, *args)


def totals_kernel(tile, core_ref, protos_ref, near_ref, far_ref, out_ref, acc):
    acc[...] = jnp.zeros_like(acc)
    pairs, rows, _ = near_ref.shape
    blocks = 2 * pairs

    def one_tile(step, carry):
        protos = protos_ref[pl.ds(pl.multiple_of(step * tile, tile), tile), :]
        for block in range(blocks):
            logits = dot_nt(protos, block_of(near_ref, far_ref, block))
            acc[:, block * rows : (block + 1) * rows] += fold_rows(jnp.exp2(logits * SSCALE))
        return carry

    lax.fori_loop(0, protos_ref.shape[0] // tile, one_tile, 0)
    for at, place in enumerate(places(core_ref[0], pairs, rows // LANES)):
        out_ref[pl.ds(place, 1), :] = jnp.sum(
            acc[:, at * LANES : (at + 1) * LANES], axis=0, keepdims=True
        )


def totals(core, protos, near, far, tile=512):
    count, depth = protos.shape
    pairs, rows, _ = near.shape
    blocks = 2 * pairs
    groups = blocks * rows // LANES
    return pl.pallas_call(
        functools.partial(totals_kernel, tile),
        in_specs=[smem()] + [vmem()] * 3,
        out_specs=vmem(),
        out_shape=jax.ShapeDtypeStruct((groups, LANES), F32),
        scratch_shapes=[pltpu.VMEM((8, blocks * rows), F32)],
        compiler_params=params(24),
        cost_estimate=pl.CostEstimate(
            flops=2 * count * depth * blocks * rows,
            bytes_accessed=4 * MIB,
            transcendentals=count * blocks * rows,
        ),
        name="totals",
    )(core, protos, near, far)


def hop_kernel(copies, in_ref, out_ref):
    total = jnp.sum(in_ref[...], axis=0)
    for copy in range(copies):
        out_ref[copy] = total


def hop(parts, copies):
    return pl.pallas_call(
        functools.partial(hop_kernel, copies),
        in_specs=[vmem()],
        out_specs=vmem(),
        out_shape=jax.ShapeDtypeStruct((copies,) + parts.shape[1:], F32),
        compiler_params=params(4),
        name="hop",
    )(parts)


def exchange(parts, axes):
    return lax.all_to_all(parts, axes, 0, 0, tiled=True)


def spread(parts, pillar):
    return exchange(hop(exchange(parts, PLANE), pillar), PILLAR)


def diff_kernel(
    tile, core_ref, parts_ref, col_ref, protos_ref, cols_ref, near_ref, far_ref, stud_near_ref, stud_far_ref,
    out_ref, mine_ref, other_ref, all_sums, scale, norm, diff, sems,
):
    pairs, rows, _ = near_ref.shape
    blocks = 2 * pairs
    per = rows // LANES
    groups = blocks * per
    all_sums[...] = LOG_INV - jnp.log2(jnp.sum(parts_ref[...], axis=0))
    for at, place in enumerate(places(core_ref[0], pairs, per)):
        scale[at : at + 1, :] = all_sums[pl.ds(place, 1), :]
        norm[at : at + 1, :] = all_sums[pl.ds(groups + place, 1), :]
    tiles = protos_ref.shape[0] // tile

    def span(step):
        return pl.ds(pl.multiple_of(step * tile, tile), tile)

    def store(step):
        return pltpu.make_async_copy(diff.at[span(step), :], out_ref.at[span(step), :], sems.at[step])

    def one_tile(step, carry):
        here = span(step)
        log_col = jnp.log2(col_ref[here, :])
        for block in range(blocks):
            teach_logits = dot_nt(protos_ref[here, :], block_of(near_ref, far_ref, block))
            stud_logits = dot_nt(protos_ref[here, :], block_of(stud_near_ref, stud_far_ref, block))
            for part in range(per):
                at = block * per + part
                lanes = slice(part * LANES, (part + 1) * LANES)
                target = jnp.exp2(teach_logits[:, lanes] * TSCALE + (scale[at : at + 1, :] + log_col))
                prob = jnp.exp2(stud_logits[:, lanes] * SSCALE + norm[at : at + 1, :])
                diff[here, at * LANES : (at + 1) * LANES] = (prob - target).astype(BF16)
        store(step).start()
        return carry

    lax.fori_loop(0, tiles, one_tile, 0)

    def one_pair(pair, carry):
        for first, ref in ((0, mine_ref), (pairs, other_ref)):
            start = pl.multiple_of((pair + first) * rows, rows)
            ref[pair] = dot(cols_ref[...], diff[:, pl.ds(start, rows)])
        return carry

    lax.fori_loop(0, pairs, one_pair, 0)

    def finish(step, carry):
        store(step).wait()
        return carry

    lax.fori_loop(0, tiles, finish, 0)


def differences(core, parts, col, protos, cols, near, far, stud_near, stud_far, tile=512):
    count, depth = protos.shape
    pairs, rows, _ = near.shape
    blocks = 2 * pairs
    groups = blocks * rows // LANES
    return pl.pallas_call(
        functools.partial(diff_kernel, tile),
        in_specs=[smem()] + [vmem()] * 8,
        out_specs=[pl.BlockSpec(memory_space=pl.ANY)] + [vmem()] * 2,
        out_shape=[
            jax.ShapeDtypeStruct((count, blocks * rows), BF16),
            jax.ShapeDtypeStruct((pairs, depth, rows), F32),
            jax.ShapeDtypeStruct((pairs, depth, rows), F32),
        ],
        scratch_shapes=[
            pltpu.VMEM((2 * groups, LANES), F32),
            pltpu.VMEM((groups, LANES), F32),
            pltpu.VMEM((groups, LANES), F32),
            pltpu.VMEM((count, blocks * rows), BF16),
            pltpu.SemaphoreType.DMA((count // tile,)),
        ],
        compiler_params=params(40),
        name="differences",
    )(core, parts, col, protos, cols, near, far, stud_near, stud_far)


SPAN = 250.0
FLOOR = 125.0


def power_of(top):
    return jnp.minimum(jnp.ceil(jnp.log2(jnp.maximum(top, 2.0**-120))), 126.0)


def encode(values, power):
    size = jnp.exp2(jnp.minimum(jnp.abs(values) * jnp.exp2(-power), 1.0) * SPAN - FLOOR)
    return jnp.where(values < 0, -size, size).astype(BF16)


def decode(code, power):
    wide = code.astype(F32)
    size = (jnp.log2(jnp.abs(wide)) + FLOOR) * (1.0 / SPAN) * jnp.exp2(power)
    return jnp.where(wide < 0, -size, size)


def decode_kernel(code_ref, out_ref):
    sources, share, width = code_ref.shape
    count = out_ref.shape[1] // sources

    def one_source(source, carry):
        powers = code_ref[source, :, count:].astype(F32)
        for part in range(count // LANES):
            code = code_ref[source, :, part * LANES : (part + 1) * LANES]
            start = pl.multiple_of(source * count + part * LANES, LANES)
            out_ref[:, pl.ds(start, LANES)] = decode(code, powers[part : part + 1, :])
        return carry

    lax.fori_loop(0, sources, one_source, 0)


def decoded(codes):
    sources, share, width = codes.shape
    return pl.pallas_call(
        decode_kernel,
        in_specs=[vmem()],
        out_specs=vmem(),
        out_shape=jax.ShapeDtypeStruct((share, sources * (width - LANES)), F32),
        compiler_params=params(16),
        cost_estimate=pl.CostEstimate(flops=16 * sources * share * width, bytes_accessed=4 * MIB, transcendentals=0),
        name="decoded",
    )(codes)


def pgrad_kernel(tile, diff_ref, near_ref, far_ref, out_ref, diff, powers, sems):
    tiles = diff.shape[0] // tile
    pairs, rows, depth = near_ref.shape
    reach = pairs * rows
    dests, share, _ = out_ref.shape

    def span(step):
        return pl.ds(pl.multiple_of(step * tile, tile), tile)

    def load(step):
        return pltpu.make_async_copy(diff_ref.at[span(step), :], diff.at[span(step), :], sems.at[step])

    def begin(step, carry):
        load(step).start()
        return carry

    def one_tile(step, carry):
        load(step).wait()
        mine = dot(diff[span(step), :reach], near_ref[...].reshape(reach, depth))
        others = dot(diff[span(step), reach:], far_ref[...].reshape(reach, depth))
        grads = (4096.0 * (mine + others)).T
        for dest in range(dests):
            values = grads[dest * share : (dest + 1) * share, :]
            power = power_of(jnp.max(jnp.abs(values), axis=0, keepdims=True))
            out_ref[dest, :, span(step)] = encode(values, power)
            for part in range(tile // LANES):
                row = step * (tile // LANES) + part
                powers[dest, pl.ds(row, 1), :] = power[:, part * LANES : (part + 1) * LANES]
        return carry

    lax.fori_loop(0, tiles, begin, 0)
    lax.fori_loop(0, tiles, one_tile, 0)
    out_ref[:, :, diff.shape[0] :] = powers[...].astype(BF16)


def proto_part(diff, near, far, dests, tile=512):
    count, total = diff.shape
    depth = near.shape[2]
    return pl.pallas_call(
        functools.partial(pgrad_kernel, tile),
        in_specs=[pl.BlockSpec(memory_space=pl.ANY), vmem(), vmem()],
        out_specs=vmem(),
        out_shape=jax.ShapeDtypeStruct((dests, depth // dests, count + LANES), BF16),
        scratch_shapes=[
            pltpu.VMEM((count, total), BF16),
            pltpu.VMEM((dests, count // LANES, LANES), F32),
            pltpu.SemaphoreType.DMA((count // tile,)),
        ],
        compiler_params=params(56),
        cost_estimate=pl.CostEstimate(
            flops=2 * count * total * depth, bytes_accessed=20 * MIB, transcendentals=0
        ),
        name="proto_part",
    )(diff, near, far)


GROUP = 16


def cut_kernel(level_ref, mine_ref, given_ref, own_ref, *code_refs):
    quarter = own_ref.shape[1]
    for by in range(len(code_refs) + 1):
        start = pl.multiple_of(lax.rem(level_ref[0] + by, len(code_refs) + 1) * quarter, quarter)
        for pair in range(own_ref.shape[0]):
            values = mine_ref[pair, pl.ds(start, quarter), :] + given_ref[pair, pl.ds(start, quarter), :]
            if by == 0:
                own_ref[pair] = values
                continue
            parts = [values[at : at + GROUP] for at in range(0, quarter, GROUP)]
            power = power_of(functools.reduce(jnp.maximum, [jnp.abs(part) for part in parts]))
            for at, part in enumerate(parts):
                code_refs[by - 1][pair, at * GROUP : (at + 1) * GROUP, :] = encode(part, power)
            code_refs[by - 1][pair, quarter:, :] = power.astype(BF16)


def cuts(level, mine, given, levels):
    pairs, depth, rows = mine.shape
    quarter = depth // levels
    return pl.pallas_call(
        cut_kernel,
        in_specs=[smem(), vmem(), vmem()],
        out_specs=[vmem()] * levels,
        out_shape=[jax.ShapeDtypeStruct((pairs, quarter, rows), F32)]
        + [jax.ShapeDtypeStruct((pairs, quarter + GROUP, rows), BF16)] * (levels - 1),
        compiler_params=params(16),
        name="cuts",
    )(level, mine, given)


def join_kernel(own_ref, *refs):
    out_ref = refs[-1]
    quarter = own_ref.shape[1]
    for pair in range(own_ref.shape[0]):
        powers = [ref[pair, quarter:, :].astype(F32) for ref in refs[:-1]]
        for at in range(0, quarter, GROUP):
            total = own_ref[pair, at : at + GROUP, :]
            for ref, power in zip(refs[:-1], powers):
                total = total + decode(ref[pair, at : at + GROUP, :], power)
            out_ref[pair, at : at + GROUP, :] = total


def joined(own, codes):
    return pl.pallas_call(
        join_kernel,
        in_specs=[vmem()] * (1 + len(codes)),
        out_specs=vmem(),
        out_shape=jax.ShapeDtypeStruct(own.shape, F32),
        compiler_params=params(8),
        name="joined",
    )(own, *codes)


def protos_kernel(place_ref, weight_ref, cols_ref, protos_ref, held, sem):
    depth, count = cols_ref.shape
    start = pl.multiple_of(place_ref[0] * count, count)
    copy = pltpu.make_async_copy(weight_ref.at[:, pl.ds(start, count)], held, sem)
    copy.start()
    copy.wait()
    tile = 512
    for at in range(0, count, tile):
        wide = held[:, at : at + tile].astype(F32)
        squares = jnp.sum(wide * wide, axis=0, keepdims=True)
        unit = wide * lax.rsqrt(squares + EPS)
        cols_ref[:, at : at + tile] = unit.astype(BF16)
        protos_ref[at : at + tile, :] = unit.T.astype(BF16)


def unit_protos(place, weight, count):
    depth = weight.shape[0]
    return pl.pallas_call(
        protos_kernel,
        in_specs=[smem(), pl.BlockSpec(memory_space=pl.ANY)],
        out_specs=[vmem()] * 2,
        out_shape=[
            jax.ShapeDtypeStruct((depth, count), BF16),
            jax.ShapeDtypeStruct((count, depth), BF16),
        ],
        scratch_shapes=[pltpu.VMEM((depth, count), BF16), pltpu.SemaphoreType.DMA(())],
        compiler_params=params(56),
        cost_estimate=pl.CostEstimate(
            flops=8 * count * depth, bytes_accessed=20 * MIB, transcendentals=count
        ),
        name="unit_protos",
    )(place, weight)


def swap(value):
    return lax.ppermute(value, "c", [(0, 1), (1, 0)])


def turn(value, by, size):
    return lax.ppermute(value, "z", [(i, (i + by) % size) for i in range(size)])


def copied(value, count):
    return jnp.broadcast_to(value[None], (count,) + value.shape)


def on_device(size, teacher_feats, student_feats, proto_weight):
    depth, held = proto_weight.shape
    devices = size["yl"] * size["x"] * size["c"]
    chips = size["yl"] * size["x"]
    plane = chips * size["yh"]
    pillar = size["z"] * size["c"]
    count = held // devices
    rows = teacher_feats.shape[0]
    core = lax.axis_index("c").reshape(1)
    level = lax.axis_index("z")

    near = exchange(copied(unit_rows(teacher_feats), chips), CHIPS)
    cols, protos = unit_protos(lax.axis_index(DP).reshape(1), proto_weight, count)
    stud_own = unit_rows(student_feats)
    near, protos, cols = lax.optimization_barrier((near, protos, cols))
    far = swap(near)
    stud_own, near = lax.optimization_barrier((stud_own, near))
    stud_near = lax.all_gather(stud_own, CHIPS)

    parts = None
    extra = None
    for step in range(ITERS):
        if step == ITERS - 1:
            extra = totals(core, protos, stud_near, stud_far)
        col, copies = sweep(core, parts, extra, protos, near, far, plane)
        parts = spread(copies, pillar)
        if step == 0:
            stud_near, parts = lax.optimization_barrier((stud_near, parts))
            stud_far = swap(stud_near)

    diff, mine_feat, other_feat = differences(
        core, parts, col, protos, cols, near, far, stud_near, stud_far
    )
    given_feat = swap(other_feat)
    own, *others = cuts(level.reshape(1), mine_feat, given_feat, size["z"])
    turned = [turn(part, by + 1, size["z"]) for by, part in enumerate(others)]
    codes = exchange(proto_part(diff, stud_near, stud_far, devices), DP)
    *turned, codes = lax.optimization_barrier((*turned, codes))
    proto_grad = decoded(codes)
    feat = joined(own, turned).reshape(plane, -1, rows)
    feat = jnp.sum(exchange(feat, PLANE), axis=0)
    feat = exchange(copied(feat, size["z"] * size["yh"]), PROTO)
    feature_grad = 512.0 * feat.reshape(depth, rows).T
    return feature_grad, proto_grad


def solution(mesh):
    split = jax.sharding.Mesh(mesh.devices.reshape(2, 4, 2, 4, 2), AXES)
    return jax.shard_map(
        functools.partial(on_device, dict(split.shape)),
        mesh=split,
        in_specs=(P(DP, None), P(DP, None), P(None, PROTO)),
        out_specs=(P(DP, None), P(DP, PROTO)),
        check_vma=False,
    )
```

```python
import functools
import math

import jax
import jax.numpy as jnp
import numpy as np
from jax import lax
from jax.experimental import pallas as pl
from jax.experimental.pallas import tpu as pltpu
from jax.sharding import PartitionSpec as P

ITERS = 3
EPS = 1e-06
TEACH = float(np.float32(0.07))
STUD = float(np.float32(0.1))
LOG2E = math.log2(math.e)
TSCALE = LOG2E / TEACH
SSCALE = LOG2E / STUD
LOG_INV = -math.log2(STUD)
F32 = jnp.float32
BF16 = jnp.bfloat16
LANES = 128
MIB = 1024 * 1024
AXES = ("yl", "x", "c", "z", "yh")
DP = ("yl", "x", "c")
PROTO = ("z", "yh")
CHIPS = ("yl", "x")
PLANE = ("yl", "x", "yh")
CUBE = ("yl", "x", "yh", "z")


def unit_rows(feats):
    wide = feats.astype(F32)
    squares = jnp.sum(wide * wide, axis=1, keepdims=True)
    return (wide * lax.rsqrt(squares + EPS)).astype(BF16)


def dot(a, b):
    return jnp.dot(a, b, preferred_element_type=F32)


def dot_nt(a, b):
    return lax.dot_general(a, b, (((1,), (1,)), ((), ())), preferred_element_type=F32)


def fold_rows(value):
    return jnp.sum(value.reshape(value.shape[0] // 8, 8, value.shape[1]), axis=0)


def params(mib):
    return pltpu.CompilerParams(vmem_limit_bytes=mib * MIB)


def vmem():
    return pl.BlockSpec(memory_space=pltpu.VMEM)


def smem():
    return pl.BlockSpec(memory_space=pltpu.SMEM)


def block_of(near_ref, far_ref, block):
    pairs = near_ref.shape[0]
    return near_ref[block] if block < pairs else far_ref[block - pairs]


def places(core, pairs, per):
    found = []
    for block in range(2 * pairs):
        parity = core if block < pairs else 1 - core
        found += [(2 * (block % pairs) + parity) * per + part for part in range(per)]
    return found


def put_halves(core, part_refs, sums, start=0):
    half = sums.shape[0] // 2
    for ref, first in zip(part_refs, (core, 1 - core)):
        sums[pl.ds(pl.multiple_of(first * half, half), half), :] = ref[start : start + half, :]


def sweep_kernel(tile, has_parts, has_extra, *refs):
    refs = list(refs)
    core = refs.pop(0)[0]
    part_refs = [refs.pop(0), refs.pop(0)] if has_parts else None
    extra_ref = refs.pop(0) if has_extra else None
    protos_ref, near_ref, far_ref, col_ref, out_ref, sums, scale, kern, acc = refs
    pairs, rows, _ = near_ref.shape
    blocks = 2 * pairs
    per = rows // LANES
    groups = blocks * per
    placed = places(core, pairs, per)
    if has_parts:
        put_halves(core, part_refs, sums)
        sums[...] = 1.0 / sums[...]
        for at, place in enumerate(placed):
            scale[at : at + 1, :] = sums[pl.ds(place, 1), :]
    acc[...] = jnp.zeros_like(acc)

    def one_tile(step, carry):
        here = pl.ds(pl.multiple_of(step * tile, tile), tile)
        protos = protos_ref[here, :]
        col_acc = jnp.zeros((tile, LANES), F32)
        for block in range(blocks):
            logits = dot_nt(protos, block_of(near_ref, far_ref, block))
            for part in range(per):
                value = jnp.exp2(logits[:, part * LANES : (part + 1) * LANES] * TSCALE)
                at = block * per + part
                kern[:, at * LANES : (at + 1) * LANES] = value
                col_acc = col_acc + (value * scale[at : at + 1, :] if has_parts else value)
        col = 1.0 / jnp.sum(col_acc, axis=1, keepdims=True)
        wide_col = jnp.broadcast_to(col, (tile, LANES))
        col_ref[here, :] = wide_col
        for at in range(groups):
            lanes = slice(at * LANES, (at + 1) * LANES)
            acc[:, lanes] += fold_rows(kern[:, lanes] * wide_col)
        return carry

    lax.fori_loop(0, protos_ref.shape[0] // tile, one_tile, 0)
    for at, place in enumerate(placed):
        total = jnp.sum(acc[:, at * LANES : (at + 1) * LANES], axis=0, keepdims=True)
        out_ref[pl.ds(place, 1), :] = total
    if has_extra:
        out_ref[groups:, :] = extra_ref[...]


def sweep(core, parts, extra, protos, near, far, tile=256):
    count = protos.shape[0]
    pairs, rows, _ = near.shape
    total = 2 * pairs * rows
    groups = total // LANES
    sent = groups if extra is None else groups + extra.shape[0]
    args = list(parts or []) + ([] if extra is None else [extra]) + [protos, near, far]
    return pl.pallas_call(
        functools.partial(sweep_kernel, tile, parts is not None, extra is not None),
        in_specs=[smem()] + [vmem()] * len(args),
        out_specs=[vmem()] * 2,
        out_shape=[
            jax.ShapeDtypeStruct((count, LANES), F32),
            jax.ShapeDtypeStruct((sent, LANES), F32),
        ],
        scratch_shapes=[
            pltpu.VMEM((groups, LANES), F32),
            pltpu.VMEM((groups, LANES), F32),
            pltpu.VMEM((tile, total), F32),
            pltpu.VMEM((8, total), F32),
        ],
        compiler_params=params(24),
        name="sweep",
    )(core, *args)


def totals_kernel(tile, core_ref, protos_ref, near_ref, far_ref, out_ref, acc):
    acc[...] = jnp.zeros_like(acc)
    pairs, rows, _ = near_ref.shape
    blocks = 2 * pairs

    def one_tile(step, carry):
        protos = protos_ref[pl.ds(pl.multiple_of(step * tile, tile), tile), :]
        for block in range(blocks):
            logits = dot_nt(protos, block_of(near_ref, far_ref, block))
            acc[:, block * rows : (block + 1) * rows] += fold_rows(jnp.exp2(logits * SSCALE))
        return carry

    lax.fori_loop(0, protos_ref.shape[0] // tile, one_tile, 0)
    for at, place in enumerate(places(core_ref[0], pairs, rows // LANES)):
        out_ref[pl.ds(place, 1), :] = jnp.sum(
            acc[:, at * LANES : (at + 1) * LANES], axis=0, keepdims=True
        )


def totals(core, protos, near, far, tile=512):
    count, depth = protos.shape
    pairs, rows, _ = near.shape
    blocks = 2 * pairs
    groups = blocks * rows // LANES
    return pl.pallas_call(
        functools.partial(totals_kernel, tile),
        in_specs=[smem()] + [vmem()] * 3,
        out_specs=vmem(),
        out_shape=jax.ShapeDtypeStruct((groups, LANES), F32),
        scratch_shapes=[pltpu.VMEM((8, blocks * rows), F32)],
        compiler_params=params(24),
        cost_estimate=pl.CostEstimate(
            flops=2 * count * depth * blocks * rows,
            bytes_accessed=4 * MIB,
            transcendentals=count * blocks * rows,
        ),
        name="totals",
    )(core, protos, near, far)


def halve_kernel(groups, core_ref, mine_ref, other_ref, out_ref):
    half = groups // 2
    parts = []
    for at in range(0, mine_ref.shape[0], groups):
        rows = pl.ds(pl.multiple_of(at + core_ref[0] * half, half), half)
        parts.append(mine_ref[rows, :] + other_ref[rows, :])
    total = jnp.concatenate(parts, axis=0)
    for copy in range(out_ref.shape[0]):
        out_ref[copy] = total


def halved(core, mine, other, groups, copies):
    return pl.pallas_call(
        functools.partial(halve_kernel, groups),
        in_specs=[smem(), vmem(), vmem()],
        out_specs=vmem(),
        out_shape=jax.ShapeDtypeStruct((copies, mine.shape[0] // 2, LANES), F32),
        compiler_params=params(8),
        name="halved",
    )(core, mine, other)


def total_kernel(in_ref, out_ref):
    out_ref[...] = jnp.sum(in_ref[...], axis=0)


def totalled(parts):
    return pl.pallas_call(
        total_kernel,
        in_specs=[vmem()],
        out_specs=vmem(),
        out_shape=jax.ShapeDtypeStruct(parts.shape[1:], F32),
        compiler_params=params(8),
        name="totalled",
    )(parts)


def exchange(parts, axes):
    return lax.all_to_all(parts, axes, 0, 0, tiled=True)


def spread(core, part, groups, chips, beside):
    parts = exchange(halved(core, part, swap(part), groups, chips), CUBE)
    parts, beside = lax.optimization_barrier((parts, beside))
    mine = totalled(parts)
    return (mine, swap(mine)), beside


def diff_kernel(
    tile, core_ref, mine_part_ref, other_part_ref, col_ref, protos_ref, cols_ref, near_ref, far_ref, stud_near_ref, stud_far_ref,
    out_ref, mine_ref, other_ref, sums, scale, norm, diff, sems,
):
    pairs, rows, _ = near_ref.shape
    blocks = 2 * pairs
    per = rows // LANES
    groups = blocks * per
    core = core_ref[0]
    for start, ref in ((0, scale), (groups // 2, norm)):
        put_halves(core, (mine_part_ref, other_part_ref), sums, start)
        sums[...] = LOG_INV - jnp.log2(sums[...])
        for at, place in enumerate(places(core, pairs, per)):
            ref[at : at + 1, :] = sums[pl.ds(place, 1), :]
    tiles = protos_ref.shape[0] // tile

    def span(step):
        return pl.ds(pl.multiple_of(step * tile, tile), tile)

    def store(step):
        return pltpu.make_async_copy(diff.at[span(step), :], out_ref.at[span(step), :], sems.at[step])

    def one_tile(step, carry):
        here = span(step)
        log_col = jnp.log2(col_ref[here, :])
        for block in range(blocks):
            teach_logits = dot_nt(protos_ref[here, :], block_of(near_ref, far_ref, block))
            stud_logits = dot_nt(protos_ref[here, :], block_of(stud_near_ref, stud_far_ref, block))
            for part in range(per):
                at = block * per + part
                lanes = slice(part * LANES, (part + 1) * LANES)
                target = jnp.exp2(teach_logits[:, lanes] * TSCALE + (scale[at : at + 1, :] + log_col))
                prob = jnp.exp2(stud_logits[:, lanes] * SSCALE + norm[at : at + 1, :])
                diff[here, at * LANES : (at + 1) * LANES] = (prob - target).astype(BF16)
        store(step).start()
        return carry

    lax.fori_loop(0, tiles, one_tile, 0)

    def one_pair(pair, carry):
        for first, ref in ((0, mine_ref), (pairs, other_ref)):
            start = pl.multiple_of((pair + first) * rows, rows)
            ref[pair] = dot(cols_ref[...], diff[:, pl.ds(start, rows)])
        return carry

    lax.fori_loop(0, pairs, one_pair, 0)

    def finish(step, carry):
        store(step).wait()
        return carry

    lax.fori_loop(0, tiles, finish, 0)


def differences(core, parts, col, protos, cols, near, far, stud_near, stud_far, tile=512):
    count, depth = protos.shape
    pairs, rows, _ = near.shape
    blocks = 2 * pairs
    groups = blocks * rows // LANES
    return pl.pallas_call(
        functools.partial(diff_kernel, tile),
        in_specs=[smem()] + [vmem()] * 9,
        out_specs=[pl.BlockSpec(memory_space=pl.ANY)] + [vmem()] * 2,
        out_shape=[
            jax.ShapeDtypeStruct((count, blocks * rows), BF16),
            jax.ShapeDtypeStruct((pairs, depth, rows), F32),
            jax.ShapeDtypeStruct((pairs, depth, rows), F32),
        ],
        scratch_shapes=[
            pltpu.VMEM((groups, LANES), F32),
            pltpu.VMEM((groups, LANES), F32),
            pltpu.VMEM((groups, LANES), F32),
            pltpu.VMEM((count, blocks * rows), BF16),
            pltpu.SemaphoreType.DMA((count // tile,)),
        ],
        compiler_params=params(40),
        name="differences",
    )(core, *parts, col, protos, cols, near, far, stud_near, stud_far)


SPAN = 250.0
FLOOR = 125.0


def power_of(top):
    return jnp.minimum(jnp.ceil(jnp.log2(jnp.maximum(top, 2.0**-120))), 126.0)


def encode(values, power):
    size = jnp.exp2(jnp.minimum(jnp.abs(values) * jnp.exp2(-power), 1.0) * SPAN - FLOOR)
    return jnp.where(values < 0, -size, size).astype(BF16)


def decode(code, power):
    wide = code.astype(F32)
    size = (jnp.log2(jnp.abs(wide)) + FLOOR) * (1.0 / SPAN) * jnp.exp2(power)
    return jnp.where(wide < 0, -size, size)


def decode_kernel(code_ref, out_ref):
    sources, share, width = code_ref.shape
    count = out_ref.shape[1] // sources

    def one_source(source, carry):
        powers = code_ref[source, :, count:].astype(F32)
        for part in range(count // LANES):
            code = code_ref[source, :, part * LANES : (part + 1) * LANES]
            start = pl.multiple_of(source * count + part * LANES, LANES)
            out_ref[:, pl.ds(start, LANES)] = decode(code, powers[part : part + 1, :])
        return carry

    lax.fori_loop(0, sources, one_source, 0)


def decoded(codes):
    sources, share, width = codes.shape
    return pl.pallas_call(
        decode_kernel,
        in_specs=[vmem()],
        out_specs=vmem(),
        out_shape=jax.ShapeDtypeStruct((share, sources * (width - LANES)), F32),
        compiler_params=params(16),
        cost_estimate=pl.CostEstimate(flops=16 * sources * share * width, bytes_accessed=4 * MIB, transcendentals=0),
        name="decoded",
    )(codes)


def pgrad_kernel(tile, diff_ref, near_ref, far_ref, out_ref, diff, powers, sems):
    tiles = diff.shape[0] // tile
    pairs, rows, depth = near_ref.shape
    reach = pairs * rows
    dests, share, _ = out_ref.shape

    def span(step):
        return pl.ds(step * tile, tile)

    def load(step):
        return pltpu.make_async_copy(diff_ref.at[span(step), :], diff.at[span(step), :], sems.at[step])

    def begin(step, carry):
        load(step).start()
        return carry

    def one_tile(step, carry):
        load(step).wait()
        mine = dot(diff[span(step), :reach], near_ref[...].reshape(reach, depth))
        others = dot(diff[span(step), reach:], far_ref[...].reshape(reach, depth))
        grads = (4096.0 * (mine + others)).T
        for dest in range(dests):
            values = grads[dest * share : (dest + 1) * share, :]
            power = power_of(jnp.max(jnp.abs(values), axis=0, keepdims=True))
            out_ref[dest, :, span(step)] = encode(values, power)
            for part in range(tile // LANES):
                row = step * (tile // LANES) + part
                powers[dest, pl.ds(row, 1), :] = power[:, part * LANES : (part + 1) * LANES]
        return carry

    for step in range(tiles):
        begin(step, 0)
    for step in range(tiles):
        one_tile(step, 0)
    out_ref[:, :, diff.shape[0] :] = powers[...].astype(BF16)


def proto_part(diff, near, far, dests, tile=512):
    count, total = diff.shape
    depth = near.shape[2]
    return pl.pallas_call(
        functools.partial(pgrad_kernel, tile),
        in_specs=[pl.BlockSpec(memory_space=pl.ANY), vmem(), vmem()],
        out_specs=vmem(),
        out_shape=jax.ShapeDtypeStruct((dests, depth // dests, count + LANES), BF16),
        scratch_shapes=[
            pltpu.VMEM((count, total), BF16),
            pltpu.VMEM((dests, count // LANES, LANES), F32),
            pltpu.SemaphoreType.DMA((count // tile,)),
        ],
        compiler_params=params(56),
        cost_estimate=pl.CostEstimate(
            flops=2 * count * total * depth, bytes_accessed=20 * MIB, transcendentals=0
        ),
        name="proto_part",
    )(diff, near, far)


GROUP = 16


def cut_kernel(level_ref, mine_ref, given_ref, own_ref, *code_refs):
    quarter = own_ref.shape[1]
    for by in range(len(code_refs) + 1):
        start = pl.multiple_of(lax.rem(level_ref[0] + by, len(code_refs) + 1) * quarter, quarter)
        for pair in range(own_ref.shape[0]):
            values = mine_ref[pair, pl.ds(start, quarter), :] + given_ref[pair, pl.ds(start, quarter), :]
            if by == 0:
                own_ref[pair] = values
                continue
            parts = [values[at : at + GROUP] for at in range(0, quarter, GROUP)]
            power = power_of(functools.reduce(jnp.maximum, [jnp.abs(part) for part in parts]))
            for at, part in enumerate(parts):
                code_refs[by - 1][pair, at * GROUP : (at + 1) * GROUP, :] = encode(part, power)
            code_refs[by - 1][pair, quarter:, :] = power.astype(BF16)


def cuts(level, mine, given, levels):
    pairs, depth, rows = mine.shape
    quarter = depth // levels
    return pl.pallas_call(
        cut_kernel,
        in_specs=[smem(), vmem(), vmem()],
        out_specs=[vmem()] * levels,
        out_shape=[jax.ShapeDtypeStruct((pairs, quarter, rows), F32)]
        + [jax.ShapeDtypeStruct((pairs, quarter + GROUP, rows), BF16)] * (levels - 1),
        compiler_params=params(16),
        name="cuts",
    )(level, mine, given)


def join_kernel(own_ref, *refs):
    out_ref = refs[-1]
    quarter = own_ref.shape[1]
    for pair in range(own_ref.shape[0]):
        powers = [ref[pair, quarter:, :].astype(F32) for ref in refs[:-1]]
        for at in range(0, quarter, GROUP):
            total = own_ref[pair, at : at + GROUP, :]
            for ref, power in zip(refs[:-1], powers):
                total = total + decode(ref[pair, at : at + GROUP, :], power)
            out_ref[pair, at : at + GROUP, :] = total


def joined(own, codes):
    return pl.pallas_call(
        join_kernel,
        in_specs=[vmem()] * (1 + len(codes)),
        out_specs=vmem(),
        out_shape=jax.ShapeDtypeStruct(own.shape, F32),
        compiler_params=params(8),
        name="joined",
    )(own, *codes)


def protos_kernel(place_ref, weight_ref, cols_ref, protos_ref, held, sem):
    depth, count = cols_ref.shape
    start = pl.multiple_of(place_ref[0] * count, count)
    copy = pltpu.make_async_copy(weight_ref.at[:, pl.ds(start, count)], held, sem)
    copy.start()
    copy.wait()
    tile = 512
    for at in range(0, count, tile):
        wide = held[:, at : at + tile].astype(F32)
        squares = jnp.sum(wide * wide, axis=0, keepdims=True)
        unit = wide * lax.rsqrt(squares + EPS)
        cols_ref[:, at : at + tile] = unit.astype(BF16)
        protos_ref[at : at + tile, :] = unit.T.astype(BF16)


def unit_protos(place, weight, count):
    depth = weight.shape[0]
    return pl.pallas_call(
        protos_kernel,
        in_specs=[smem(), pl.BlockSpec(memory_space=pl.ANY)],
        out_specs=[vmem()] * 2,
        out_shape=[
            jax.ShapeDtypeStruct((depth, count), BF16),
            jax.ShapeDtypeStruct((count, depth), BF16),
        ],
        scratch_shapes=[pltpu.VMEM((depth, count), BF16), pltpu.SemaphoreType.DMA(())],
        compiler_params=params(56),
        cost_estimate=pl.CostEstimate(
            flops=8 * count * depth, bytes_accessed=20 * MIB, transcendentals=count
        ),
        name="unit_protos",
    )(place, weight)


def swap(value):
    return lax.ppermute(value, "c", [(0, 1), (1, 0)])


def turn(value, by, size):
    return lax.ppermute(value, "z", [(i, (i + by) % size) for i in range(size)])


def copied(value, count):
    return jnp.broadcast_to(value[None], (count,) + value.shape)


def on_device(size, teacher_feats, student_feats, proto_weight):
    depth, held = proto_weight.shape
    devices = size["yl"] * size["x"] * size["c"]
    chips = size["yl"] * size["x"]
    plane = chips * size["yh"]
    count = held // devices
    rows = teacher_feats.shape[0]
    core = lax.axis_index("c").reshape(1)
    level = lax.axis_index("z")

    near = exchange(copied(unit_rows(teacher_feats), chips), CHIPS)
    cols, protos = unit_protos(lax.axis_index(DP).reshape(1), proto_weight, count)
    stud_own = unit_rows(student_feats)
    near, protos, cols = lax.optimization_barrier((near, protos, cols))
    far = swap(near)
    stud_own, near = lax.optimization_barrier((stud_own, near))
    stud_near = lax.all_gather(stud_own, CHIPS)

    parts = None
    extra = None
    for step in range(ITERS):
        col, part = sweep(core, parts, extra if step == ITERS - 1 else None, protos, near, far)
        if step == ITERS - 2:
            extra = totals(core, protos, stud_near, stud_far)
        parts, extra = spread(core, part, devices * rows // LANES, plane * size["z"], extra)
        if step == 0:
            stud_near, *parts = lax.optimization_barrier((stud_near, *parts))
            stud_far = swap(stud_near)

    diff, mine_feat, other_feat = differences(
        core, parts, col, protos, cols, near, far, stud_near, stud_far
    )
    given_feat = swap(other_feat)
    own, *others = cuts(level.reshape(1), mine_feat, given_feat, size["z"])
    turned = [turn(part, by + 1, size["z"]) for by, part in enumerate(others)]
    codes = exchange(proto_part(diff, stud_near, stud_far, devices), DP)
    *turned, codes = lax.optimization_barrier((*turned, codes))
    proto_grad = decoded(codes)
    feat = joined(own, turned).reshape(plane, -1, rows)
    feat = jnp.sum(exchange(feat, PLANE), axis=0)
    feat = exchange(copied(feat, size["z"] * size["yh"]), PROTO)
    feature_grad = 512.0 * feat.reshape(depth, rows).T
    return feature_grad, proto_grad


def solution(mesh):
    split = jax.sharding.Mesh(mesh.devices.reshape(2, 4, 2, 4, 2), AXES)
    return jax.shard_map(
        functools.partial(on_device, dict(split.shape)),
        mesh=split,
        in_specs=(P(DP, None), P(DP, None), P(None, PROTO)),
        out_specs=(P(DP, None), P(DP, PROTO)),
        check_vma=False,
    )
```

```python
import functools
import math

import jax
import jax.numpy as jnp
import numpy as np
from jax import lax
from jax.experimental import pallas as pl
from jax.experimental.pallas import tpu as pltpu
from jax.sharding import PartitionSpec as P

ITERS = 3
EPS = 1e-06
TEACH = float(np.float32(0.07))
STUD = float(np.float32(0.1))
LOG2E = math.log2(math.e)
TSCALE = LOG2E / TEACH
SSCALE = LOG2E / STUD
LOG_INV = -math.log2(STUD)
F32 = jnp.float32
BF16 = jnp.bfloat16
LANES = 128
MIB = 1024 * 1024
AXES = ("yl", "x", "c", "z", "yh")
DP = ("yl", "x", "c")
PROTO = ("z", "yh")
CHIPS = ("yl", "x")
PLANE = ("yl", "x", "yh")
PILLAR = ("z", "c")


def unit_rows(feats):
    wide = feats.astype(F32)
    squares = jnp.sum(wide * wide, axis=1, keepdims=True)
    return (wide * lax.rsqrt(squares + EPS)).astype(BF16)


def dot(a, b):
    return jnp.dot(a, b, preferred_element_type=F32)


def dot_nt(a, b):
    return lax.dot_general(a, b, (((1,), (1,)), ((), ())), preferred_element_type=F32)


def fold_rows(value):
    return jnp.sum(value.reshape(value.shape[0] // 8, 8, value.shape[1]), axis=0)


def params(mib):
    return pltpu.CompilerParams(vmem_limit_bytes=mib * MIB)


def vmem():
    return pl.BlockSpec(memory_space=pltpu.VMEM)


def smem():
    return pl.BlockSpec(memory_space=pltpu.SMEM)


def unit_copies_kernel(feats_ref, out_ref):
    unit = unit_rows(feats_ref[...])
    for copy in range(out_ref.shape[0]):
        out_ref[copy] = unit


def unit_copies(feats, copies):
    return pl.pallas_call(
        unit_copies_kernel,
        in_specs=[vmem()],
        out_specs=vmem(),
        out_shape=jax.ShapeDtypeStruct((copies,) + feats.shape, BF16),
        compiler_params=params(8),
        name="unit_copies",
    )(feats)


def block_of(near_ref, far_ref, block):
    pairs = near_ref.shape[0]
    return near_ref[block] if block < pairs else far_ref[block - pairs]


def places(core, pairs, per):
    found = []
    for block in range(2 * pairs):
        parity = core if block < pairs else 1 - core
        found += [(2 * (block % pairs) + parity) * per + part for part in range(per)]
    return found


def sweep_kernel(copies, tile, has_parts, has_extra, *refs):
    refs = list(refs)
    core = refs.pop(0)[0]
    parts_ref = refs.pop(0) if has_parts else None
    extra_ref = refs.pop(0) if has_extra else None
    protos_ref, near_ref, far_ref, col_ref, out_ref, sums, scale, kern, acc = refs
    pairs, rows, _ = near_ref.shape
    blocks = 2 * pairs
    per = rows // LANES
    groups = blocks * per
    placed = places(core, pairs, per)
    if has_parts:
        sums[...] = 1.0 / jnp.sum(parts_ref[...], axis=0)
        for at, place in enumerate(placed):
            scale[at : at + 1, :] = sums[pl.ds(place, 1), :]
    acc[...] = jnp.zeros_like(acc)

    def one_tile(step, carry):
        here = pl.ds(pl.multiple_of(step * tile, tile), tile)
        protos = protos_ref[here, :]
        col_acc = jnp.zeros((tile, LANES), F32)
        for block in range(blocks):
            logits = dot_nt(protos, block_of(near_ref, far_ref, block))
            for part in range(per):
                value = jnp.exp2(logits[:, part * LANES : (part + 1) * LANES] * TSCALE)
                at = block * per + part
                kern[:, at * LANES : (at + 1) * LANES] = value
                col_acc = col_acc + (value * scale[at : at + 1, :] if has_parts else value)
        col = 1.0 / jnp.sum(col_acc, axis=1, keepdims=True)
        wide_col = jnp.broadcast_to(col, (tile, LANES))
        col_ref[here, :] = wide_col
        for at in range(groups):
            lanes = slice(at * LANES, (at + 1) * LANES)
            acc[:, lanes] += fold_rows(kern[:, lanes] * wide_col)
        return carry

    lax.fori_loop(0, protos_ref.shape[0] // tile, one_tile, 0)
    for at, place in enumerate(placed):
        total = jnp.sum(acc[:, at * LANES : (at + 1) * LANES], axis=0, keepdims=True)
        for copy in range(copies):
            out_ref[copy, pl.ds(place, 1), :] = total
    if has_extra:
        extra = extra_ref[...]
        for copy in range(copies):
            out_ref[copy, groups:, :] = extra


def sweep(core, parts, extra, protos, near, far, copies, tile=256):
    count = protos.shape[0]
    pairs, rows, _ = near.shape
    total = 2 * pairs * rows
    groups = total // LANES
    sent = groups if extra is None else groups + extra.shape[0]
    args = [a for a in (parts, extra) if a is not None] + [protos, near, far]
    return pl.pallas_call(
        functools.partial(sweep_kernel, copies, tile, parts is not None, extra is not None),
        in_specs=[smem()] + [vmem()] * len(args),
        out_specs=[vmem()] * 2,
        out_shape=[
            jax.ShapeDtypeStruct((count, LANES), F32),
            jax.ShapeDtypeStruct((copies, sent, LANES), F32),
        ],
        scratch_shapes=[
            pltpu.VMEM((groups, LANES), F32),
            pltpu.VMEM((groups, LANES), F32),
            pltpu.VMEM((tile, total), F32),
            pltpu.VMEM((8, total), F32),
        ],
        compiler_params=params(24),
        name="sweep",
    )(core, *args)


def totals_kernel(tile, core_ref, protos_ref, near_ref, far_ref, out_ref, acc):
    acc[...] = jnp.zeros_like(acc)
    pairs, rows, _ = near_ref.shape
    blocks = 2 * pairs

    def one_tile(step, carry):
        protos = protos_ref[pl.ds(pl.multiple_of(step * tile, tile), tile), :]
        for block in range(blocks):
            logits = dot_nt(protos, block_of(near_ref, far_ref, block))
            acc[:, block * rows : (block + 1) * rows] += fold_rows(jnp.exp2(logits * SSCALE))
        return carry

    lax.fori_loop(0, protos_ref.shape[0] // tile, one_tile, 0)
    for at, place in enumerate(places(core_ref[0], pairs, rows // LANES)):
        out_ref[pl.ds(place, 1), :] = jnp.sum(
            acc[:, at * LANES : (at + 1) * LANES], axis=0, keepdims=True
        )


def totals(core, protos, near, far, tile=512):
    count, depth = protos.shape
    pairs, rows, _ = near.shape
    blocks = 2 * pairs
    groups = blocks * rows // LANES
    return pl.pallas_call(
        functools.partial(totals_kernel, tile),
        in_specs=[smem()] + [vmem()] * 3,
        out_specs=vmem(),
        out_shape=jax.ShapeDtypeStruct((groups, LANES), F32),
        scratch_shapes=[pltpu.VMEM((8, blocks * rows), F32)],
        compiler_params=params(24),
        cost_estimate=pl.CostEstimate(
            flops=2 * count * depth * blocks * rows,
            bytes_accessed=4 * MIB,
            transcendentals=count * blocks * rows,
        ),
        name="totals",
    )(core, protos, near, far)


def hop_kernel(copies, in_ref, out_ref):
    total = jnp.sum(in_ref[...], axis=0)
    for copy in range(copies):
        out_ref[copy] = total


def hop(parts, copies):
    return pl.pallas_call(
        functools.partial(hop_kernel, copies),
        in_specs=[vmem()],
        out_specs=vmem(),
        out_shape=jax.ShapeDtypeStruct((copies,) + parts.shape[1:], F32),
        compiler_params=params(4),
        name="hop",
    )(parts)


def exchange(parts, axes):
    return lax.all_to_all(parts, axes, 0, 0, tiled=True)


def spread(parts, pillar):
    return exchange(hop(exchange(parts, PLANE), pillar), PILLAR)


def diff_kernel(
    tile, core_ref, parts_ref, col_ref, protos_ref, cols_ref, near_ref, far_ref, stud_near_ref, stud_far_ref,
    out_ref, mine_ref, other_ref, all_sums, scale, norm, diff, sems,
):
    pairs, rows, _ = near_ref.shape
    blocks = 2 * pairs
    per = rows // LANES
    groups = blocks * per
    all_sums[...] = LOG_INV - jnp.log2(jnp.sum(parts_ref[...], axis=0))
    for at, place in enumerate(places(core_ref[0], pairs, per)):
        scale[at : at + 1, :] = all_sums[pl.ds(place, 1), :]
        norm[at : at + 1, :] = all_sums[pl.ds(groups + place, 1), :]
    tiles = protos_ref.shape[0] // tile

    def span(step):
        return pl.ds(pl.multiple_of(step * tile, tile), tile)

    def store(step):
        return pltpu.make_async_copy(diff.at[span(step), :], out_ref.at[span(step), :], sems.at[step])

    def one_tile(step, carry):
        here = span(step)
        log_col = jnp.log2(col_ref[here, :])
        for block in range(blocks):
            teach_logits = dot_nt(protos_ref[here, :], block_of(near_ref, far_ref, block))
            stud_logits = dot_nt(protos_ref[here, :], block_of(stud_near_ref, stud_far_ref, block))
            for part in range(per):
                at = block * per + part
                lanes = slice(part * LANES, (part + 1) * LANES)
                target = jnp.exp2(teach_logits[:, lanes] * TSCALE + (scale[at : at + 1, :] + log_col))
                prob = jnp.exp2(stud_logits[:, lanes] * SSCALE + norm[at : at + 1, :])
                diff[here, at * LANES : (at + 1) * LANES] = (prob - target).astype(BF16)
        store(step).start()
        return carry

    lax.fori_loop(0, tiles, one_tile, 0)

    def one_pair(pair, carry):
        for first, ref in ((0, mine_ref), (pairs, other_ref)):
            start = pl.multiple_of((pair + first) * rows, rows)
            ref[pair] = dot(cols_ref[...], diff[:, pl.ds(start, rows)])
        return carry

    lax.fori_loop(0, pairs, one_pair, 0)

    def finish(step, carry):
        store(step).wait()
        return carry

    lax.fori_loop(0, tiles, finish, 0)


def differences(core, parts, col, protos, cols, near, far, stud_near, stud_far, tile=512):
    count, depth = protos.shape
    pairs, rows, _ = near.shape
    blocks = 2 * pairs
    groups = blocks * rows // LANES
    return pl.pallas_call(
        functools.partial(diff_kernel, tile),
        in_specs=[smem()] + [vmem()] * 8,
        out_specs=[pl.BlockSpec(memory_space=pl.ANY)] + [vmem()] * 2,
        out_shape=[
            jax.ShapeDtypeStruct((count, blocks * rows), BF16),
            jax.ShapeDtypeStruct((pairs, depth, rows), F32),
            jax.ShapeDtypeStruct((pairs, depth, rows), F32),
        ],
        scratch_shapes=[
            pltpu.VMEM((2 * groups, LANES), F32),
            pltpu.VMEM((groups, LANES), F32),
            pltpu.VMEM((groups, LANES), F32),
            pltpu.VMEM((count, blocks * rows), BF16),
            pltpu.SemaphoreType.DMA((count // tile,)),
        ],
        compiler_params=params(40),
        name="differences",
    )(core, parts, col, protos, cols, near, far, stud_near, stud_far)


SPAN = 250.0
FLOOR = 125.0


def power_of(top):
    return jnp.minimum(jnp.ceil(jnp.log2(jnp.maximum(top, 2.0**-120))), 126.0)


def encode(values, power):
    size = jnp.exp2(jnp.minimum(jnp.abs(values) * jnp.exp2(-power), 1.0) * SPAN - FLOOR)
    return jnp.where(values < 0, -size, size).astype(BF16)


def decode(code, power):
    wide = code.astype(F32)
    size = (jnp.log2(jnp.abs(wide)) + FLOOR) * (1.0 / SPAN) * jnp.exp2(power)
    return jnp.where(wide < 0, -size, size)


def decode_kernel(code_ref, out_ref):
    sources, share, width = code_ref.shape
    count = out_ref.shape[1] // sources

    def one_source(source, carry):
        powers = code_ref[source, :, count:].astype(F32)
        for part in range(count // LANES):
            code = code_ref[source, :, part * LANES : (part + 1) * LANES]
            start = pl.multiple_of(source * count + part * LANES, LANES)
            out_ref[:, pl.ds(start, LANES)] = decode(code, powers[part : part + 1, :])
        return carry

    lax.fori_loop(0, sources, one_source, 0)


def decoded(codes):
    sources, share, width = codes.shape
    return pl.pallas_call(
        decode_kernel,
        in_specs=[vmem()],
        out_specs=vmem(),
        out_shape=jax.ShapeDtypeStruct((share, sources * (width - LANES)), F32),
        compiler_params=params(16),
        cost_estimate=pl.CostEstimate(flops=16 * sources * share * width, bytes_accessed=4 * MIB, transcendentals=0),
        name="decoded",
    )(codes)


def pgrad_kernel(tile, diff_ref, near_ref, far_ref, out_ref, diff, powers, sems):
    tiles = diff.shape[0] // tile
    pairs, rows, depth = near_ref.shape
    reach = pairs * rows
    dests, share, _ = out_ref.shape

    def span(step):
        return pl.ds(pl.multiple_of(step * tile, tile), tile)

    def load(step):
        return pltpu.make_async_copy(diff_ref.at[span(step), :], diff.at[span(step), :], sems.at[step])

    def begin(step, carry):
        load(step).start()
        return carry

    def one_tile(step, carry):
        load(step).wait()
        mine = dot(diff[span(step), :reach], near_ref[...].reshape(reach, depth))
        others = dot(diff[span(step), reach:], far_ref[...].reshape(reach, depth))
        grads = (4096.0 * (mine + others)).T
        for dest in range(dests):
            values = grads[dest * share : (dest + 1) * share, :]
            power = power_of(jnp.max(jnp.abs(values), axis=0, keepdims=True))
            out_ref[dest, :, span(step)] = encode(values, power)
            for part in range(tile // LANES):
                row = step * (tile // LANES) + part
                powers[dest, pl.ds(row, 1), :] = power[:, part * LANES : (part + 1) * LANES]
        return carry

    lax.fori_loop(0, tiles, begin, 0)
    lax.fori_loop(0, tiles, one_tile, 0)
    out_ref[:, :, diff.shape[0] :] = powers[...].astype(BF16)


def proto_part(diff, near, far, dests, tile=512):
    count, total = diff.shape
    depth = near.shape[2]
    return pl.pallas_call(
        functools.partial(pgrad_kernel, tile),
        in_specs=[pl.BlockSpec(memory_space=pl.ANY), vmem(), vmem()],
        out_specs=vmem(),
        out_shape=jax.ShapeDtypeStruct((dests, depth // dests, count + LANES), BF16),
        scratch_shapes=[
            pltpu.VMEM((count, total), BF16),
            pltpu.VMEM((dests, count // LANES, LANES), F32),
            pltpu.SemaphoreType.DMA((count // tile,)),
        ],
        compiler_params=params(56),
        cost_estimate=pl.CostEstimate(
            flops=2 * count * total * depth, bytes_accessed=20 * MIB, transcendentals=0
        ),
        name="proto_part",
    )(diff, near, far)


GROUP = 16


def cut_kernel(level_ref, mine_ref, given_ref, own_ref, *code_refs):
    quarter = own_ref.shape[1]
    for by in range(len(code_refs) + 1):
        start = pl.multiple_of(lax.rem(level_ref[0] + by, len(code_refs) + 1) * quarter, quarter)
        for pair in range(own_ref.shape[0]):
            values = mine_ref[pair, pl.ds(start, quarter), :] + given_ref[pair, pl.ds(start, quarter), :]
            if by == 0:
                own_ref[pair] = values
                continue
            parts = [values[at : at + GROUP] for at in range(0, quarter, GROUP)]
            power = power_of(functools.reduce(jnp.maximum, [jnp.abs(part) for part in parts]))
            for at, part in enumerate(parts):
                code_refs[by - 1][pair, at * GROUP : (at + 1) * GROUP, :] = encode(part, power)
            code_refs[by - 1][pair, quarter:, :] = power.astype(BF16)


def cuts(level, mine, given, levels):
    pairs, depth, rows = mine.shape
    quarter = depth // levels
    return pl.pallas_call(
        cut_kernel,
        in_specs=[smem(), vmem(), vmem()],
        out_specs=[vmem()] * levels,
        out_shape=[jax.ShapeDtypeStruct((pairs, quarter, rows), F32)]
        + [jax.ShapeDtypeStruct((pairs, quarter + GROUP, rows), BF16)] * (levels - 1),
        compiler_params=params(16),
        name="cuts",
    )(level, mine, given)


def join_kernel(own_ref, *refs):
    out_ref = refs[-1]
    quarter = own_ref.shape[1]
    for pair in range(own_ref.shape[0]):
        powers = [ref[pair, quarter:, :].astype(F32) for ref in refs[:-1]]
        for at in range(0, quarter, GROUP):
            total = own_ref[pair, at : at + GROUP, :]
            for ref, power in zip(refs[:-1], powers):
                total = total + decode(ref[pair, at : at + GROUP, :], power)
            out_ref[pair, at : at + GROUP, :] = total


def joined(own, codes):
    return pl.pallas_call(
        join_kernel,
        in_specs=[vmem()] * (1 + len(codes)),
        out_specs=vmem(),
        out_shape=jax.ShapeDtypeStruct(own.shape, F32),
        compiler_params=params(8),
        name="joined",
    )(own, *codes)


def protos_kernel(place_ref, weight_ref, cols_ref, protos_ref, held, sem):
    depth, count = cols_ref.shape
    start = pl.multiple_of(place_ref[0] * count, count)
    copy = pltpu.make_async_copy(weight_ref.at[:, pl.ds(start, count)], held, sem)
    copy.start()
    copy.wait()
    tile = 512
    for at in range(0, count, tile):
        wide = held[:, at : at + tile].astype(F32)
        squares = jnp.sum(wide * wide, axis=0, keepdims=True)
        unit = wide * lax.rsqrt(squares + EPS)
        cols_ref[:, at : at + tile] = unit.astype(BF16)
        protos_ref[at : at + tile, :] = unit.T.astype(BF16)


def unit_protos(place, weight, count):
    depth = weight.shape[0]
    return pl.pallas_call(
        protos_kernel,
        in_specs=[smem(), pl.BlockSpec(memory_space=pl.ANY)],
        out_specs=[vmem()] * 2,
        out_shape=[
            jax.ShapeDtypeStruct((depth, count), BF16),
            jax.ShapeDtypeStruct((count, depth), BF16),
        ],
        scratch_shapes=[pltpu.VMEM((depth, count), BF16), pltpu.SemaphoreType.DMA(())],
        compiler_params=params(56),
        cost_estimate=pl.CostEstimate(
            flops=8 * count * depth, bytes_accessed=20 * MIB, transcendentals=count
        ),
        name="unit_protos",
    )(place, weight)


def swap(value):
    return lax.ppermute(value, "c", [(0, 1), (1, 0)])


def turn(value, by, size):
    return lax.ppermute(value, "z", [(i, (i + by) % size) for i in range(size)])


def copied(value, count):
    return jnp.broadcast_to(value[None], (count,) + value.shape)


def on_device(size, teacher_feats, student_feats, proto_weight):
    depth, held = proto_weight.shape
    devices = size["yl"] * size["x"] * size["c"]
    chips = size["yl"] * size["x"]
    plane = chips * size["yh"]
    pillar = size["z"] * size["c"]
    count = held // devices
    rows = teacher_feats.shape[0]
    core = lax.axis_index("c").reshape(1)
    level = lax.axis_index("z")

    near = exchange(unit_copies(teacher_feats, chips), CHIPS)
    cols, protos = unit_protos(lax.axis_index(DP).reshape(1), proto_weight, count)
    stud_own = unit_rows(student_feats)
    near, protos, cols = lax.optimization_barrier((near, protos, cols))
    far = swap(near)
    stud_own, near = lax.optimization_barrier((stud_own, near))
    stud_near = lax.all_gather(stud_own, CHIPS)

    parts = None
    extra = None
    for step in range(ITERS):
        if step == ITERS - 1:
            extra = totals(core, protos, stud_near, stud_far)
        col, copies = sweep(core, parts, extra, protos, near, far, plane)
        parts = spread(copies, pillar)
        if step == 0:
            stud_near, parts = lax.optimization_barrier((stud_near, parts))
            stud_far = swap(stud_near)

    diff, mine_feat, other_feat = differences(
        core, parts, col, protos, cols, near, far, stud_near, stud_far
    )
    given_feat = swap(other_feat)
    own, *others = cuts(level.reshape(1), mine_feat, given_feat, size["z"])
    turned = [turn(part, by + 1, size["z"]) for by, part in enumerate(others)]
    codes = exchange(proto_part(diff, stud_near, stud_far, devices), DP)
    *turned, codes = lax.optimization_barrier((*turned, codes))
    proto_grad = decoded(codes)
    feat = joined(own, turned).reshape(plane, -1, rows)
    feat = jnp.sum(exchange(feat, PLANE), axis=0)
    feat = exchange(copied(feat, size["z"] * size["yh"]), PROTO)
    feature_grad = 512.0 * feat.reshape(depth, rows).T
    return feature_grad, proto_grad


def solution(mesh):
    split = jax.sharding.Mesh(mesh.devices.reshape(2, 4, 2, 4, 2), AXES)
    return jax.shard_map(
        functools.partial(on_device, dict(split.shape)),
        mesh=split,
        in_specs=(P(DP, None), P(DP, None), P(None, PROTO)),
        out_specs=(P(DP, None), P(DP, PROTO)),
        check_vma=False,
    )
```

```python
import functools
import math

import jax
import jax.numpy as jnp
import numpy as np
from jax import lax
from jax.experimental import pallas as pl
from jax.experimental.pallas import tpu as pltpu
from jax.sharding import PartitionSpec as P

ITERS = 3
EPS = 1e-06
TEACH = float(np.float32(0.07))
STUD = float(np.float32(0.1))
LOG2E = math.log2(math.e)
TSCALE = LOG2E / TEACH
SSCALE = LOG2E / STUD
LOG_INV = -math.log2(STUD)
F32 = jnp.float32
BF16 = jnp.bfloat16
LANES = 128
MIB = 1024 * 1024
AXES = ("yl", "x", "c", "z", "yh")
DP = ("yl", "x", "c")
PROTO = ("z", "yh")
CHIPS = ("yl", "x")
PLANE = ("yl", "x", "yh")
PILLAR = ("z", "c")


def unit_rows(feats):
    wide = feats.astype(F32)
    squares = jnp.sum(wide * wide, axis=1, keepdims=True)
    return (wide * lax.rsqrt(squares + EPS)).astype(BF16)


def dot(a, b):
    return jnp.dot(a, b, preferred_element_type=F32)


def dot_nt(a, b):
    return lax.dot_general(a, b, (((1,), (1,)), ((), ())), preferred_element_type=F32)


def fold_rows(value):
    return jnp.sum(value.reshape(value.shape[0] // 8, 8, value.shape[1]), axis=0)


def params(mib):
    return pltpu.CompilerParams(vmem_limit_bytes=mib * MIB)


def vmem():
    return pl.BlockSpec(memory_space=pltpu.VMEM)


def smem():
    return pl.BlockSpec(memory_space=pltpu.SMEM)


def unit_copies_kernel(feats_ref, out_ref):
    unit = unit_rows(feats_ref[...])
    for copy in range(out_ref.shape[0]):
        out_ref[copy] = unit


def unit_copies(feats, copies):
    return pl.pallas_call(
        unit_copies_kernel,
        in_specs=[vmem()],
        out_specs=vmem(),
        out_shape=jax.ShapeDtypeStruct((copies,) + feats.shape, BF16),
        compiler_params=params(8),
        name="unit_copies",
    )(feats)


def block_of(near_ref, far_ref, block):
    pairs = near_ref.shape[0]
    return near_ref[block] if block < pairs else far_ref[block - pairs]


def places(core, pairs, per):
    found = []
    for block in range(2 * pairs):
        parity = core if block < pairs else 1 - core
        found += [(2 * (block % pairs) + parity) * per + part for part in range(per)]
    return found


def sweep_kernel(copies, tile, has_parts, has_extra, *refs):
    refs = list(refs)
    core = refs.pop(0)[0]
    parts_ref = refs.pop(0) if has_parts else None
    extra_ref = refs.pop(0) if has_extra else None
    protos_ref, near_ref, far_ref, col_ref, out_ref, sums, scale, kern, acc = refs
    pairs, rows, _ = near_ref.shape
    blocks = 2 * pairs
    per = rows // LANES
    groups = blocks * per
    placed = places(core, pairs, per)
    if has_parts:
        sums[...] = 1.0 / jnp.sum(parts_ref[...], axis=0)
        for at, place in enumerate(placed):
            scale[at : at + 1, :] = sums[pl.ds(place, 1), :]
    acc[...] = jnp.zeros_like(acc)

    def one_tile(step, carry):
        here = pl.ds(pl.multiple_of(step * tile, tile), tile)
        protos = protos_ref[here, :]
        col_acc = jnp.zeros((tile, LANES), F32)
        for block in range(blocks):
            logits = dot_nt(protos, block_of(near_ref, far_ref, block))
            for part in range(per):
                value = jnp.exp2(logits[:, part * LANES : (part + 1) * LANES] * TSCALE)
                at = block * per + part
                kern[:, at * LANES : (at + 1) * LANES] = value
                col_acc = col_acc + (value * scale[at : at + 1, :] if has_parts else value)
        col = 1.0 / jnp.sum(col_acc, axis=1, keepdims=True)
        wide_col = jnp.broadcast_to(col, (tile, LANES))
        col_ref[here, :] = wide_col
        for at in range(groups):
            lanes = slice(at * LANES, (at + 1) * LANES)
            acc[:, lanes] += fold_rows(kern[:, lanes] * wide_col)
        return carry

    lax.fori_loop(0, protos_ref.shape[0] // tile, one_tile, 0)
    for at, place in enumerate(placed):
        total = jnp.sum(acc[:, at * LANES : (at + 1) * LANES], axis=0, keepdims=True)
        for copy in range(copies):
            out_ref[copy, pl.ds(place, 1), :] = total
    if has_extra:
        extra = extra_ref[...]
        for copy in range(copies):
            out_ref[copy, groups:, :] = extra


def sweep(core, parts, extra, protos, near, far, copies, tile=512):
    count = protos.shape[0]
    pairs, rows, _ = near.shape
    total = 2 * pairs * rows
    groups = total // LANES
    sent = groups if extra is None else groups + extra.shape[0]
    args = [a for a in (parts, extra) if a is not None] + [protos, near, far]
    return pl.pallas_call(
        functools.partial(sweep_kernel, copies, tile, parts is not None, extra is not None),
        in_specs=[smem()] + [vmem()] * len(args),
        out_specs=[vmem()] * 2,
        out_shape=[
            jax.ShapeDtypeStruct((count, LANES), F32),
            jax.ShapeDtypeStruct((copies, sent, LANES), F32),
        ],
        scratch_shapes=[
            pltpu.VMEM((groups, LANES), F32),
            pltpu.VMEM((groups, LANES), F32),
            pltpu.VMEM((tile, total), F32),
            pltpu.VMEM((8, total), F32),
        ],
        compiler_params=params(24),
        name="sweep",
    )(core, *args)


def totals_kernel(tile, core_ref, protos_ref, near_ref, far_ref, out_ref, acc):
    acc[...] = jnp.zeros_like(acc)
    pairs, rows, _ = near_ref.shape
    blocks = 2 * pairs

    def one_tile(step, carry):
        protos = protos_ref[pl.ds(pl.multiple_of(step * tile, tile), tile), :]
        for block in range(blocks):
            logits = dot_nt(protos, block_of(near_ref, far_ref, block))
            acc[:, block * rows : (block + 1) * rows] += fold_rows(jnp.exp2(logits * SSCALE))
        return carry

    lax.fori_loop(0, protos_ref.shape[0] // tile, one_tile, 0)
    for at, place in enumerate(places(core_ref[0], pairs, rows // LANES)):
        out_ref[pl.ds(place, 1), :] = jnp.sum(
            acc[:, at * LANES : (at + 1) * LANES], axis=0, keepdims=True
        )


def totals(core, protos, near, far, tile=512):
    count, depth = protos.shape
    pairs, rows, _ = near.shape
    blocks = 2 * pairs
    groups = blocks * rows // LANES
    return pl.pallas_call(
        functools.partial(totals_kernel, tile),
        in_specs=[smem()] + [vmem()] * 3,
        out_specs=vmem(),
        out_shape=jax.ShapeDtypeStruct((groups, LANES), F32),
        scratch_shapes=[pltpu.VMEM((8, blocks * rows), F32)],
        compiler_params=params(24),
        cost_estimate=pl.CostEstimate(
            flops=2 * count * depth * blocks * rows,
            bytes_accessed=4 * MIB,
            transcendentals=count * blocks * rows,
        ),
        name="totals",
    )(core, protos, near, far)


def hop_kernel(copies, in_ref, out_ref):
    total = jnp.sum(in_ref[...], axis=0)
    for copy in range(copies):
        out_ref[copy] = total


def hop(parts, copies):
    return pl.pallas_call(
        functools.partial(hop_kernel, copies),
        in_specs=[vmem()],
        out_specs=vmem(),
        out_shape=jax.ShapeDtypeStruct((copies,) + parts.shape[1:], F32),
        compiler_params=params(4),
        name="hop",
    )(parts)


def exchange(parts, axes):
    return lax.all_to_all(parts, axes, 0, 0, tiled=True)


def spread(parts, pillar):
    return exchange(hop(exchange(parts, PLANE), pillar), PILLAR)


def diff_kernel(
    tile, core_ref, parts_ref, col_ref, protos_ref, cols_ref, near_ref, far_ref, stud_near_ref, stud_far_ref,
    out_ref, mine_ref, other_ref, all_sums, scale, norm, diff, sems,
):
    pairs, rows, _ = near_ref.shape
    blocks = 2 * pairs
    per = rows // LANES
    groups = blocks * per
    all_sums[...] = LOG_INV - jnp.log2(jnp.sum(parts_ref[...], axis=0))
    for at, place in enumerate(places(core_ref[0], pairs, per)):
        scale[at : at + 1, :] = all_sums[pl.ds(place, 1), :]
        norm[at : at + 1, :] = all_sums[pl.ds(groups + place, 1), :]
    tiles = protos_ref.shape[0] // tile

    def span(step):
        return pl.ds(pl.multiple_of(step * tile, tile), tile)

    def store(step):
        return pltpu.make_async_copy(diff.at[span(step), :], out_ref.at[span(step), :], sems.at[step])

    def one_tile(step, carry):
        here = span(step)
        log_col = jnp.log2(col_ref[here, :])
        for block in range(blocks):
            teach_logits = dot_nt(protos_ref[here, :], block_of(near_ref, far_ref, block))
            stud_logits = dot_nt(protos_ref[here, :], block_of(stud_near_ref, stud_far_ref, block))
            for part in range(per):
                at = block * per + part
                lanes = slice(part * LANES, (part + 1) * LANES)
                target = jnp.exp2(teach_logits[:, lanes] * TSCALE + (scale[at : at + 1, :] + log_col))
                prob = jnp.exp2(stud_logits[:, lanes] * SSCALE + norm[at : at + 1, :])
                diff[here, at * LANES : (at + 1) * LANES] = (prob - target).astype(BF16)
        store(step).start()
        return carry

    lax.fori_loop(0, tiles, one_tile, 0)

    def one_pair(pair, carry):
        for first, ref in ((0, mine_ref), (pairs, other_ref)):
            start = pl.multiple_of((pair + first) * rows, rows)
            ref[pair] = dot(cols_ref[...], diff[:, pl.ds(start, rows)])
        return carry

    lax.fori_loop(0, pairs, one_pair, 0)

    def finish(step, carry):
        store(step).wait()
        return carry

    lax.fori_loop(0, tiles, finish, 0)


def differences(core, parts, col, protos, cols, near, far, stud_near, stud_far, tile=512):
    count, depth = protos.shape
    pairs, rows, _ = near.shape
    blocks = 2 * pairs
    groups = blocks * rows // LANES
    return pl.pallas_call(
        functools.partial(diff_kernel, tile),
        in_specs=[smem()] + [vmem()] * 8,
        out_specs=[pl.BlockSpec(memory_space=pl.ANY)] + [vmem()] * 2,
        out_shape=[
            jax.ShapeDtypeStruct((count, blocks * rows), BF16),
            jax.ShapeDtypeStruct((pairs, depth, rows), F32),
            jax.ShapeDtypeStruct((pairs, depth, rows), F32),
        ],
        scratch_shapes=[
            pltpu.VMEM((2 * groups, LANES), F32),
            pltpu.VMEM((groups, LANES), F32),
            pltpu.VMEM((groups, LANES), F32),
            pltpu.VMEM((count, blocks * rows), BF16),
            pltpu.SemaphoreType.DMA((count // tile,)),
        ],
        compiler_params=params(40),
        name="differences",
    )(core, parts, col, protos, cols, near, far, stud_near, stud_far)


SPAN = 250.0
FLOOR = 125.0


def power_of(top):
    return jnp.minimum(jnp.ceil(jnp.log2(jnp.maximum(top, 2.0**-120))), 126.0)


def encode(values, power):
    size = jnp.exp2(jnp.minimum(jnp.abs(values) * jnp.exp2(-power), 1.0) * SPAN - FLOOR)
    return jnp.where(values < 0, -size, size).astype(BF16)


def decode(code, power):
    wide = code.astype(F32)
    size = (jnp.log2(jnp.abs(wide)) + FLOOR) * (1.0 / SPAN) * jnp.exp2(power)
    return jnp.where(wide < 0, -size, size)


def decode_kernel(code_ref, out_ref):
    sources, share, width = code_ref.shape
    count = out_ref.shape[1] // sources

    def one_source(source, carry):
        powers = code_ref[source, :, count:].astype(F32)
        for part in range(count // LANES):
            code = code_ref[source, :, part * LANES : (part + 1) * LANES]
            start = pl.multiple_of(source * count + part * LANES, LANES)
            out_ref[:, pl.ds(start, LANES)] = decode(code, powers[part : part + 1, :])
        return carry

    lax.fori_loop(0, sources, one_source, 0)


def decoded(codes):
    sources, share, width = codes.shape
    return pl.pallas_call(
        decode_kernel,
        in_specs=[vmem()],
        out_specs=vmem(),
        out_shape=jax.ShapeDtypeStruct((share, sources * (width - LANES)), F32),
        compiler_params=params(16),
        cost_estimate=pl.CostEstimate(flops=16 * sources * share * width, bytes_accessed=4 * MIB, transcendentals=0),
        name="decoded",
    )(codes)


def pgrad_kernel(tile, diff_ref, near_ref, far_ref, out_ref, diff, powers, sems):
    tiles = diff.shape[0] // tile
    pairs, rows, depth = near_ref.shape
    reach = pairs * rows
    dests, share, _ = out_ref.shape

    def span(step):
        return pl.ds(pl.multiple_of(step * tile, tile), tile)

    def load(step):
        return pltpu.make_async_copy(diff_ref.at[span(step), :], diff.at[span(step), :], sems.at[step])

    def begin(step, carry):
        load(step).start()
        return carry

    def one_tile(step, carry):
        load(step).wait()
        mine = dot(diff[span(step), :reach], near_ref[...].reshape(reach, depth))
        others = dot(diff[span(step), reach:], far_ref[...].reshape(reach, depth))
        grads = (4096.0 * (mine + others)).T
        for dest in range(dests):
            values = grads[dest * share : (dest + 1) * share, :]
            power = power_of(jnp.max(jnp.abs(values), axis=0, keepdims=True))
            out_ref[dest, :, span(step)] = encode(values, power)
            for part in range(tile // LANES):
                row = step * (tile // LANES) + part
                powers[dest, pl.ds(row, 1), :] = power[:, part * LANES : (part + 1) * LANES]
        return carry

    lax.fori_loop(0, tiles, begin, 0)
    lax.fori_loop(0, tiles, one_tile, 0)
    out_ref[:, :, diff.shape[0] :] = powers[...].astype(BF16)


def proto_part(diff, near, far, dests, tile=512):
    count, total = diff.shape
    depth = near.shape[2]
    return pl.pallas_call(
        functools.partial(pgrad_kernel, tile),
        in_specs=[pl.BlockSpec(memory_space=pl.ANY), vmem(), vmem()],
        out_specs=vmem(),
        out_shape=jax.ShapeDtypeStruct((dests, depth // dests, count + LANES), BF16),
        scratch_shapes=[
            pltpu.VMEM((count, total), BF16),
            pltpu.VMEM((dests, count // LANES, LANES), F32),
            pltpu.SemaphoreType.DMA((count // tile,)),
        ],
        compiler_params=params(56),
        cost_estimate=pl.CostEstimate(
            flops=2 * count * total * depth, bytes_accessed=20 * MIB, transcendentals=0
        ),
        name="proto_part",
    )(diff, near, far)


GROUP = 16


def cut_kernel(level_ref, mine_ref, given_ref, own_ref, *code_refs):
    quarter = own_ref.shape[1]
    for by in range(len(code_refs) + 1):
        start = pl.multiple_of(lax.rem(level_ref[0] + by, len(code_refs) + 1) * quarter, quarter)
        for pair in range(own_ref.shape[0]):
            values = mine_ref[pair, pl.ds(start, quarter), :] + given_ref[pair, pl.ds(start, quarter), :]
            if by == 0:
                own_ref[pair] = values
                continue
            parts = [values[at : at + GROUP] for at in range(0, quarter, GROUP)]
            power = power_of(functools.reduce(jnp.maximum, [jnp.abs(part) for part in parts]))
            for at, part in enumerate(parts):
                code_refs[by - 1][pair, at * GROUP : (at + 1) * GROUP, :] = encode(part, power)
            code_refs[by - 1][pair, quarter:, :] = power.astype(BF16)


def cuts(level, mine, given, levels):
    pairs, depth, rows = mine.shape
    quarter = depth // levels
    return pl.pallas_call(
        cut_kernel,
        in_specs=[smem(), vmem(), vmem()],
        out_specs=[vmem()] * levels,
        out_shape=[jax.ShapeDtypeStruct((pairs, quarter, rows), F32)]
        + [jax.ShapeDtypeStruct((pairs, quarter + GROUP, rows), BF16)] * (levels - 1),
        compiler_params=params(16),
        name="cuts",
    )(level, mine, given)


def join_kernel(own_ref, *refs):
    out_ref = refs[-1]
    quarter = own_ref.shape[1]
    for pair in range(own_ref.shape[0]):
        powers = [ref[pair, quarter:, :].astype(F32) for ref in refs[:-1]]
        for at in range(0, quarter, GROUP):
            total = own_ref[pair, at : at + GROUP, :]
            for ref, power in zip(refs[:-1], powers):
                total = total + decode(ref[pair, at : at + GROUP, :], power)
            out_ref[pair, at : at + GROUP, :] = total


def joined(own, codes):
    return pl.pallas_call(
        join_kernel,
        in_specs=[vmem()] * (1 + len(codes)),
        out_specs=vmem(),
        out_shape=jax.ShapeDtypeStruct(own.shape, F32),
        compiler_params=params(8),
        name="joined",
    )(own, *codes)


def protos_kernel(place_ref, weight_ref, cols_ref, protos_ref, held, sem):
    depth, count = cols_ref.shape
    start = pl.multiple_of(place_ref[0] * count, count)
    copy = pltpu.make_async_copy(weight_ref.at[:, pl.ds(start, count)], held, sem)
    copy.start()
    copy.wait()
    tile = 512
    for at in range(0, count, tile):
        wide = held[:, at : at + tile].astype(F32)
        squares = jnp.sum(wide * wide, axis=0, keepdims=True)
        unit = wide * lax.rsqrt(squares + EPS)
        cols_ref[:, at : at + tile] = unit.astype(BF16)
        protos_ref[at : at + tile, :] = unit.T.astype(BF16)


def unit_protos(place, weight, count):
    depth = weight.shape[0]
    return pl.pallas_call(
        protos_kernel,
        in_specs=[smem(), pl.BlockSpec(memory_space=pl.ANY)],
        out_specs=[vmem()] * 2,
        out_shape=[
            jax.ShapeDtypeStruct((depth, count), BF16),
            jax.ShapeDtypeStruct((count, depth), BF16),
        ],
        scratch_shapes=[pltpu.VMEM((depth, count), BF16), pltpu.SemaphoreType.DMA(())],
        compiler_params=params(56),
        cost_estimate=pl.CostEstimate(
            flops=8 * count * depth, bytes_accessed=20 * MIB, transcendentals=count
        ),
        name="unit_protos",
    )(place, weight)


def swap(value):
    return lax.ppermute(value, "c", [(0, 1), (1, 0)])


def turn(value, by, size):
    return lax.ppermute(value, "z", [(i, (i + by) % size) for i in range(size)])


def copied(value, count):
    return jnp.broadcast_to(value[None], (count,) + value.shape)


def on_device(size, teacher_feats, student_feats, proto_weight):
    depth, held = proto_weight.shape
    devices = size["yl"] * size["x"] * size["c"]
    chips = size["yl"] * size["x"]
    plane = chips * size["yh"]
    pillar = size["z"] * size["c"]
    count = held // devices
    rows = teacher_feats.shape[0]
    core = lax.axis_index("c").reshape(1)
    level = lax.axis_index("z")

    near = exchange(unit_copies(teacher_feats, chips), CHIPS)
    cols, protos = unit_protos(lax.axis_index(DP).reshape(1), proto_weight, count)
    stud_own = unit_rows(student_feats)
    near, protos, cols = lax.optimization_barrier((near, protos, cols))
    far = swap(near)
    stud_own, near = lax.optimization_barrier((stud_own, near))
    stud_near = lax.all_gather(stud_own, CHIPS)

    parts = None
    extra = None
    for step in range(ITERS):
        if step == ITERS - 1:
            extra = totals(core, protos, stud_near, stud_far)
        col, copies = sweep(core, parts, extra, protos, near, far, plane)
        parts = spread(copies, pillar)
        if step == 0:
            stud_near, parts = lax.optimization_barrier((stud_near, parts))
            stud_far = swap(stud_near)

    diff, mine_feat, other_feat = differences(
        core, parts, col, protos, cols, near, far, stud_near, stud_far
    )
    given_feat = swap(other_feat)
    own, *others = cuts(level.reshape(1), mine_feat, given_feat, size["z"])
    turned = [turn(part, by + 1, size["z"]) for by, part in enumerate(others)]
    codes = exchange(proto_part(diff, stud_near, stud_far, devices), DP)
    *turned, codes = lax.optimization_barrier((*turned, codes))
    proto_grad = decoded(codes)
    feat = joined(own, turned).reshape(plane, -1, rows)
    feat = jnp.sum(exchange(feat, PLANE), axis=0)
    feat = exchange(copied(feat, size["z"] * size["yh"]), PROTO)
    feature_grad = 512.0 * feat.reshape(depth, rows).T
    return feature_grad, proto_grad


def solution(mesh):
    split = jax.sharding.Mesh(mesh.devices.reshape(2, 4, 2, 4, 2), AXES)
    return jax.shard_map(
        functools.partial(on_device, dict(split.shape)),
        mesh=split,
        in_specs=(P(DP, None), P(DP, None), P(None, PROTO)),
        out_specs=(P(DP, None), P(DP, PROTO)),
        check_vma=False,
    )
```

```python
import functools
import math

import jax
import jax.numpy as jnp
import numpy as np
from jax import lax
from jax.experimental import pallas as pl
from jax.experimental.pallas import tpu as pltpu
from jax.sharding import PartitionSpec as P

ITERS = 3
EPS = 1e-06
TEACH = float(np.float32(0.07))
STUD = float(np.float32(0.1))
LOG2E = math.log2(math.e)
TSCALE = LOG2E / TEACH
SSCALE = LOG2E / STUD
LOG_INV = -math.log2(STUD)
F32 = jnp.float32
BF16 = jnp.bfloat16
LANES = 128
MIB = 1024 * 1024
AXES = ("yl", "x", "c", "z", "yh")
DP = ("yl", "x", "c")
PROTO = ("z", "yh")
CHIPS = ("yl", "x")
PLANE = ("yl", "x", "yh")
PILLAR = ("z", "c")


def unit_rows(feats):
    wide = feats.astype(F32)
    squares = jnp.sum(wide * wide, axis=1, keepdims=True)
    return (wide * lax.rsqrt(squares + EPS)).astype(BF16)


def dot(a, b):
    return jnp.dot(a, b, preferred_element_type=F32)


def dot_nt(a, b):
    return lax.dot_general(a, b, (((1,), (1,)), ((), ())), preferred_element_type=F32)


def fold_rows(value):
    return jnp.sum(value.reshape(value.shape[0] // 8, 8, value.shape[1]), axis=0)


def params(mib):
    return pltpu.CompilerParams(vmem_limit_bytes=mib * MIB)


def vmem():
    return pl.BlockSpec(memory_space=pltpu.VMEM)


def smem():
    return pl.BlockSpec(memory_space=pltpu.SMEM)


def unit_copies_kernel(feats_ref, out_ref):
    unit = unit_rows(feats_ref[...])
    for copy in range(out_ref.shape[0]):
        out_ref[copy] = unit


def unit_copies(feats, copies):
    return pl.pallas_call(
        unit_copies_kernel,
        in_specs=[vmem()],
        out_specs=vmem(),
        out_shape=jax.ShapeDtypeStruct((copies,) + feats.shape, BF16),
        compiler_params=params(8),
        name="unit_copies",
    )(feats)


def block_of(near_ref, far_ref, block):
    pairs = near_ref.shape[0]
    return near_ref[block] if block < pairs else far_ref[block - pairs]


def places(core, pairs, per):
    found = []
    for block in range(2 * pairs):
        parity = core if block < pairs else 1 - core
        found += [(2 * (block % pairs) + parity) * per + part for part in range(per)]
    return found


def sweep_kernel(copies, tile, has_parts, has_extra, *refs):
    refs = list(refs)
    core = refs.pop(0)[0]
    parts_ref = refs.pop(0) if has_parts else None
    extra_ref = refs.pop(0) if has_extra else None
    protos_ref, near_ref, far_ref, col_ref, out_ref, sums, scale, kern, acc = refs
    pairs, rows, _ = near_ref.shape
    blocks = 2 * pairs
    per = rows // LANES
    groups = blocks * per
    placed = places(core, pairs, per)
    if has_parts:
        sums[...] = 1.0 / jnp.sum(parts_ref[...], axis=0)
        for at, place in enumerate(placed):
            scale[at : at + 1, :] = sums[pl.ds(place, 1), :]
    acc[...] = jnp.zeros_like(acc)

    def one_tile(step, carry):
        here = pl.ds(pl.multiple_of(step * tile, tile), tile)
        protos = protos_ref[here, :]
        col_acc = jnp.zeros((tile, LANES), F32)
        for block in range(blocks):
            logits = dot_nt(protos, block_of(near_ref, far_ref, block))
            for part in range(per):
                value = jnp.exp2(logits[:, part * LANES : (part + 1) * LANES] * TSCALE)
                at = block * per + part
                kern[:, at * LANES : (at + 1) * LANES] = value
                col_acc = col_acc + (value * scale[at : at + 1, :] if has_parts else value)
        col = 1.0 / jnp.sum(col_acc, axis=1, keepdims=True)
        wide_col = jnp.broadcast_to(col, (tile, LANES))
        col_ref[here, :] = wide_col
        for at in range(groups):
            lanes = slice(at * LANES, (at + 1) * LANES)
            acc[:, lanes] += fold_rows(kern[:, lanes] * wide_col)
        return carry

    lax.fori_loop(0, protos_ref.shape[0] // tile, one_tile, 0)
    for at, place in enumerate(placed):
        total = jnp.sum(acc[:, at * LANES : (at + 1) * LANES], axis=0, keepdims=True)
        for copy in range(copies):
            out_ref[copy, pl.ds(place, 1), :] = total
    if has_extra:
        extra = extra_ref[...]
        for copy in range(copies):
            out_ref[copy, groups:, :] = extra


def sweep(core, parts, extra, protos, near, far, copies, tile=512):
    count = protos.shape[0]
    pairs, rows, _ = near.shape
    total = 2 * pairs * rows
    groups = total // LANES
    sent = groups if extra is None else groups + extra.shape[0]
    args = [a for a in (parts, extra) if a is not None] + [protos, near, far]
    return pl.pallas_call(
        functools.partial(sweep_kernel, copies, tile, parts is not None, extra is not None),
        in_specs=[smem()] + [vmem()] * len(args),
        out_specs=[vmem()] * 2,
        out_shape=[
            jax.ShapeDtypeStruct((count, LANES), F32),
            jax.ShapeDtypeStruct((copies, sent, LANES), F32),
        ],
        scratch_shapes=[
            pltpu.VMEM((groups, LANES), F32),
            pltpu.VMEM((groups, LANES), F32),
            pltpu.VMEM((tile, total), F32),
            pltpu.VMEM((8, total), F32),
        ],
        compiler_params=params(24),
        name="sweep",
    )(core, *args)


def totals_kernel(tile, core_ref, protos_ref, near_ref, far_ref, out_ref, acc):
    acc[...] = jnp.zeros_like(acc)
    pairs, rows, _ = near_ref.shape
    blocks = 2 * pairs

    def one_tile(step, carry):
        protos = protos_ref[pl.ds(pl.multiple_of(step * tile, tile), tile), :]
        for block in range(blocks):
            logits = dot_nt(protos, block_of(near_ref, far_ref, block))
            acc[:, block * rows : (block + 1) * rows] += fold_rows(jnp.exp2(logits * SSCALE))
        return carry

    lax.fori_loop(0, protos_ref.shape[0] // tile, one_tile, 0)
    for at, place in enumerate(places(core_ref[0], pairs, rows // LANES)):
        out_ref[pl.ds(place, 1), :] = jnp.sum(
            acc[:, at * LANES : (at + 1) * LANES], axis=0, keepdims=True
        )


def totals(core, protos, near, far, tile=512):
    count, depth = protos.shape
    pairs, rows, _ = near.shape
    blocks = 2 * pairs
    groups = blocks * rows // LANES
    return pl.pallas_call(
        functools.partial(totals_kernel, tile),
        in_specs=[smem()] + [vmem()] * 3,
        out_specs=vmem(),
        out_shape=jax.ShapeDtypeStruct((groups, LANES), F32),
        scratch_shapes=[pltpu.VMEM((8, blocks * rows), F32)],
        compiler_params=params(24),
        cost_estimate=pl.CostEstimate(
            flops=2 * count * depth * blocks * rows,
            bytes_accessed=4 * MIB,
            transcendentals=count * blocks * rows,
        ),
        name="totals",
    )(core, protos, near, far)


def hop_kernel(copies, in_ref, out_ref):
    total = jnp.sum(in_ref[...], axis=0)
    for copy in range(copies):
        out_ref[copy] = total


def hop(parts, copies):
    return pl.pallas_call(
        functools.partial(hop_kernel, copies),
        in_specs=[vmem()],
        out_specs=vmem(),
        out_shape=jax.ShapeDtypeStruct((copies,) + parts.shape[1:], F32),
        compiler_params=params(4),
        name="hop",
    )(parts)


def exchange(parts, axes):
    return lax.all_to_all(parts, axes, 0, 0, tiled=True)


def spread(parts, pillar):
    return exchange(hop(exchange(parts, PLANE), pillar), PILLAR)


def diff_kernel(
    tile, core_ref, parts_ref, col_ref, protos_ref, cols_ref, near_ref, far_ref, stud_near_ref, stud_far_ref,
    out_ref, mine_ref, other_ref, all_sums, scale, norm, diff, sems,
):
    pairs, rows, _ = near_ref.shape
    blocks = 2 * pairs
    per = rows // LANES
    groups = blocks * per
    all_sums[...] = LOG_INV - jnp.log2(jnp.sum(parts_ref[...], axis=0))
    for at, place in enumerate(places(core_ref[0], pairs, per)):
        scale[at : at + 1, :] = all_sums[pl.ds(place, 1), :]
        norm[at : at + 1, :] = all_sums[pl.ds(groups + place, 1), :]
    tiles = protos_ref.shape[0] // tile

    def span(step):
        return pl.ds(pl.multiple_of(step * tile, tile), tile)

    def store(step):
        return pltpu.make_async_copy(diff.at[span(step), :], out_ref.at[span(step), :], sems.at[step])

    def one_tile(step, carry):
        here = span(step)
        log_col = jnp.log2(col_ref[here, :])
        for block in range(blocks):
            teach_logits = dot_nt(protos_ref[here, :], block_of(near_ref, far_ref, block))
            stud_logits = dot_nt(protos_ref[here, :], block_of(stud_near_ref, stud_far_ref, block))
            for part in range(per):
                at = block * per + part
                lanes = slice(part * LANES, (part + 1) * LANES)
                target = jnp.exp2(teach_logits[:, lanes] * TSCALE + (scale[at : at + 1, :] + log_col))
                prob = jnp.exp2(stud_logits[:, lanes] * SSCALE + norm[at : at + 1, :])
                diff[here, at * LANES : (at + 1) * LANES] = (prob - target).astype(BF16)
        store(step).start()
        return carry

    lax.fori_loop(0, tiles, one_tile, 0)

    def one_pair(pair, carry):
        for first, ref in ((0, mine_ref), (pairs, other_ref)):
            start = pl.multiple_of((pair + first) * rows, rows)
            ref[pair] = dot(cols_ref[...], diff[:, pl.ds(start, rows)])
        return carry

    lax.fori_loop(0, pairs, one_pair, 0, unroll=4)

    def finish(step, carry):
        store(step).wait()
        return carry

    lax.fori_loop(0, tiles, finish, 0)


def differences(core, parts, col, protos, cols, near, far, stud_near, stud_far, tile=512):
    count, depth = protos.shape
    pairs, rows, _ = near.shape
    blocks = 2 * pairs
    groups = blocks * rows // LANES
    return pl.pallas_call(
        functools.partial(diff_kernel, tile),
        in_specs=[smem()] + [vmem()] * 8,
        out_specs=[pl.BlockSpec(memory_space=pl.ANY)] + [vmem()] * 2,
        out_shape=[
            jax.ShapeDtypeStruct((count, blocks * rows), BF16),
            jax.ShapeDtypeStruct((pairs, depth, rows), F32),
            jax.ShapeDtypeStruct((pairs, depth, rows), F32),
        ],
        scratch_shapes=[
            pltpu.VMEM((2 * groups, LANES), F32),
            pltpu.VMEM((groups, LANES), F32),
            pltpu.VMEM((groups, LANES), F32),
            pltpu.VMEM((count, blocks * rows), BF16),
            pltpu.SemaphoreType.DMA((count // tile,)),
        ],
        compiler_params=params(40),
        name="differences",
    )(core, parts, col, protos, cols, near, far, stud_near, stud_far)


SPAN = 250.0
FLOOR = 125.0


def power_of(top):
    return jnp.minimum(jnp.ceil(jnp.log2(jnp.maximum(top, 2.0**-120))), 126.0)


def encode(values, power):
    size = jnp.exp2(jnp.minimum(jnp.abs(values) * jnp.exp2(-power), 1.0) * SPAN - FLOOR)
    return jnp.where(values < 0, -size, size).astype(BF16)


def decode(code, power):
    wide = code.astype(F32)
    size = (jnp.log2(jnp.abs(wide)) + FLOOR) * (1.0 / SPAN) * jnp.exp2(power)
    return jnp.where(wide < 0, -size, size)


def decode_kernel(code_ref, out_ref):
    sources, share, width = code_ref.shape
    count = out_ref.shape[1] // sources

    def one_source(source, carry):
        powers = code_ref[source, :, count:].astype(F32)
        for part in range(count // LANES):
            code = code_ref[source, :, part * LANES : (part + 1) * LANES]
            start = pl.multiple_of(source * count + part * LANES, LANES)
            out_ref[:, pl.ds(start, LANES)] = decode(code, powers[part : part + 1, :])
        return carry

    lax.fori_loop(0, sources, one_source, 0)


def decoded(codes):
    sources, share, width = codes.shape
    return pl.pallas_call(
        decode_kernel,
        in_specs=[vmem()],
        out_specs=vmem(),
        out_shape=jax.ShapeDtypeStruct((share, sources * (width - LANES)), F32),
        compiler_params=params(16),
        cost_estimate=pl.CostEstimate(flops=16 * sources * share * width, bytes_accessed=4 * MIB, transcendentals=0),
        name="decoded",
    )(codes)


def pgrad_kernel(tile, diff_ref, near_ref, far_ref, out_ref, diff, powers, sems):
    tiles = diff.shape[0] // tile
    pairs, rows, depth = near_ref.shape
    reach = pairs * rows
    dests, share, _ = out_ref.shape

    def span(step):
        return pl.ds(pl.multiple_of(step * tile, tile), tile)

    def load(step):
        return pltpu.make_async_copy(diff_ref.at[span(step), :], diff.at[span(step), :], sems.at[step])

    def begin(step, carry):
        load(step).start()
        return carry

    def one_tile(step, carry):
        load(step).wait()
        mine = dot(diff[span(step), :reach], near_ref[...].reshape(reach, depth))
        others = dot(diff[span(step), reach:], far_ref[...].reshape(reach, depth))
        grads = (4096.0 * (mine + others)).T
        for dest in range(dests):
            values = grads[dest * share : (dest + 1) * share, :]
            power = power_of(jnp.max(jnp.abs(values), axis=0, keepdims=True))
            out_ref[dest, :, span(step)] = encode(values, power)
            for part in range(tile // LANES):
                row = step * (tile // LANES) + part
                powers[dest, pl.ds(row, 1), :] = power[:, part * LANES : (part + 1) * LANES]
        return carry

    lax.fori_loop(0, tiles, begin, 0)
    lax.fori_loop(0, tiles, one_tile, 0)
    out_ref[:, :, diff.shape[0] :] = powers[...].astype(BF16)


def proto_part(diff, near, far, dests, tile=512):
    count, total = diff.shape
    depth = near.shape[2]
    return pl.pallas_call(
        functools.partial(pgrad_kernel, tile),
        in_specs=[pl.BlockSpec(memory_space=pl.ANY), vmem(), vmem()],
        out_specs=vmem(),
        out_shape=jax.ShapeDtypeStruct((dests, depth // dests, count + LANES), BF16),
        scratch_shapes=[
            pltpu.VMEM((count, total), BF16),
            pltpu.VMEM((dests, count // LANES, LANES), F32),
            pltpu.SemaphoreType.DMA((count // tile,)),
        ],
        compiler_params=params(56),
        cost_estimate=pl.CostEstimate(
            flops=2 * count * total * depth, bytes_accessed=20 * MIB, transcendentals=0
        ),
        name="proto_part",
    )(diff, near, far)


GROUP = 16


def cut_kernel(level_ref, mine_ref, given_ref, own_ref, *code_refs):
    quarter = own_ref.shape[1]
    for by in range(len(code_refs) + 1):
        start = pl.multiple_of(lax.rem(level_ref[0] + by, len(code_refs) + 1) * quarter, quarter)
        for pair in range(own_ref.shape[0]):
            values = mine_ref[pair, pl.ds(start, quarter), :] + given_ref[pair, pl.ds(start, quarter), :]
            if by == 0:
                own_ref[pair] = values
                continue
            parts = [values[at : at + GROUP] for at in range(0, quarter, GROUP)]
            power = power_of(functools.reduce(jnp.maximum, [jnp.abs(part) for part in parts]))
            for at, part in enumerate(parts):
                code_refs[by - 1][pair, at * GROUP : (at + 1) * GROUP, :] = encode(part, power)
            code_refs[by - 1][pair, quarter:, :] = power.astype(BF16)


def cuts(level, mine, given, levels):
    pairs, depth, rows = mine.shape
    quarter = depth // levels
    return pl.pallas_call(
        cut_kernel,
        in_specs=[smem(), vmem(), vmem()],
        out_specs=[vmem()] * levels,
        out_shape=[jax.ShapeDtypeStruct((pairs, quarter, rows), F32)]
        + [jax.ShapeDtypeStruct((pairs, quarter + GROUP, rows), BF16)] * (levels - 1),
        compiler_params=params(16),
        name="cuts",
    )(level, mine, given)


def join_kernel(own_ref, *refs):
    out_ref = refs[-1]
    quarter = own_ref.shape[1]
    for pair in range(own_ref.shape[0]):
        powers = [ref[pair, quarter:, :].astype(F32) for ref in refs[:-1]]
        for at in range(0, quarter, GROUP):
            total = own_ref[pair, at : at + GROUP, :]
            for ref, power in zip(refs[:-1], powers):
                total = total + decode(ref[pair, at : at + GROUP, :], power)
            out_ref[pair, at : at + GROUP, :] = total


def joined(own, codes):
    return pl.pallas_call(
        join_kernel,
        in_specs=[vmem()] * (1 + len(codes)),
        out_specs=vmem(),
        out_shape=jax.ShapeDtypeStruct(own.shape, F32),
        compiler_params=params(8),
        name="joined",
    )(own, *codes)


def protos_kernel(place_ref, weight_ref, cols_ref, protos_ref, held, sem):
    depth, count = cols_ref.shape
    start = pl.multiple_of(place_ref[0] * count, count)
    copy = pltpu.make_async_copy(weight_ref.at[:, pl.ds(start, count)], held, sem)
    copy.start()
    copy.wait()
    tile = 512
    for at in range(0, count, tile):
        wide = held[:, at : at + tile].astype(F32)
        squares = jnp.sum(wide * wide, axis=0, keepdims=True)
        unit = wide * lax.rsqrt(squares + EPS)
        cols_ref[:, at : at + tile] = unit.astype(BF16)
        protos_ref[at : at + tile, :] = unit.T.astype(BF16)


def unit_protos(place, weight, count):
    depth = weight.shape[0]
    return pl.pallas_call(
        protos_kernel,
        in_specs=[smem(), pl.BlockSpec(memory_space=pl.ANY)],
        out_specs=[vmem()] * 2,
        out_shape=[
            jax.ShapeDtypeStruct((depth, count), BF16),
            jax.ShapeDtypeStruct((count, depth), BF16),
        ],
        scratch_shapes=[pltpu.VMEM((depth, count), BF16), pltpu.SemaphoreType.DMA(())],
        compiler_params=params(56),
        cost_estimate=pl.CostEstimate(
            flops=8 * count * depth, bytes_accessed=20 * MIB, transcendentals=count
        ),
        name="unit_protos",
    )(place, weight)


def swap(value):
    return lax.ppermute(value, "c", [(0, 1), (1, 0)])


def turn(value, by, size):
    return lax.ppermute(value, "z", [(i, (i + by) % size) for i in range(size)])


def copied(value, count):
    return jnp.broadcast_to(value[None], (count,) + value.shape)


def on_device(size, teacher_feats, student_feats, proto_weight):
    depth, held = proto_weight.shape
    devices = size["yl"] * size["x"] * size["c"]
    chips = size["yl"] * size["x"]
    plane = chips * size["yh"]
    pillar = size["z"] * size["c"]
    count = held // devices
    rows = teacher_feats.shape[0]
    core = lax.axis_index("c").reshape(1)
    level = lax.axis_index("z")

    near = exchange(unit_copies(teacher_feats, chips), CHIPS)
    cols, protos = unit_protos(lax.axis_index(DP).reshape(1), proto_weight, count)
    stud_own = unit_rows(student_feats)
    near, protos, cols = lax.optimization_barrier((near, protos, cols))
    far = swap(near)
    stud_own, near = lax.optimization_barrier((stud_own, near))
    stud_near = lax.all_gather(stud_own, CHIPS)

    parts = None
    extra = None
    for step in range(ITERS):
        if step == ITERS - 1:
            extra = totals(core, protos, stud_near, stud_far)
        col, copies = sweep(core, parts, extra, protos, near, far, plane)
        parts = spread(copies, pillar)
        if step == 0:
            stud_near, parts = lax.optimization_barrier((stud_near, parts))
            stud_far = swap(stud_near)

    diff, mine_feat, other_feat = differences(
        core, parts, col, protos, cols, near, far, stud_near, stud_far
    )
    given_feat = swap(other_feat)
    own, *others = cuts(level.reshape(1), mine_feat, given_feat, size["z"])
    turned = [turn(part, by + 1, size["z"]) for by, part in enumerate(others)]
    codes = exchange(proto_part(diff, stud_near, stud_far, devices), DP)
    *turned, codes = lax.optimization_barrier((*turned, codes))
    proto_grad = decoded(codes)
    feat = joined(own, turned).reshape(plane, -1, rows)
    feat = jnp.sum(exchange(feat, PLANE), axis=0)
    feat = exchange(copied(feat, size["z"] * size["yh"]), PROTO)
    feature_grad = 512.0 * feat.reshape(depth, rows).T
    return feature_grad, proto_grad


def solution(mesh):
    split = jax.sharding.Mesh(mesh.devices.reshape(2, 4, 2, 4, 2), AXES)
    return jax.shard_map(
        functools.partial(on_device, dict(split.shape)),
        mesh=split,
        in_specs=(P(DP, None), P(DP, None), P(None, PROTO)),
        out_specs=(P(DP, None), P(DP, PROTO)),
        check_vma=False,
    )
```
